32 devices in a mesh: ctx: 8 (over y, x, core), wt: 4 (over z).
Axes of the slice: x: 2, y: 2, z: 4, core: 2. Of those that a mesh axis runs over, the one named last changes fastest.
Arguments:
- x_in: bfloat16 [4, 2048, 512], P(None, 'ctx'), may hold values from -13 to 13
- grad_out: bfloat16 [4, 2048, 512], P(None, 'ctx'), may hold values from -6 to 6
- seg_ids: int32 [4, 2048], replicated, may hold values from 0 to 2, as said below
- norm1_gain: float32 [512], replicated, may hold values from 0.1 to 1.9
- norm1_bias: float32 [512], replicated, may hold values from -1.75 to 1.75
- q_weight: bfloat16 [512, 512], P(None, 'wt'), may hold values from -0.375 to 0.375
- q_bias: float32 [512], P('wt'), may hold values from -3 to 3
- k_weight: bfloat16 [512, 512], P(None, 'wt'), may hold values from -0.25 to 0.25
- v_weight: bfloat16 [512, 512], P(None, 'wt'), may hold values from -0.25 to 0.25
- v_bias: float32 [512], P('wt'), may hold values from -3 to 3
- out_weight: bfloat16 [512, 512], P('wt'), may hold values from -0.5 to 0.5
- out_bias: float32 [512], replicated, may hold values from -3 to 3
- norm2_gain: float32 [512], replicated, may hold values from 0.1 to 1.9
- norm2_bias: float32 [512], replicated, may hold values from -1.75 to 1.75
- up_weight: bfloat16 [512, 2048], P(None, 'wt'), may hold values from -0.25 to 0.25
- up_bias: float32 [2048], P('wt'), may hold values from -1.75 to 1.75
- down_weight: bfloat16 [2048, 512], P('wt'), may hold values from -0.1875 to 0.1875
- down_bias: float32 [512], replicated, may hold values from -3 to 3
Outputs:
- layer_out: float32 [4, 2048, 512], P(None, 'ctx')
- input_grad: float32 [4, 2048, 512], P(None, 'ctx')
- norm1_gain_grad: float32 [512], P('wt')
- norm1_bias_grad: float32 [512], P('wt')
- q_weight_grad: float32 [512, 512], P(None, 'wt')
- q_bias_grad: float32 [512], P('wt')
- k_weight_grad: float32 [512, 512], P(None, 'wt')
- v_weight_grad: float32 [512, 512], P(None, 'wt')
- v_bias_grad: float32 [512], P('wt')
- out_weight_grad: float32 [512, 512], P('wt')
- out_bias_grad: float32 [512], P('wt')
- norm2_gain_grad: float32 [512], P('wt')
- norm2_bias_grad: float32 [512], P('wt')
- up_weight_grad: float32 [512, 2048], P(None, 'wt')
- up_bias_grad: float32 [2048], P('wt')
- down_weight_grad: float32 [2048, 512], P('wt')
- down_bias_grad: float32 [512], P('wt')
The draws below stay inside these ranges and needn't reach their ends.
Inputs may be any that keep to these rules, and one draw needn't show every extreme that they name: `seg_ids`: in each micro-batch the segment numbers never fall along the tokens; there are three documents, each present, and the middle one covers tokens on every index of ctx.
All inputs are finite; a program needn't handle non-finite values.
Results may differ from the reference program's by a relative error of at most 0.02.
Values may be sent and summed in bfloat16 or wider, within the bound.
A program may use at most 192 MiB of HBM per device.

```python
import jax
import jax.numpy as jnp
from jax import lax

D = 512
HEADS = 8
HEAD_DIM = 64
FF = 2048
BLOCK = 16
LEVELS = 10
FINE = 3
MICRO = 4
TOK_DEV = 256
TOKENS = 2048


def draw_x_in(key, part):
    noise_key = jax.random.fold_in(key, 7)
    base = jax.random.truncated_normal(noise_key, -4.0, 4.0, (MICRO, TOKENS, D), jnp.float32)
    amount = 0.35
    total_sum = 0.6 * base
    for scale_bits in range(FINE, LEVELS):
        cell_size = 2 ** scale_bits
        table_key = jax.random.fold_in(key, 100 + scale_bits)
        coarse_rows = jax.random.truncated_normal(table_key, -4.0, 4.0, (MICRO, TOKENS // cell_size, 1, D), jnp.float32)
        spread_rows = jnp.broadcast_to(coarse_rows, (MICRO, TOKENS // cell_size, cell_size, D)).reshape(MICRO, TOKENS, D)
        total_sum = total_sum + amount * spread_rows
    return total_sum.astype(jnp.bfloat16)


def draw_seg_ids(key, part):
    key = jax.random.fold_in(key, 11)
    first_key, last_key = jax.random.split(key)
    heads = jax.random.randint(first_key, (MICRO, 1), 1, TOK_DEV // 2 + 1, dtype=jnp.int32)
    tails = jax.random.randint(last_key, (MICRO, 1), 1, TOK_DEV // 2 + 1, dtype=jnp.int32)
    position = jnp.arange(TOKENS, dtype=jnp.int32)[None, :]
    return (position >= heads).astype(jnp.int32) + (position >= TOKENS - tails).astype(jnp.int32)


def levels(stream_key, dims, cuts, smallest, top_value):
    loudness, own = 1.0, jax.random.fold_in(stream_key, 6)
    for dim, shards_of in cuts:
        heights = jnp.exp(jax.random.uniform(jax.random.fold_in(own, dim), (shards_of,), jnp.float32, smallest / len(cuts), top_value / len(cuts)))
        loudness = loudness * jnp.repeat(heights, dims[dim] // shards_of).reshape([-1 if axis == dim else 1 for axis in range(len(dims))])
    return loudness


def scatter_about(rng, shape, spread, reach, cuts=(), held_as=jnp.bfloat16):
    array = jax.random.normal(rng, shape, jnp.float32) * spread
    if len(cuts) > 0:
        array = levels(rng, shape, cuts, -0.22, 0.18) * array
    return jnp.clip(array, min=-reach, max=reach).astype(held_as)


def setup_inputs(seed: int = 0) -> dict:
    key_of = jax.random.split(jax.random.key(seed), 19)
    return {
        "x_in": draw_x_in(jax.random.fold_in(key_of[18], 71), 0),
        "grad_out": scatter_about(key_of[1], (MICRO, TOKENS, D), 1.0, 6.0, ((1, 8),)),
        "seg_ids": draw_seg_ids(jax.random.fold_in(key_of[18], 71), 0),
        "norm1_gain": jnp.clip(1.0 + 0.18 * jax.random.normal(key_of[3], (D,), jnp.float32), 0.1, 1.9),
        "norm1_bias": scatter_about(key_of[4], (D,), 0.3, 1.75, (), jnp.float32),
        "q_weight": scatter_about(key_of[5], (D, HEADS * HEAD_DIM), (D // 2) ** -0.5, 0.375, ((1, 4),)),
        "q_bias": scatter_about(key_of[6], (HEADS * HEAD_DIM,), 0.5, 3.0, ((0, 4),), jnp.float32),
        "k_weight": scatter_about(key_of[7], (D, HEADS * HEAD_DIM), D ** -0.5, 0.25, ((1, 4),)),
        "v_weight": scatter_about(key_of[8], (D, HEADS * HEAD_DIM), D ** -0.5, 0.25, ((1, 4),)),
        "v_bias": scatter_about(key_of[9], (HEADS * HEAD_DIM,), 0.5, 3.0, ((0, 4),), jnp.float32),
        "out_weight": scatter_about(key_of[10], (HEADS * HEAD_DIM, D), (HEADS * HEAD_DIM // 4) ** -0.5, 0.5, ((0, 4),)),
        "out_bias": scatter_about(key_of[11], (D,), 0.5, 3.0, (), jnp.float32),
        "norm2_gain": jnp.clip(1.0 + 0.18 * jax.random.normal(key_of[12], (D,), jnp.float32), 0.1, 1.9),
        "norm2_bias": scatter_about(key_of[13], (D,), 0.3, 1.75, (), jnp.float32),
        "up_weight": scatter_about(key_of[14], (D, FF), D ** -0.5, 0.25, ((1, 4),)),
        "up_bias": scatter_about(key_of[15], (FF,), 0.3, 1.75, ((0, 4),), jnp.float32),
        "down_weight": scatter_about(key_of[16], (FF, D), (FF // 2) ** -0.5, 0.1875, ((0, 4),)),
        "down_bias": scatter_about(key_of[17], (D,), 0.5, 3.0, (), jnp.float32),
    }


EPSILON = 1e-05
NEGATIVE = -1e+30
LOG_TWO = 0.6931471805599453

@jax.custom_vjp
def low(v):
    return lax.optimization_barrier(v.astype(jnp.bfloat16)).astype(jnp.float32)

@jax.custom_vjp
def low_back(v):
    return v

def low_keep(v):
    return (low(v), None)

def low_pass(kept, grad):
    return (grad,)

def back_keep(v):
    return (v, None)

def back_low(kept, grad):
    return (low(grad),)
low.defvjp(low_keep, low_pass)
low_back.defvjp(back_keep, back_low)

def matmul(left, right):
    return jnp.dot(left, right, precision=lax.Precision.HIGHEST, preferred_element_type=jnp.float32)

def layer_norm(source, gain, shift):
    centre = lax.optimization_barrier(jnp.mean(source, axis=-1, keepdims=True))
    centred = source - centre
    variance = lax.optimization_barrier(jnp.mean(centred * centred, axis=-1, keepdims=True))
    return centred * lax.rsqrt(variance + EPSILON) * gain + shift

def cell_means(source, cell_size):
    grouped = source.reshape(source.shape[0] // cell_size, cell_size, source.shape[1])
    return low(lax.optimization_barrier(jnp.mean(grouped, axis=1)))

def candidates(offset, seg_row, tail_len, query_count):
    window_len = tail_len + query_count
    padded = jnp.concatenate([jnp.full((tail_len,), -1, jnp.int32), seg_row])
    seg_window = lax.dynamic_slice_in_dim(padded, offset, window_len)
    first_pos = offset - tail_len
    starts = [first_pos + jnp.arange(window_len, dtype=jnp.int32)]
    lengths = [jnp.ones((window_len,), jnp.int32)]
    depths = [jnp.zeros((window_len,), jnp.int32)]
    firsts = [seg_window]
    lasts = [seg_window]
    for level_at in range(1, LEVELS):
        cell_size = 2 ** level_at
        if level_at < FINE:
            cell_count = window_len // cell_size
            base_pos = first_pos
            grouped = seg_window.reshape(cell_count, cell_size)
        else:
            cell_count = seg_row.shape[0] // cell_size
            base_pos = 0
            grouped = seg_row.reshape(cell_count, cell_size)
        starts.append(base_pos + cell_size * jnp.arange(cell_count, dtype=jnp.int32))
        lengths.append(jnp.full((cell_count,), cell_size, jnp.int32))
        depths.append(jnp.full((cell_count,), level_at, jnp.int32))
        firsts.append(grouped[:, 0])
        lasts.append(grouped[:, cell_size - 1])
    return tuple((jnp.concatenate(column_set) for column_set in (starts, lengths, depths, firsts, lasts)))

def valid_mask(offset, seg_row, layout, query_count):
    starts, lengths, depths, firsts, lasts = layout
    position = offset + jnp.arange(query_count, dtype=jnp.int32)[:, None]
    seg_query = lax.dynamic_slice_in_dim(seg_row, offset, query_count)[:, None]
    span = (BLOCK * lengths)[None, :]
    lower = span * (position // span - 1)
    half_span = span // 2
    finer = half_span * (position // half_span - 1)
    upper = jnp.where(depths[None, :] == 0, position + 1, finer)
    begin = starts[None, :]
    inside = (begin >= 0) & (begin >= lower) & (begin + lengths[None, :] <= upper)
    return inside & (firsts[None, :] == seg_query) & (lasts[None, :] == seg_query)

def attention(queries, keys, values, seg_row):
    head_width = HEADS * HEAD_DIM
    tail_len = BLOCK * 2 ** (FINE - 1)
    paired = jnp.concatenate([keys, values], axis=1)
    padded = jnp.concatenate([jnp.zeros((tail_len, 2 * head_width), jnp.float32), paired], axis=0)
    base_cells = cell_means(paired, 2 ** FINE)
    coarse = jnp.concatenate([base_cells] + [cell_means(base_cells, 2 ** (level_at - FINE)) for level_at in range(FINE + 1, LEVELS)], axis=0)

    def one_block(block_index):
        offset = block_index * TOK_DEV
        window = lax.dynamic_slice_in_dim(padded, offset, tail_len + TOK_DEV)
        table = jnp.concatenate([window] + [cell_means(window, 2 ** level_at) for level_at in range(1, FINE)] + [coarse], axis=0)
        layout = candidates(offset, seg_row, tail_len, TOK_DEV)
        allowed = valid_mask(offset, seg_row, layout, TOK_DEV)
        level_bias = layout[2].astype(jnp.float32) * LOG_TWO
        query_heads = lax.dynamic_slice_in_dim(queries, offset, TOK_DEV).reshape(TOK_DEV, HEADS, HEAD_DIM)
        key_heads = table[:, :head_width].reshape(-1, HEADS, HEAD_DIM)
        value_heads = table[:, head_width:].reshape(-1, HEADS, HEAD_DIM)
        raw = low_back(jnp.einsum('thd,khd->htk', query_heads, key_heads, precision=lax.Precision.HIGHEST) * HEAD_DIM ** (-0.5))
        scores = jnp.where(allowed[None], raw + level_bias[None, None, :], NEGATIVE)
        row_top = lax.optimization_barrier(jnp.max(scores, axis=-1, keepdims=True))
        exponent = jnp.exp(scores - row_top)
        weights = exponent / lax.optimization_barrier(jnp.sum(exponent, axis=-1, keepdims=True))
        mixed = jnp.einsum('htk,khd->thd', low(weights), value_heads, precision=lax.Precision.HIGHEST)
        return mixed.reshape(TOK_DEV, head_width)
    blocks = lax.map(jax.checkpoint(one_block), jnp.arange(seg_row.shape[0] // TOK_DEV, dtype=jnp.int32))
    return blocks.reshape(seg_row.shape[0], head_width)

def layer(source, params, seg_row):
    norm1_gain, norm1_bias, q_weight, q_bias, k_weight, v_weight, v_bias, out_weight, out_bias, norm2_gain, norm2_bias, up_weight, up_bias, down_weight, down_bias = params
    normed1 = low(layer_norm(source, norm1_gain, norm1_bias))
    queries = low(low_back(matmul(normed1, q_weight) + q_bias))
    keys = low(low_back(matmul(normed1, k_weight)))
    values = low(low_back(matmul(normed1, v_weight) + v_bias))
    mixed = low(low_back(attention(queries, keys, values, seg_row)))
    middle = source + low_back(matmul(mixed, out_weight)) + out_bias
    normed2 = low(layer_norm(middle, norm2_gain, norm2_bias))
    pre_active = low_back(matmul(normed2, up_weight) + up_bias)
    hidden = low(low_back(pre_active * jax.nn.sigmoid(pre_active)))
    return middle + low_back(matmul(hidden, down_weight)) + down_bias

def reference(x_in, grad_out, seg_ids, norm1_gain, norm1_bias, q_weight, q_bias, k_weight, v_weight, v_bias, out_weight, out_bias, norm2_gain, norm2_bias, up_weight, up_bias, down_weight, down_bias):
    params = (norm1_gain, norm1_bias, q_weight.astype(jnp.float32), q_bias, k_weight.astype(jnp.float32), v_weight.astype(jnp.float32), v_bias, out_weight.astype(jnp.float32), out_bias, norm2_gain, norm2_bias, up_weight.astype(jnp.float32), up_bias, down_weight.astype(jnp.float32), down_bias)

    def micro_step(carried, inputs_now):
        source_rows, upstream, seg_row = inputs_now
        result, pullback = jax.vjp(lambda rows_in, weights_in: layer(rows_in, weights_in, seg_row), source_rows.astype(jnp.float32), params)
        d_source, d_params = pullback(upstream.astype(jnp.float32))
        return (jax.tree.map(jnp.add, carried, d_params), (result, d_source))
    zero_grads = jax.tree.map(jnp.zeros_like, params)
    totals, (layer_out, input_grad) = lax.scan(micro_step, zero_grads, (x_in, grad_out, seg_ids))
    return (layer_out, input_grad, totals[0], totals[1], totals[2], totals[3], totals[4], totals[5], totals[6], totals[7], totals[8], totals[9], totals[10], totals[11], totals[12], totals[13], totals[14])
```

```python
import functools

import jax
import jax.numpy as jnp
from jax import lax
from jax.experimental import pallas as pl
from jax.experimental.pallas import tpu as pltpu
from jax.sharding import PartitionSpec as P

HEAD_DIM = 64
BLOCK = 16
LEVELS = 10
FINE = 3
EPSILON = 1e-05
NEGATIVE = -1e30
LOG_TWO = 0.6931471805599453
LANES = 128
BF16 = jnp.bfloat16
F32 = jnp.float32


def dot(left, right, dims):
    return lax.dot_general(left, right, (dims, ((), ())), preferred_element_type=F32)


def dot_nn(left, right):
    return dot(left, right, ((1,), (0,)))


def dot_nt(left, right):
    return dot(left, right, ((1,), (1,)))


def dot_tn(left, right):
    return dot(left, right, ((0,), (0,)))


def norm_parts(source):
    centre = jnp.mean(source, axis=-1, keepdims=True)
    centred = source - centre
    variance = jnp.mean(centred * centred, axis=-1, keepdims=True)
    inverse = lax.rsqrt(variance + EPSILON)
    return centred * inverse, inverse


def norm_backward(upstream, normed, inverse, gain):
    scaled = upstream * gain
    first_mean = jnp.mean(scaled, axis=-1, keepdims=True)
    second_mean = jnp.mean(scaled * normed, axis=-1, keepdims=True)
    return inverse * (scaled - first_mean - normed * second_mean)


def iota(shape, axis):
    return lax.broadcasted_iota(jnp.int32, shape, axis)


class Geometry:
    def __init__(self, ctx, wt, tok_dev):
        self.ctx, self.wt, self.tok_dev = ctx, wt, tok_dev
        tokens = ctx * tok_dev
        self.levels = len([l for l in range(LEVELS) if BLOCK * 2**l < tokens])
        self.own_cells = [tok_dev // 2**l if l <= FINE else 0 for l in range(self.levels)]
        self.tile = tok_dev // 2
        self.tile_slots = [BLOCK + self.tile] + [BLOCK * 4 >> (l - 1) if l < FINE else BLOCK for l in range(1, self.levels)]
        self.slots = sum(self.tile_slots)
        self.slot_at = [sum(self.tile_slots[:l]) for l in range(self.levels + 1)]
        self.far = self.levels - (FINE + 2)
        self.near = FINE + 2


def pool_matrix():
    parts = []
    for level, count in ((1, 128), (2, 64), (3, 32)):
        hit = (iota((count, 256), 1) >> level) == iota((count, 256), 0)
        parts.append(jnp.where(hit, 1.0 / 2**level, 0.0))
    return jnp.concatenate(parts, axis=0).astype(BF16)


def coarse_matrix():
    row, column = iota((32, 32), 0), iota((32, 32), 1)
    out = jnp.zeros((32, 32), F32)
    first = 0
    for level, count in ((4, 16), (5, 8), (6, 4), (7, 2), (8, 1)):
        up = level - FINE
        hit = (row >= first) & (row < first + count) & ((column >> up) == row - first)
        out = jnp.where(hit, 1.0 / 2**up, out)
        first += count
    return out.astype(BF16)


def far_matrix(geo, me):
    parts = []
    first = 0
    for step in range(geo.far):
        up = step + 1
        each = BLOCK >> up
        row, column = iota((BLOCK, geo.ctx * BLOCK), 0), iota((BLOCK, geo.ctx * BLOCK), 1)
        group = (me >> up) - 1
        device = (group << up) + (row >> (4 - up))
        wanted = device * BLOCK + first + (row & (each - 1))
        parts.append(jnp.where((column == wanted) & (group >= 0), 1.0, 0.0))
        first += each
    return jnp.concatenate(parts, axis=0).astype(BF16)


def mask_bias(geo, me, segs, tile):
    first_pos = me * geo.tok_dev + tile * geo.tile
    seg_one = jnp.sum((segs < 1).astype(jnp.int32), axis=1, keepdims=True)
    seg_two = jnp.sum((segs < 2).astype(jnp.int32), axis=1, keepdims=True)
    position = first_pos + iota((1, geo.tile), 1)
    begins = jnp.where(position >= seg_two, seg_two, jnp.where(position >= seg_one, seg_one, 0))
    parts = []
    for level in range(geo.levels):
        size, shift = 2**level, level + 4
        count = geo.tile_slots[level]
        span = BLOCK * size
        if level <= FINE:
            base = first_pos - span
        else:
            base = (((me * geo.tok_dev) >> shift) - 1) << shift
        begin = base + size * iota((count, geo.tile), 0)
        lower = jnp.maximum(((position >> shift) - 1) << shift, begins)
        if level == 0:
            upper = position + 1
        else:
            upper = ((position >> (shift - 1)) - 1) << (shift - 1)
        valid = (begin >= lower) & (begin + size <= upper)
        parts.append(jnp.where(valid, level * LOG_TWO, NEGATIVE))
    return jnp.concatenate(parts, axis=0)


def both_heads(pair):
    lane = iota(pair.shape, 1)
    zero = jnp.zeros_like(pair)
    return jnp.concatenate([jnp.where(lane < HEAD_DIM, pair, zero), jnp.where(lane >= HEAD_DIM, pair, zero)], axis=0)


def own_lanes(stacked):
    rows = stacked.shape[0] // 2
    lane = iota((rows, stacked.shape[1]), 1)
    return jnp.where(lane < HEAD_DIM, stacked[:rows], stacked[rows:])


def project(geo, x, gain, shift, wa, extra, n1, q, own, cells, near, far):
    normed, _ = norm_parts(x[...].astype(F32))
    n1[...] = (normed * gain[...] + shift[...]).astype(BF16)
    pool, coarse = pool_matrix(), coarse_matrix()

    def shard(w, carry):
        out = dot_nn(n1[...], wa[w, :, : 3 * LANES])
        bias = extra[w, 1:2, :]
        q[w] = ((out[:, :LANES] + bias[:, :LANES]).astype(BF16) * 0.125).astype(BF16)
        kv = jnp.concatenate(
            [out[:, LANES : 2 * LANES], out[:, 2 * LANES :] + bias[:, LANES : 2 * LANES]], axis=1
        ).astype(BF16)
        own[w] = kv
        fine = dot_nn(pool, kv).astype(BF16)
        cells[w] = fine
        rough = dot_nn(coarse, fine[192:224]).astype(BF16)
        near[w, 0:16] = kv[240:256]
        near[w, 16:32] = fine[112:128]
        near[w, 32:48] = fine[176:192]
        near[w, 48:64] = fine[208:224]
        near[w, 64:80] = rough[0:16]
        far[w] = rough[16:32]
        return carry

    lax.fori_loop(0, geo.wt, shard, 0)


def tables(geo, me, own, cells, near_in, far_in, table):
    pick = far_matrix(geo, me)

    def shard(w, carry):
        rough = dot_nn(pick, far_in[w]).astype(BF16)
        at = geo.slot_at
        table[w, 0, 0:16] = near_in[w, 0:16]
        table[w, 0, 16:144] = own[w, 0:128]
        table[w, 1, 0:144] = own[w, 112:256]
        table[w, 0, at[1] : at[1] + 16] = near_in[w, 16:32]
        table[w, 0, at[1] + 16 : at[2]] = cells[w, 0:48]
        table[w, 1, at[1] : at[2]] = cells[w, 48:112]
        table[w, 0, at[2] : at[2] + 16] = near_in[w, 32:48]
        table[w, 0, at[2] + 16 : at[3]] = cells[w, 128:144]
        table[w, 1, at[2] : at[3]] = cells[w, 144:176]
        table[w, 0, at[3] : at[4]] = near_in[w, 48:64]
        table[w, 1, at[3] : at[4]] = cells[w, 192:208]
        for tile in (0, 1):
            table[w, tile, at[4] : at[5]] = near_in[w, 64:80]
            table[w, tile, at[5] :] = rough
        return carry

    lax.fori_loop(0, geo.wt, shard, 0)


def attend(geo, q, table, bias, probs, mixed):
    def shard(w, carry):
        for tile in (0, 1):
            rows = slice(tile * geo.tile, (tile + 1) * geo.tile)
            both = both_heads(q[w, rows, :])
            level_bias = bias[tile]
            scores = dot_nt(table[w, tile, :, :LANES], both)
            scores = scores + jnp.concatenate([level_bias, level_bias], axis=1)
            top = jnp.max(scores, axis=0, keepdims=True)
            exponent = jnp.exp(scores - top)
            total = jnp.sum(exponent, axis=0, keepdims=True)
            low = (exponent * (1.0 / total)).astype(BF16)
            probs[w, tile] = low
            mixed[w, rows, :] = own_lanes(dot_tn(low, table[w, tile, :, LANES:])).astype(BF16)
        return carry

    lax.fori_loop(0, geo.wt, shard, 0)


def attend_back(geo, q, table, probs, d_mixed, d_queries, d_table):
    def shard(w, carry):
        for tile in (0, 1):
            rows = slice(tile * geo.tile, (tile + 1) * geo.tile)
            both = both_heads(q[w, rows, :])
            d_both = both_heads(d_mixed[w, rows, :])
            low = probs[w, tile]
            d_probs = dot_nt(table[w, tile, :, LANES:], d_both)
            wide = low.astype(F32)
            product = wide * d_probs
            centre = jnp.sum(product, axis=0, keepdims=True)
            d_scores = (product - wide * centre).astype(BF16)
            d_table[w, tile, :, :LANES] = dot_nn(d_scores, both)
            d_table[w, tile, :, LANES:] = dot_nn(low, d_both)
            back = own_lanes(dot_tn(d_scores, table[w, tile, :, :LANES]))
            d_queries[w, rows, :] = (back * 0.125).astype(BF16)
        return carry

    lax.fori_loop(0, geo.wt, shard, 0)


def return_cells(geo, me, d_table, near, far):
    pick = far_matrix(geo, me)
    at = geo.slot_at

    def shard(w, carry):
        near[w, 0:16] = d_table[w, 0, 0:16].astype(BF16)
        near[w, 16:32] = d_table[w, 0, at[1] : at[1] + 16].astype(BF16)
        near[w, 32:48] = d_table[w, 0, at[2] : at[2] + 16].astype(BF16)
        near[w, 48:64] = d_table[w, 0, at[3] : at[4]].astype(BF16)
        near[w, 64:80] = (d_table[w, 0, at[4] : at[5]] + d_table[w, 1, at[4] : at[5]]).astype(BF16)
        rough = (d_table[w, 0, at[5] :] + d_table[w, 1, at[5] :]).astype(BF16)
        far[w] = dot_tn(pick, rough).astype(BF16)
        return carry

    lax.fori_loop(0, geo.wt, shard, 0)


def own_gradients(geo, w, d_table, near_back, far_back):
    at = geo.slot_at
    first, second = d_table.at[w, 0], d_table.at[w, 1]
    back = near_back[w].astype(F32)
    tokens = jnp.concatenate(
        [first[16:128], first[128:144] + second[0:16], second[16:128], second[128:144] + back[0:16]], axis=0
    )
    rough = jnp.concatenate([back[64:80], far_back], axis=0)
    fine = dot_tn(coarse_matrix(), rough.astype(BF16))
    level3 = jnp.concatenate([second[at[3] : at[4]], back[48:64]], axis=0) + fine
    cells = jnp.concatenate(
        [
            first[at[1] + 16 : at[2]],
            second[at[1] : at[2]],
            back[16:32],
            first[at[2] + 16 : at[3]],
            second[at[2] : at[3]],
            back[32:48],
            level3,
        ],
        axis=0,
    )
    return tokens + dot_tn(pool_matrix(), cells.astype(BF16))


def forward_rest(geo, x, out_shift, gain, shift, wa, extra, up, down, down_shift, mixed, middle, n2, hidden, slope, result):
    middle[...] = x[...].astype(F32) + out_shift[...]

    def shard(w, carry):
        middle[...] += dot_nt(mixed[w], wa[w, :, 3 * LANES :])
        return carry

    lax.fori_loop(0, geo.wt, shard, 0)
    normed, _ = norm_parts(middle[...])
    n2[...] = (normed * gain[...] + shift[...]).astype(BF16)
    result[...] = middle[...] + down_shift[...]

    def ff(w, carry):
        pre = dot_nn(n2[...], up[w]) + extra[w, 0:1, :]
        gate = jax.nn.sigmoid(pre)
        hidden[w] = (pre * gate).astype(BF16)
        slope[w] = gate * (1.0 + pre * (1.0 - gate))
        result[...] += dot_nn(hidden[w], down[w])
        return carry

    lax.fori_loop(0, geo.wt, ff, 0)


def feed_back(geo, g2, gain, wa, up, down, middle, n2, hidden, slope, mixed, g1, d_mixed, sums, grads, total):
    total[...] = jnp.zeros_like(total)

    def ff(w, carry):
        d_hidden = dot_nt(g2[...], down[w]).astype(BF16).astype(F32)
        d_up = (d_hidden * slope[w]).astype(BF16)
        sums[w, 0:1, :] = jnp.sum(d_up.astype(F32), axis=0, keepdims=True)
        grads[2, w] = dot_tn(hidden[w], g2[...]).astype(BF16)
        grads[1, w] = dot_tn(n2[...], d_up).astype(BF16)
        total[...] += dot_nt(d_up, up[w])
        return carry

    lax.fori_loop(0, geo.wt, ff, 0)
    normed, inverse = norm_parts(middle[...])
    d_normed = total[...]
    wide = g2[...].astype(F32)
    first = wide + norm_backward(d_normed, normed, inverse, gain[...])
    g1[...] = first
    low = first.astype(BF16)

    def add(column, row):
        for w in range(geo.wt):
            sums[w, 2 + column // 4 : 3 + column // 4, (column % 4) * LANES : (column % 4 + 1) * LANES] = row[
                :, w * LANES : (w + 1) * LANES
            ]

    add(2, jnp.sum(first, axis=0, keepdims=True))
    add(3, jnp.sum(d_normed * normed, axis=0, keepdims=True))
    add(4, jnp.sum(d_normed, axis=0, keepdims=True))
    add(5, jnp.sum(wide, axis=0, keepdims=True))

    def out(w, carry):
        d_mixed[w] = dot_nn(low, wa[w, :, 3 * LANES :]).astype(BF16)
        grads[0, w, :, 3 * LANES :] = dot_tn(low, mixed[w]).astype(BF16)
        return carry

    lax.fori_loop(0, geo.wt, out, 0)


def project_back(geo, x, gain, wa, n1, g1, d_queries, d_table, near_back, far_back, sums, grads, total, d_source):
    total[...] = jnp.zeros_like(total)

    def shard(w, carry):
        far = far_back[w, 0].astype(F32)
        for step in range(1, far_back.shape[1]):
            far = far + far_back[w, step].astype(F32)
        kv = own_gradients(geo, w, d_table, near_back, far).astype(BF16)
        d_qkv = jnp.concatenate([d_queries[w], kv], axis=1)
        sums[w, 1:2, :LANES] = jnp.sum(d_qkv[:, :LANES].astype(F32), axis=0, keepdims=True)
        sums[w, 1:2, LANES : 2 * LANES] = jnp.sum(d_qkv[:, 2 * LANES :].astype(F32), axis=0, keepdims=True)
        grads[w, :, : 3 * LANES] = dot_tn(n1[...], d_qkv).astype(BF16)
        total[...] += dot_nt(d_qkv, wa[w, :, : 3 * LANES])
        return carry

    lax.fori_loop(0, geo.wt, shard, 0)
    normed, inverse = norm_parts(x[...].astype(F32))
    d_normed = total[...]
    d_source[...] = (g1[...] + norm_backward(d_normed, normed, inverse, gain[...])).astype(d_source.dtype)
    rows = (jnp.sum(d_normed * normed, axis=0, keepdims=True), jnp.sum(d_normed, axis=0, keepdims=True))
    for w in range(geo.wt):
        for column, row in enumerate(rows):
            sums[w, 2:3, column * LANES : (column + 1) * LANES] = row[:, w * LANES : (w + 1) * LANES]


def shards(
    x_in,
    grad_out,
    seg_ids,
    norm1_gain,
    norm1_bias,
    q_weight,
    q_bias,
    k_weight,
    v_weight,
    v_bias,
    out_weight,
    out_bias,
    norm2_gain,
    norm2_bias,
    up_weight,
    up_bias,
    down_weight,
    down_bias,
):
    ctx, wt = lax.axis_size("ctx"), lax.axis_size("wt")
    runs, tok_dev, width = x_in.shape
    geo = Geometry(ctx, wt, tok_dev)
    z = lax.axis_index("wt")
    me_out = lax.axis_index("ctx")
    x = lax.dynamic_index_in_dim(x_in, z, 0, keepdims=False)
    g2 = lax.dynamic_index_in_dim(grad_out, z, 0, keepdims=False)
    segs = lax.dynamic_index_in_dim(seg_ids, z, 0, keepdims=True)
    row = lambda v: v.reshape(1, -1)
    wa_own = jnp.concatenate([q_weight, k_weight, v_weight, out_weight.T], axis=1)
    extra_own = jnp.zeros((8, up_bias.shape[0]), F32)
    extra_own = extra_own.at[0].set(up_bias).at[1, :128].set(q_bias).at[1, 128:256].set(v_bias)
    wa, up, down, extra = (lax.all_gather(t, "wt") for t in (wa_own, up_weight, down_weight, extra_own))
    sds = jax.ShapeDtypeStruct
    params = pltpu.CompilerParams(vmem_limit_bytes=60 * 2**20)
    T = tok_dev

    def call(body, outs, *args):
        return pl.pallas_call(body, out_shape=outs, compiler_params=params)(*args)

    n1, q, own, cells, near, far = call(
        functools.partial(project, geo),
        [
            sds((T, width), BF16),
            sds((wt, T, LANES), BF16),
            sds((wt, T, 256), BF16),
            sds((wt, 224, 256), BF16),
            sds((wt, 80, 256), BF16),
            sds((wt, 16, 256), BF16),
        ],
        x, row(norm1_gain), row(norm1_bias), wa, extra,
    )
    near_in = lax.ppermute(near, "ctx", [(i, i + 1) for i in range(ctx - 1)])
    far_in = lax.all_gather(far, "ctx", axis=1).reshape(wt, ctx * 16, 256)

    def middle_body(x, g2, segs, out_b, n2g, n2b, wa, extra, up, down, down_b, q, own, cells, near_in, far_in,
                    result, g1, d_queries, d_table, near_out, far_out, sums, grads,
                    table, bias, probs, mixed, mid, n2, hidden, slope, d_mixed, total):
        me = lax.axis_index("ctx")
        bias[0] = mask_bias(geo, me, segs[...], 0)
        bias[1] = mask_bias(geo, me, segs[...], 1)
        tables(geo, me, own, cells, near_in, far_in, table)
        attend(geo, q, table, bias, probs, mixed)
        forward_rest(geo, x, out_b, n2g, n2b, wa, extra, up, down, down_b, mixed, mid, n2, hidden, slope, result)
        sums[...] = jnp.zeros_like(sums)
        feed_back(geo, g2, n2g, wa, up, down, mid, n2, hidden, slope, mixed, g1, d_mixed, sums, grads, total)
        attend_back(geo, q, table, probs, d_mixed, d_queries, d_table)
        return_cells(geo, me, d_table, near_out, far_out)

    S = geo.slots
    result, g1, d_queries, d_table, near_out, far_out, sums, grads = pl.pallas_call(
        middle_body,
        out_shape=[
            sds((T, width), F32),
            sds((T, width), F32),
            sds((wt, T, LANES), BF16),
            sds((wt, 2, S, 256), F32),
            sds((wt, 80, 256), BF16),
            sds((wt, ctx * 16, 256), BF16),
            sds((wt, 8, 512), F32),
            sds((3, wt, 512, 512), BF16),
        ],
        scratch_shapes=[
            pltpu.VMEM((wt, 2, S, 256), BF16),
            pltpu.VMEM((2, S, T // 2), F32),
            pltpu.VMEM((wt, 2, S, 256), BF16),
            pltpu.VMEM((wt, T, LANES), BF16),
            pltpu.VMEM((T, width), F32),
            pltpu.VMEM((T, width), BF16),
            pltpu.VMEM((wt, T, 512), BF16),
            pltpu.VMEM((wt, T, 512), F32),
            pltpu.VMEM((wt, T, LANES), BF16),
            pltpu.VMEM((T, width), F32),
        ],
        compiler_params=params,
    )(x, g2, segs, row(out_bias), row(norm2_gain), row(norm2_bias), wa, extra, up, down, row(down_bias), q, own, cells, near_in, far_in)
    near_back = lax.ppermute(near_out, "ctx", [(i + 1, i) for i in range(ctx - 1)])
    far_back = lax.psum_scatter(far_out, "ctx", scatter_dimension=1, tiled=True).reshape(wt, 1, 16, 256)

    def last_body(x, n1g, wa, n1, g1, d_queries, d_table, near_back, far_back, sums_in, grads_in, d_source, sums, grads, total):
        sums[...] = sums_in[...]
        grads[...] = grads_in[...]
        project_back(geo, x, n1g, wa, n1, g1, d_queries, d_table, near_back, far_back, sums, grads, total, d_source)

    d_source, sums, grads0 = pl.pallas_call(
        last_body,
        out_shape=[sds((T, width), F32), sds((wt, 8, 512), F32), sds((wt, 512, 512), BF16)],
        scratch_shapes=[pltpu.VMEM((T, width), F32)],
        compiler_params=params,
    )(x, row(norm1_gain), wa, n1, g1, d_queries, d_table, near_back, far_back, sums, grads[0])
    layer_rows = lax.all_gather(result.astype(BF16), "wt").astype(F32)
    grad_rows = lax.all_gather(d_source.astype(BF16), "wt").astype(F32)
    grads = jnp.stack([grads0, grads[1], grads[2]])
    mine = lax.psum(lax.psum_scatter(grads, "wt", scatter_dimension=1, tiled=True), "ctx").astype(F32)[:, 0]
    small = lax.psum(lax.psum_scatter(sums, "wt", scatter_dimension=0, tiled=True), "ctx")[0]
    d_a = mine[0]
    return (
        layer_rows,
        grad_rows,
        small[2, 0:128],
        small[2, 128:256],
        d_a[:, :128],
        small[1, :128],
        d_a[:, 128:256],
        d_a[:, 256:384],
        small[1, 128:256],
        d_a[:, 384:].T,
        small[2, 256:384],
        small[2, 384:512],
        small[3, 0:128],
        mine[1],
        small[0],
        mine[2],
        small[3, 128:256],
    )


def solution(mesh):
    in_specs = (
        P(None, "ctx", None),
        P(None, "ctx", None),
        P(),
        P(),
        P(),
        P(None, "wt"),
        P("wt"),
        P(None, "wt"),
        P(None, "wt"),
        P("wt"),
        P("wt", None),
        P(),
        P(),
        P(),
        P(None, "wt"),
        P("wt"),
        P("wt", None),
        P(),
    )
    out_specs = (
        P(None, "ctx", None),
        P(None, "ctx", None),
        P("wt"),
        P("wt"),
        P(None, "wt"),
        P("wt"),
        P(None, "wt"),
        P(None, "wt"),
        P("wt"),
        P("wt", None),
        P("wt"),
        P("wt"),
        P("wt"),
        P(None, "wt"),
        P("wt"),
        P("wt", None),
        P("wt"),
    )
    return jax.shard_map(shards, mesh=mesh, in_specs=in_specs, out_specs=out_specs, check_vma=False)
```

```python
import functools

import jax
import jax.numpy as jnp
from jax import lax
from jax.experimental import pallas as pl
from jax.experimental.pallas import tpu as pltpu
from jax.sharding import PartitionSpec as P

HEAD_DIM = 64
BLOCK = 16
LEVELS = 10
FINE = 3
EPSILON = 1e-05
NEGATIVE = -1e30
LOG_TWO = 0.6931471805599453
LANES = 128
BF16 = jnp.bfloat16
F32 = jnp.float32


def dot(left, right, dims):
    return lax.dot_general(left, right, (dims, ((), ())), preferred_element_type=F32)


def dot_nn(left, right):
    return dot(left, right, ((1,), (0,)))


def dot_nt(left, right):
    return dot(left, right, ((1,), (1,)))


def dot_tn(left, right):
    return dot(left, right, ((0,), (0,)))


def norm_parts(source):
    centre = jnp.mean(source, axis=-1, keepdims=True)
    centred = source - centre
    variance = jnp.mean(centred * centred, axis=-1, keepdims=True)
    inverse = lax.rsqrt(variance + EPSILON)
    return centred * inverse, inverse


def norm_backward(upstream, normed, inverse, gain):
    scaled = upstream * gain
    first_mean = jnp.mean(scaled, axis=-1, keepdims=True)
    second_mean = jnp.mean(scaled * normed, axis=-1, keepdims=True)
    return inverse * (scaled - first_mean - normed * second_mean)


def iota(shape, axis):
    return lax.broadcasted_iota(jnp.int32, shape, axis)


class Geometry:
    def __init__(self, ctx, wt, tok_dev):
        self.ctx, self.wt, self.tok_dev = ctx, wt, tok_dev
        tokens = ctx * tok_dev
        self.levels = len([l for l in range(LEVELS) if BLOCK * 2**l < tokens])
        self.own_cells = [tok_dev // 2**l if l <= FINE else 0 for l in range(self.levels)]
        self.tile = tok_dev // 2
        self.tile_slots = [BLOCK + self.tile] + [BLOCK * 4 >> (l - 1) if l < FINE else BLOCK for l in range(1, self.levels)]
        self.slots = sum(self.tile_slots)
        self.slot_at = [sum(self.tile_slots[:l]) for l in range(self.levels + 1)]
        self.far = self.levels - (FINE + 2)
        self.near = FINE + 2


def pool_matrix():
    parts = []
    for level, count in ((1, 128), (2, 64), (3, 32)):
        hit = (iota((count, 256), 1) >> level) == iota((count, 256), 0)
        parts.append(jnp.where(hit, 1.0 / 2**level, 0.0))
    return jnp.concatenate(parts, axis=0).astype(BF16)


def coarse_matrix():
    row, column = iota((32, 32), 0), iota((32, 32), 1)
    out = jnp.zeros((32, 32), F32)
    first = 0
    for level, count in ((4, 16), (5, 8), (6, 4), (7, 2), (8, 1)):
        up = level - FINE
        hit = (row >= first) & (row < first + count) & ((column >> up) == row - first)
        out = jnp.where(hit, 1.0 / 2**up, out)
        first += count
    return out.astype(BF16)


def far_matrix(geo, me):
    parts = []
    first = 0
    for step in range(geo.far):
        up = step + 1
        each = BLOCK >> up
        row, column = iota((BLOCK, geo.ctx * BLOCK), 0), iota((BLOCK, geo.ctx * BLOCK), 1)
        group = (me >> up) - 1
        device = (group << up) + (row >> (4 - up))
        wanted = device * BLOCK + first + (row & (each - 1))
        parts.append(jnp.where((column == wanted) & (group >= 0), 1.0, 0.0))
        first += each
    return jnp.concatenate(parts, axis=0).astype(BF16)


def mask_bias(geo, me, segs, tile):
    first_pos = me * geo.tok_dev + tile * geo.tile
    seg_one = jnp.sum((segs < 1).astype(jnp.int32), axis=1, keepdims=True)
    seg_two = jnp.sum((segs < 2).astype(jnp.int32), axis=1, keepdims=True)
    position = first_pos + iota((1, geo.tile), 1)
    begins = jnp.where(position >= seg_two, seg_two, jnp.where(position >= seg_one, seg_one, 0))
    parts = []
    for level in range(geo.levels):
        size, shift = 2**level, level + 4
        count = geo.tile_slots[level]
        span = BLOCK * size
        if level <= FINE:
            base = first_pos - span
        else:
            base = (((me * geo.tok_dev) >> shift) - 1) << shift
        begin = base + size * iota((count, geo.tile), 0)
        lower = jnp.maximum(((position >> shift) - 1) << shift, begins)
        if level == 0:
            upper = position + 1
        else:
            upper = ((position >> (shift - 1)) - 1) << (shift - 1)
        valid = (begin >= lower) & (begin + size <= upper)
        parts.append(jnp.where(valid, level * LOG_TWO, NEGATIVE))
    return jnp.concatenate(parts, axis=0)


def both_heads(pair):
    lane = iota(pair.shape, 1)
    zero = jnp.zeros_like(pair)
    return jnp.concatenate([jnp.where(lane < HEAD_DIM, pair, zero), jnp.where(lane >= HEAD_DIM, pair, zero)], axis=0)


def own_lanes(stacked):
    rows = stacked.shape[0] // 2
    lane = iota((rows, stacked.shape[1]), 1)
    return jnp.where(lane < HEAD_DIM, stacked[:rows], stacked[rows:])


def project(w, n1, weights, extra, q, own, cells, near, far):
    out = dot_nn(n1[...], weights[0, w, :, : 3 * LANES])
    bias = extra[w, 1:2, :]
    q[w] = ((out[:, :LANES] + bias[:, :LANES]).astype(BF16) * 0.125).astype(BF16)
    kv = jnp.concatenate(
        [out[:, LANES : 2 * LANES], out[:, 2 * LANES :] + bias[:, LANES : 2 * LANES]], axis=1
    ).astype(BF16)
    own[w] = kv
    fine = dot_nn(pool_matrix(), kv).astype(BF16)
    cells[w] = fine
    rough = dot_nn(coarse_matrix(), fine[192:224]).astype(BF16)
    near[w, 0:16] = kv[240:256]
    near[w, 16:32] = fine[112:128]
    near[w, 32:48] = fine[176:192]
    near[w, 48:64] = fine[208:224]
    near[w, 64:80] = rough[0:16]
    far[w] = rough[16:32]


def tables(geo, w, pick, own, cells, near_in, far_in, table):
    blocks = far_in[:, w].reshape(geo.ctx * BLOCK, 2 * LANES)
    rough = dot_nn(pick, blocks).astype(BF16)
    at = geo.slot_at
    table[w, 0, 0:16] = near_in[w, 0:16]
    table[w, 0, 16:144] = own[w, 0:128]
    table[w, 1, 0:144] = own[w, 112:256]
    table[w, 0, at[1] : at[1] + 16] = near_in[w, 16:32]
    table[w, 0, at[1] + 16 : at[2]] = cells[w, 0:48]
    table[w, 1, at[1] : at[2]] = cells[w, 48:112]
    table[w, 0, at[2] : at[2] + 16] = near_in[w, 32:48]
    table[w, 0, at[2] + 16 : at[3]] = cells[w, 128:144]
    table[w, 1, at[2] : at[3]] = cells[w, 144:176]
    table[w, 0, at[3] : at[4]] = near_in[w, 48:64]
    table[w, 1, at[3] : at[4]] = cells[w, 192:208]
    for tile in (0, 1):
        table[w, tile, at[4] : at[5]] = near_in[w, 64:80]
        table[w, tile, at[5] :] = rough


def attend(geo, w, tile, q, table, bias, probs, mixed):
    rows = slice(tile * geo.tile, (tile + 1) * geo.tile)
    both = both_heads(q[w, rows, :])
    level_bias = bias[tile]
    scores = dot_nt(table[w, tile, :, :LANES], both)
    scores = scores + jnp.concatenate([level_bias, level_bias], axis=1)
    top = jnp.max(scores, axis=0, keepdims=True)
    exponent = jnp.exp(scores - top)
    total = jnp.sum(exponent, axis=0, keepdims=True)
    low = (exponent * (1.0 / total)).astype(BF16)
    probs[w, tile] = low
    mixed[w, rows, :] = own_lanes(dot_tn(low, table[w, tile, :, LANES:])).astype(BF16)


def attend_back(geo, w, tile, q, table, probs, d_mixed, d_queries, d_table):
    rows = slice(tile * geo.tile, (tile + 1) * geo.tile)
    both = both_heads(q[w, rows, :])
    d_both = both_heads(d_mixed[w, rows, :])
    low = probs[w, tile]
    d_probs = dot_nt(table[w, tile, :, LANES:], d_both)
    wide = low.astype(F32)
    product = wide * d_probs
    centre = jnp.sum(product, axis=0, keepdims=True)
    d_scores = (product - wide * centre).astype(BF16)
    d_table[w, tile, :, :LANES] = dot_nn(d_scores, both)
    d_table[w, tile, :, LANES:] = dot_nn(low, d_both)
    back = own_lanes(dot_tn(d_scores, table[w, tile, :, :LANES]))
    d_queries[w, rows, :] = (back * 0.125).astype(BF16)


def return_cells(geo, w, pick, d_table, near, far):
    at = geo.slot_at
    near[w, 0:16] = d_table[w, 0, 0:16].astype(BF16)
    near[w, 16:32] = d_table[w, 0, at[1] : at[1] + 16].astype(BF16)
    near[w, 32:48] = d_table[w, 0, at[2] : at[2] + 16].astype(BF16)
    near[w, 48:64] = d_table[w, 0, at[3] : at[4]].astype(BF16)
    near[w, 64:80] = (d_table[w, 0, at[4] : at[5]] + d_table[w, 1, at[4] : at[5]]).astype(BF16)
    rough = (d_table[w, 0, at[5] :] + d_table[w, 1, at[5] :]).astype(BF16)
    far[:, w] = dot_tn(pick, rough).astype(BF16).reshape(geo.ctx, BLOCK, 2 * LANES)


def own_gradients(geo, w, d_table, near_back, far_back):
    at = geo.slot_at
    first, second = d_table.at[w, 0], d_table.at[w, 1]
    back = near_back[w].astype(F32)
    tokens = jnp.concatenate(
        [first[16:128], first[128:144] + second[0:16], second[16:128], second[128:144] + back[0:16]], axis=0
    )
    far = jnp.sum(far_back[:, w].astype(F32), axis=0)
    rough = jnp.concatenate([back[64:80], far], axis=0)
    fine = dot_tn(coarse_matrix(), rough.astype(BF16))
    level3 = jnp.concatenate([second[at[3] : at[4]], back[48:64]], axis=0) + fine
    cells = jnp.concatenate(
        [
            first[at[1] + 16 : at[2]],
            second[at[1] : at[2]],
            back[16:32],
            first[at[2] + 16 : at[3]],
            second[at[2] : at[3]],
            back[32:48],
            level3,
        ],
        axis=0,
    )
    return tokens + dot_tn(pool_matrix(), cells.astype(BF16))


def feed(w, n2, weights, extra, hidden, slope, result):
    pre = dot_nn(n2[...], weights[1, w]) + extra[w, 0:1, :]
    gate = jax.nn.sigmoid(pre)
    hidden[w] = (pre * gate).astype(BF16)
    slope[w] = gate * (1.0 + pre * (1.0 - gate))
    result[...] += dot_nn(hidden[w], weights[2, w])


def feed_back(w, g2, weights, n2, hidden, slope, sums, grads, total):
    d_hidden = dot_nt(g2[...], weights[2, w]).astype(BF16).astype(F32)
    d_up = (d_hidden * slope[w]).astype(BF16)
    sums[w, 0:1, :] = jnp.sum(d_up.astype(F32), axis=0, keepdims=True)
    grads[2, w] = dot_tn(hidden[w], g2[...]).astype(BF16)
    grads[1, w] = dot_tn(n2[...], d_up).astype(BF16)
    part = dot_nt(d_up, weights[1, w])
    total[...] = part if w == 0 else total[...] + part


def put_sums(geo, sums, column, row):
    at, lanes = 2 + column // 4, slice(column % 4 * LANES, (column % 4 + 1) * LANES)
    for w in range(geo.wt):
        sums[w, at : at + 1, lanes] = row[:, w * LANES : (w + 1) * LANES]


def project_back(geo, w, weights, n1, d_queries, d_table, near_back, far_back, sums, grads, total):
    kv = own_gradients(geo, w, d_table, near_back, far_back).astype(BF16)
    d_qkv = jnp.concatenate([d_queries[w], kv], axis=1)
    sums[w, 1:2, :LANES] = jnp.sum(d_qkv[:, :LANES].astype(F32), axis=0, keepdims=True)
    sums[w, 1:2, LANES : 2 * LANES] = jnp.sum(d_qkv[:, 2 * LANES :].astype(F32), axis=0, keepdims=True)
    grads[0, w, :, : 3 * LANES] = dot_tn(n1[...], d_qkv).astype(BF16)
    part = dot_nt(d_qkv, weights[0, w, :, : 3 * LANES])
    total[...] = part if w == 0 else total[...] + part


def remote(source, target, sent, landed, device):
    return pltpu.make_async_remote_copy(source, target, sent, landed, device_id=device, device_id_type=pl.DeviceIdType.MESH)


class Plane:
    def __init__(self, ctx, c, rows):
        self.ctx, self.c = ctx, c
        self.bits = ctx.bit_length() - 1
        self.each = rows // ctx
        plane_bits = self.bits - 1
        half = plane_bits // 2
        plane, core = c // 2, c % 2
        turned = plane // 2**half + plane % 2**half * 2 ** (plane_bits - half)
        self.places = (plane + core * 2**plane_bits, turned + core * 2**plane_bits)
        self.masks = (
            [2 << s for s in range(plane_bits)] + [1],
            [2 << (s + half) % plane_bits for s in range(plane_bits)] + [1],
        )

    def place(self, order):
        if isinstance(order, int):
            return self.places[order]
        return jnp.where(order == 0, self.places[0], self.places[1])

    def partner(self, order, stage):
        if isinstance(order, int):
            return self.flip(self.masks[order][stage])
        return jnp.where(order == 0, self.flip(self.masks[0][stage]), self.flip(self.masks[1][stage]))

    def flip(self, mask):
        return self.c + mask * (1 - 2 * (self.c // mask % 2))

    def block(self, order, stage, other=False):
        index = self.place(order) // 2**stage
        if other:
            index = index + 1 - 2 * (index % 2)
        size = self.each * 2**stage
        return pl.ds(pl.multiple_of(index * size, size), size)


def fused(geo, *refs):
    (
        x_hbm, g_hbm, segs, n1g, n1b, q_hbm, q_bias, k_hbm, v_hbm, v_bias, o_hbm, out_bias, n2g, n2b,
        up_hbm, up_bias, down_hbm, down_bias,
        out_result, out_source, out_grads, out_sums,
        weights, extra, x, g2, o_own, n1, q, own, cells, near_send, far_send, near_in, far_in,
        table, bias, probs, mixed, middle, n2, hidden, slope, result, total, g1, d_mixed, d_queries, d_table,
        near_give, far_give, near_back, far_back, grads, sums, gathered, source_all,
        from_left, from_right, reduced, sums_in, sums_all, sums_got,
        load_sem, store_sem, zw_send, zw_recv, pw_send, pw_recv, ex_send, ex_recv, halo_send, halo_recv,
        far_s, far_r, back_send, back_recv, farb_s, farb_r, rs_send, rs_recv, zl_send, zl_recv, zr_send, zr_recv,
        ag_send, ag_recv, out_send, out_recv, sm_send, sm_recv, sc_send, sc_recv,
        *landings,
    ) = refs
    C, W = geo.ctx, geo.wt
    c, z = lax.axis_index("ctx"), lax.axis_index("wt")
    plane = Plane(C, c, 512)
    B = plane.bits

    loads = [
        pltpu.make_async_copy(q_hbm, weights.at[0, z, :, pl.ds(0, LANES)], load_sem.at[0]),
        pltpu.make_async_copy(k_hbm, weights.at[0, z, :, pl.ds(LANES, LANES)], load_sem.at[1]),
        pltpu.make_async_copy(v_hbm, weights.at[0, z, :, pl.ds(2 * LANES, LANES)], load_sem.at[2]),
        pltpu.make_async_copy(o_hbm, o_own, load_sem.at[3]),
        pltpu.make_async_copy(up_hbm, weights.at[1, z], load_sem.at[4]),
        pltpu.make_async_copy(down_hbm, weights.at[2, z], load_sem.at[5]),
        pltpu.make_async_copy(x_hbm.at[z], x, load_sem.at[6]),
        pltpu.make_async_copy(g_hbm.at[z], g2, load_sem.at[7]),
    ]
    for copy in loads:
        copy.start()
    near_in[...] = jnp.zeros_like(near_in)
    far_in[...] = jnp.zeros_like(far_in)
    near_back[...] = jnp.zeros_like(near_back)
    far_back[...] = jnp.zeros_like(far_back)
    sums[...] = jnp.zeros_like(sums)
    extra[z] = jnp.zeros_like(extra[z])
    extra[z, 0:1, :] = up_bias[...]
    extra[z, 1:2, :LANES] = q_bias[...]
    extra[z, 1:2, LANES : 2 * LANES] = v_bias[...]

    barrier = pltpu.get_barrier_semaphore()
    for step in range(1, C):
        pl.semaphore_signal(barrier, inc=1, device_id=(lax.rem(c + step, C), z), device_id_type=pl.DeviceIdType.MESH)
    for step in range(1, W):
        pl.semaphore_signal(barrier, inc=1, device_id=(c, lax.rem(z + step, W)), device_id_type=pl.DeviceIdType.MESH)
    for copy in loads[:4]:
        copy.wait()
    weights[0, z, :, 3 * LANES :] = o_own[...].T
    pl.semaphore_wait(barrier, C + W - 2)

    def order_of(k, w):
        return (k + w) % 2

    def arrival(i):
        table_of = []
        for at in range(W):
            seen = []
            for step in range(1, W):
                seen += [w for w in (at - step, at + step) if 0 <= w < W]
            table_of.append(seen[i])
        w = jnp.int32(table_of[0])
        for at in range(1, W):
            w = jnp.where(z == at, table_of[at], w)
        return w

    arrivals = [arrival(i) for i in range(W - 1)]

    def weight_hop(k, w, to, side):
        rows = plane.block(order_of(k, w), 0)
        return remote(weights.at[k, w, rows], weights.at[k, w, rows], zw_send.at[k, w, side], zw_recv.at[k, w], (c, to))

    def weight_first(k):
        @pl.when(z > 0)
        def _():
            weight_hop(k, z, z - 1, 0).start()

        @pl.when(z < W - 1)
        def _():
            weight_hop(k, z, z + 1, 1).start()

    def weight_forward(k, w):
        to = jnp.where(w < z, z + 1, z - 1)
        return (to >= 0) & (to < W), weight_hop(k, w, to, 0)

    def weight_stage(k, w, s):
        order = order_of(k, w)
        rows = plane.block(order, s)
        return remote(
            weights.at[k, w, rows], weights.at[k, w, rows], pw_send.at[k, w, s], pw_recv.at[k, w, s],
            (plane.partner(order, s), z),
        )

    def weight_arrive(k):
        for w in arrivals:
            weight_hop(k, w, lax.rem(z + 1, W), 0).wait_recv()
            onward, copy = weight_forward(k, w)

            @pl.when(onward)
            def _():
                copy.start()

            weight_stage(k, w, 0).start()

    def weight_next(k, s):
        for w in arrivals:
            weight_stage(k, w, s).wait_recv()
            if s + 1 < B:
                weight_stage(k, w, s + 1).start()

    def weight_drain(k):
        @pl.when(z > 0)
        def _():
            weight_hop(k, z, z - 1, 0).wait_send()

        @pl.when(z < W - 1)
        def _():
            weight_hop(k, z, z + 1, 1).wait_send()

        for w in arrivals:
            onward, copy = weight_forward(k, w)

            @pl.when(onward)
            def _():
                copy.wait_send()

            for s in range(B):
                weight_stage(k, w, s).wait_send()

    def extra_copy(step):
        to = lax.rem(z + step, W)
        return remote(extra.at[z], extra.at[z], ex_send.at[step], ex_recv.at[step], (c, to))

    def extra_from(step):
        source = lax.rem(z + W - step, W)
        return remote(extra.at[source], extra.at[source], ex_send.at[step], ex_recv.at[step], (c, source))

    weight_first(0)
    for step in range(1, W):
        extra_copy(step).start()
    loads[4].wait()
    weight_first(1)
    loads[5].wait()
    weight_first(2)
    loads[6].wait()
    normed, _ = norm_parts(x[...].astype(F32))
    n1[...] = (normed * n1g[...] + n1b[...]).astype(BF16)
    bias[0] = mask_bias(geo, c, segs[pl.ds(z, 1), :], 0)
    bias[1] = mask_bias(geo, c, segs[pl.ds(z, 1), :], 1)
    pick = far_matrix(geo, c)
    weight_arrive(0)
    for s in range(B):
        weight_next(0, s)
        if s == 0:
            weight_arrive(1)
    for step in range(1, W):
        extra_from(step).wait_recv()

    for w in range(W):
        project(w, n1, weights, extra, q, own, cells, near_send, far_send)

    def halo(back):
        if back:
            return remote(near_give, near_back, back_send, back_recv, (c - 1, z))
        return remote(near_send, near_in, halo_send, halo_recv, (c + 1, z))

    def needs(source, target):
        need = jnp.bool_(False)
        for step in range(geo.far):
            size = 2 ** (step + 1)
            need = need | (target // size == source // size + 1)
        return need

    def far_copy(device):
        return remote(far_send, far_in.at[c], far_s.at[device], far_r.at[c], (device, z))

    def far_wait(device):
        return remote(far_send, far_in.at[device], far_s.at[device], far_r.at[device], (device, z))

    def give_copy(device):
        return remote(far_give.at[device], far_back.at[c], farb_s.at[device], farb_r.at[c], (device, z))

    def give_wait(device):
        return remote(far_give.at[device], far_back.at[device], farb_s.at[device], farb_r.at[device], (device, z))

    def each_after(action):
        for step in range(1, C):
            device = jnp.minimum(c + step, C - 1)

            @pl.when((c + step < C) & needs(c, device))
            def _():
                action(device)

    def each_before(action):
        for step in range(1, C):
            device = jnp.maximum(c - step, 0)

            @pl.when((c - step >= 0) & needs(device, c))
            def _():
                action(device)

    @pl.when(c < C - 1)
    def _():
        halo(False).start()

    each_after(lambda device: far_copy(device).start())
    weight_next(1, 0)
    weight_arrive(2)
    weight_next(1, 1)

    @pl.when(c > 0)
    def _():
        halo(False).wait_recv()

    each_before(lambda device: far_wait(device).wait_recv())

    for w in range(W):
        tables(geo, w, pick, own, cells, near_in, far_in, table)
        for tile in (0, 1):
            attend(geo, w, tile, q, table, bias, probs, mixed)
        if w == 0:
            weight_next(2, 0)
        if w == 1:
            for s in range(2, B):
                weight_next(1, s)
        if w == 2:
            for s in range(1, B - 1):
                weight_next(2, s)

    acc = x[...].astype(F32) + out_bias[...]
    for w in range(W):
        acc = acc + dot_nt(mixed[w], weights[0, w, :, 3 * LANES :])
    middle[...] = acc
    normed, _ = norm_parts(acc)
    n2[...] = (normed * n2g[...] + n2b[...]).astype(BF16)
    result[...] = acc + down_bias[...]
    weight_next(2, B - 1)
    for w in range(W):
        feed(w, n2, weights, extra, hidden, slope, result)
    gathered[z] = result[...].astype(BF16)

    def row_hop(at, w, to, side):
        rows = (gathered, source_all)[at]
        return remote(rows.at[w], rows.at[w], out_send.at[at, w, side], out_recv.at[at, w], (c, to))

    def rows_first(at):
        @pl.when(z > 0)
        def _():
            row_hop(at, z, z - 1, 0).start()

        @pl.when(z < W - 1)
        def _():
            row_hop(at, z, z + 1, 1).start()

    def row_forward(at, w):
        to = jnp.where(w < z, z + 1, z - 1)
        return (to >= 0) & (to < W), row_hop(at, w, to, 0)

    def rows_arrive(at, i):
        w = arrivals[i]
        row_hop(at, w, lax.rem(z + 1, W), 0).wait_recv()
        onward, copy = row_forward(at, w)

        @pl.when(onward)
        def _():
            copy.start()

    def rows_drain(at):
        @pl.when(z > 0)
        def _():
            row_hop(at, z, z - 1, 0).wait_send()

        @pl.when(z < W - 1)
        def _():
            row_hop(at, z, z + 1, 1).wait_send()

        for w in arrivals:
            onward, copy = row_forward(at, w)

            @pl.when(onward)
            def _():
                copy.wait_send()

    def reduce_copy(k, w, s):
        order = order_of(k, w)
        return remote(
            grads.at[k, w, plane.block(order, s, other=True)],
            landings[s].at[k, w],
            rs_send.at[k, w, s],
            rs_recv.at[k, w, s],
            (plane.partner(order, s), z),
        )

    def reduce_add(k, w, s):
        reduce_copy(k, w, s).wait_recv()
        rows = plane.block(order_of(k, w), s)
        grads[k, w, rows] = (grads[k, w, rows].astype(F32) + landings[s][k, w].astype(F32)).astype(BF16)
        if s > 0:
            reduce_copy(k, w, s - 1).start()

    def line_copy(k, w, right):
        rows = plane.block(order_of(k, w), 0)
        if right:
            return remote(grads.at[k, w, rows], from_left.at[k, w], zr_send.at[k, w], zr_recv.at[k, w], (c, z + 1))
        return remote(grads.at[k, w, rows], from_right.at[k, w], zl_send.at[k, w], zl_recv.at[k, w], (c, z - 1))

    def line_send(k, w):
        rows = plane.block(order_of(k, w), 0)

        @pl.when(w > z)
        def _():
            @pl.when(z > 0)
            def _():
                line_copy(k, w, True).wait_recv()
                grads[k, w, rows] = (grads[k, w, rows].astype(F32) + from_left[k, w].astype(F32)).astype(BF16)

            line_copy(k, w, True).start()

        @pl.when(w < z)
        def _():
            @pl.when(z < W - 1)
            def _():
                line_copy(k, w, False).wait_recv()
                grads[k, w, rows] = (grads[k, w, rows].astype(F32) + from_right[k, w].astype(F32)).astype(BF16)

            line_copy(k, w, False).start()

    def line_drain(k, w):
        @pl.when(w > z)
        def _():
            line_copy(k, w, True).wait_send()

        @pl.when(w < z)
        def _():
            line_copy(k, w, False).wait_send()

    def own_rows(k):
        return plane.block(order_of(k, z), 0)

    def line_end(k):
        rows = own_rows(k)
        total_now = grads[k, z, rows].astype(F32)

        @pl.when(z > 0)
        def _():
            line_copy(k, z, True).wait_recv()

        @pl.when(z < W - 1)
        def _():
            line_copy(k, z, False).wait_recv()

        left = jnp.where(z > 0, from_left[k, z].astype(F32), 0.0)
        right = jnp.where(z < W - 1, from_right[k, z].astype(F32), 0.0)
        reduced[k, rows] = (total_now + left + right).astype(BF16)
        gather_copy(k, 0).start()

    def gather_copy(k, s):
        order = order_of(k, z)
        rows = plane.block(order, s)
        return remote(reduced.at[k, rows], reduced.at[k, rows], ag_send.at[k, s], ag_recv.at[k, s], (plane.partner(order, s), z))

    def gather_next(k, s):
        gather_copy(k, s).wait_recv()
        if s + 1 < B:
            gather_copy(k, s + 1).start()

    line_order = []
    for step in range((W + 1) // 2):
        line_order += [W - 1 - step] + ([step] if step != W - 1 - step else [])

    rows_first(0)
    loads[7].wait()
    for w in range(W):
        feed_back(w, g2, weights, n2, hidden, slope, sums, grads, total)
        reduce_copy(2, w, B - 1).start()
        reduce_copy(1, w, B - 1).start()
        if w > 0:
            reduce_add(2, w - 1, B - 1)
            reduce_add(1, w - 1, B - 1)
    rows_arrive(0, 0)
    normed, inverse = norm_parts(middle[...])
    d_normed = total[...]
    wide = g2[...].astype(F32)
    first = wide + norm_backward(d_normed, normed, inverse, n2g[...])
    g1[...] = first
    low = first.astype(BF16)
    put_sums(geo, sums, 2, jnp.sum(first, axis=0, keepdims=True))
    put_sums(geo, sums, 3, jnp.sum(d_normed * normed, axis=0, keepdims=True))
    put_sums(geo, sums, 4, jnp.sum(d_normed, axis=0, keepdims=True))
    put_sums(geo, sums, 5, jnp.sum(wide, axis=0, keepdims=True))
    reduce_add(2, W - 1, B - 1)
    reduce_add(1, W - 1, B - 1)
    for w in range(W):
        d_mixed[w] = dot_nn(low, weights[0, w, :, 3 * LANES :]).astype(BF16)
        grads[0, w, :, 3 * LANES :] = dot_tn(low, mixed[w]).astype(BF16)
    for w in range(W):
        for tile in (0, 1):
            attend_back(geo, w, tile, q, table, probs, d_mixed, d_queries, d_table)
        return_cells(geo, w, pick, d_table, near_give, far_give)
        if w == 1:
            rows_arrive(0, 1)
        for s in range(B - 2, 0, -1):
            reduce_add(2, w, s)

    @pl.when(c > 0)
    def _():
        halo(True).start()

    each_before(lambda device: give_copy(device).start())
    for w in range(W):
        for s in range(B - 2, 0, -1):
            reduce_add(1, w, s)
    rows_arrive(0, 2)

    @pl.when(c < C - 1)
    def _():
        halo(True).wait_recv()

    each_after(lambda device: give_wait(device).wait_recv())
    for w in range(W):
        project_back(geo, w, weights, n1, d_queries, d_table, near_back, far_back, sums, grads, total)
        reduce_copy(0, w, B - 1).start()
        reduce_add(2, w, 0)
    normed, inverse = norm_parts(x[...].astype(F32))
    d_normed = total[...]
    source_all[z] = (g1[...] + norm_backward(d_normed, normed, inverse, n1g[...])).astype(BF16)
    rows_first(1)
    put_sums(geo, sums, 0, jnp.sum(d_normed * normed, axis=0, keepdims=True))
    put_sums(geo, sums, 1, jnp.sum(d_normed, axis=0, keepdims=True))

    def sums_copy(step):
        to = lax.rem(z + step, W)
        return remote(sums.at[to], sums_in.at[step], sm_send.at[step], sm_recv.at[step], (c, to))

    def sums_stage(s):
        return remote(sums_all.at[s], sums_got.at[s], sc_send.at[s], sc_recv.at[s], (plane.flip(1 << s), z))

    for step in range(1, W):
        sums_copy(step).start()
    for w in range(W):
        reduce_add(0, w, B - 1)
    for w in line_order:
        line_send(2, w)
    for w in range(W):
        reduce_add(1, w, 0)
    rows_arrive(1, 0)
    line_end(2)
    for w in line_order:
        line_send(1, w)
    total_sums = sums[z]
    for step in range(1, W):
        sums_copy(step).wait_recv()
        total_sums = total_sums + sums_in[step]
    sums_all[0] = total_sums
    for s in range(B):
        sums_stage(s).start()
        sums_stage(s).wait_recv()
        sums_all[s + 1] = sums_all[s] + sums_got[s]
    gather_next(2, 0)
    rows_arrive(1, 1)
    line_end(1)
    for w in range(W):
        for s in range(B - 2, 0, -1):
            reduce_add(0, w, s)
    for s in range(1, B):
        gather_next(2, s)
    gather_next(1, 0)
    for w in range(W):
        reduce_add(0, w, 0)
    for s in range(1, B):
        gather_next(1, s)
    for w in line_order:
        line_send(0, w)
    rows_arrive(1, 2)
    line_end(0)
    stores = [
        pltpu.make_async_copy(gathered, out_result, store_sem.at[0]),
        pltpu.make_async_copy(source_all, out_source, store_sem.at[1]),
        pltpu.make_async_copy(sums_all.at[B], out_sums, store_sem.at[2]),
        pltpu.make_async_copy(reduced.at[1], out_grads.at[1], store_sem.at[3]),
        pltpu.make_async_copy(reduced.at[2], out_grads.at[2], store_sem.at[4]),
        pltpu.make_async_copy(reduced.at[0], out_grads.at[0], store_sem.at[5]),
    ]
    for copy in stores[:5]:
        copy.start()
    for s in range(B):
        gather_next(0, s)
    stores[5].start()

    for k in range(3):
        weight_drain(k)
        for w in range(W):
            for s in range(B):
                reduce_copy(k, w, s).wait_send()
            line_drain(k, w)
        for s in range(B):
            gather_copy(k, s).wait_send()
    for at in (0, 1):
        rows_drain(at)
    for step in range(1, W):
        extra_copy(step).wait_send()
        sums_copy(step).wait_send()
    for s in range(B):
        sums_stage(s).wait_send()

    @pl.when(c < C - 1)
    def _():
        halo(False).wait_send()

    @pl.when(c > 0)
    def _():
        halo(True).wait_send()

    each_after(lambda device: far_copy(device).wait_send())
    each_before(lambda device: give_copy(device).wait_send())
    for copy in stores:
        copy.wait()


def unpack(result, source, grads, sums, *outs):
    (
        layer_out, input_grad, d_n1g, d_n1b, d_q, d_qb, d_k, d_v, d_vb, d_o, d_ob, d_n2g, d_n2b, d_up, d_upb, d_down, d_db,
    ) = outs
    layer_out[...] = result[...].astype(F32)
    input_grad[...] = source[...].astype(F32)
    wide = grads[0].astype(F32)
    d_q[...] = wide[:, :LANES]
    d_k[...] = wide[:, LANES : 2 * LANES]
    d_v[...] = wide[:, 2 * LANES : 3 * LANES]
    d_o[...] = wide[:, 3 * LANES :].T
    d_up[...] = grads[1].astype(F32)
    d_down[...] = grads[2].astype(F32)
    for at, out in enumerate((d_n1g, d_n1b, d_ob, d_n2g, d_n2b, d_db)):
        row, lane = 2 + at // 4, at % 4 * LANES
        out[...] = sums[row : row + 1, lane : lane + LANES]
    d_qb[...] = sums[1:2, :LANES]
    d_vb[...] = sums[1:2, LANES : 2 * LANES]
    d_upb[...] = sums[0:1, :]


def shards(
    x_in,
    grad_out,
    seg_ids,
    norm1_gain,
    norm1_bias,
    q_weight,
    q_bias,
    k_weight,
    v_weight,
    v_bias,
    out_weight,
    out_bias,
    norm2_gain,
    norm2_bias,
    up_weight,
    up_bias,
    down_weight,
    down_bias,
):
    C, W = lax.axis_size("ctx"), lax.axis_size("wt")
    runs, T, width = x_in.shape
    hidden = up_weight.shape[1]
    geo = Geometry(C, W, T)
    S, B = geo.slots, C.bit_length() - 1
    each = width // C
    assert runs == W and hidden == width and q_weight.shape[1] == LANES and T == 256
    sds = jax.ShapeDtypeStruct
    vmem, dma = pltpu.VMEM, pltpu.SemaphoreType.DMA
    row = lambda v: v.reshape(1, -1)
    pair = 2 * LANES
    scratch = [
        vmem((3, W, width, width), BF16),
        vmem((W, 8, width), F32),
        vmem((T, width), BF16),
        vmem((T, width), BF16),
        vmem((LANES, width), BF16),
        vmem((T, width), BF16),
        vmem((W, T, LANES), BF16),
        vmem((W, T, pair), BF16),
        vmem((W, 224, pair), BF16),
        vmem((W, 80, pair), BF16),
        vmem((W, 16, pair), BF16),
        vmem((W, 80, pair), BF16),
        vmem((C, W, 16, pair), BF16),
        vmem((W, 2, S, pair), BF16),
        vmem((2, S, geo.tile), F32),
        vmem((W, 2, S, pair), BF16),
        vmem((W, T, LANES), BF16),
        vmem((T, width), F32),
        vmem((T, width), BF16),
        vmem((W, T, hidden), BF16),
        vmem((W, T, hidden), F32),
        vmem((T, width), F32),
        vmem((T, width), F32),
        vmem((T, width), F32),
        vmem((W, T, LANES), BF16),
        vmem((W, T, LANES), BF16),
        vmem((W, 2, S, pair), F32),
        vmem((W, 80, pair), BF16),
        vmem((C, W, 16, pair), BF16),
        vmem((W, 80, pair), BF16),
        vmem((C, W, 16, pair), BF16),
        vmem((3, W, width, width), BF16),
        vmem((W, 8, width), F32),
        vmem((W, T, width), BF16),
        vmem((W, T, width), BF16),
        vmem((3, W, each, width), BF16),
        vmem((3, W, each, width), BF16),
        vmem((3, width, width), BF16),
        vmem((W, 8, width), F32),
        vmem((B + 1, 8, width), F32),
        vmem((B, 8, width), F32),
        dma((8,)),
        dma((6,)),
        dma((3, W, 2)),
        dma((3, W)),
        dma((3, W, B)),
        dma((3, W, B)),
        dma((W,)),
        dma((W,)),
        dma(()),
        dma(()),
        dma((C,)),
        dma((C,)),
        dma(()),
        dma(()),
        dma((C,)),
        dma((C,)),
        dma((3, W, B)),
        dma((3, W, B)),
        dma((3, W)),
        dma((3, W)),
        dma((3, W)),
        dma((3, W)),
        dma((3, B)),
        dma((3, B)),
        dma((2, W, 2)),
        dma((2, W)),
        dma((W,)),
        dma((W,)),
        dma((B,)),
        dma((B,)),
    ] + [vmem((3, W, each * 2**s, width), BF16) for s in range(B)]
    far, near = pl.BlockSpec(memory_space=pl.ANY), pl.BlockSpec(memory_space=pltpu.VMEM)
    result, source, grads, sums = pl.pallas_call(
        functools.partial(fused, geo),
        name="fused",
        out_shape=[sds((W, T, width), BF16), sds((W, T, width), BF16), sds((3, width, width), BF16), sds((8, width), F32)],
        in_specs=[far, far, near, near, near, far, near, far, far, near, far, near, near, near, far, near, far, near],
        out_specs=[far] * 4,
        scratch_shapes=scratch,
        compiler_params=pltpu.CompilerParams(collective_id=0, has_side_effects=True, vmem_limit_bytes=58 * 2**20),
    )(
        x_in, grad_out, seg_ids, row(norm1_gain), row(norm1_bias), q_weight, row(q_bias), k_weight, v_weight, row(v_bias),
        out_weight, row(out_bias), row(norm2_gain), row(norm2_bias), up_weight, row(up_bias), down_weight, row(down_bias),
    )
    part = width // W
    rows = lambda shape: pl.BlockSpec(shape, lambda i: (i, 0))
    still = lambda shape: pl.BlockSpec(shape, lambda i: (0, 0))
    one, wide = (sds((1, LANES), F32), still((1, LANES))), (sds((1, hidden), F32), still((1, hidden)))
    blocks = (sds((W, T, width), F32), pl.BlockSpec((1, T, width), lambda i: (i, 0, 0)))
    thin = (sds((width, LANES), F32), rows((part, LANES)))
    full = (sds((width, width), F32), rows((part, width)))
    turned = (sds((LANES, width), F32), pl.BlockSpec((LANES, part), lambda i: (0, i)))
    outs = [blocks, blocks, one, one, thin, one, thin, thin, one, turned, one, one, one, full, wide, full, one]
    values = pl.pallas_call(
        unpack,
        name="unpack",
        grid=(W,),
        out_shape=[o[0] for o in outs],
        in_specs=[blocks[1], blocks[1], pl.BlockSpec((3, part, width), lambda i: (0, i, 0)), still((8, width))],
        out_specs=[o[1] for o in outs],
    )(result, source, grads, sums)
    return tuple(v.reshape(-1) if v.shape[0] == 1 else v for v in values)


def solution(mesh):
    in_specs = (
        P(None, "ctx", None),
        P(None, "ctx", None),
        P(),
        P(),
        P(),
        P(None, "wt"),
        P("wt"),
        P(None, "wt"),
        P(None, "wt"),
        P("wt"),
        P("wt", None),
        P(),
        P(),
        P(),
        P(None, "wt"),
        P("wt"),
        P("wt", None),
        P(),
    )
    out_specs = (
        P(None, "ctx", None),
        P(None, "ctx", None),
        P("wt"),
        P("wt"),
        P(None, "wt"),
        P("wt"),
        P(None, "wt"),
        P(None, "wt"),
        P("wt"),
        P("wt", None),
        P("wt"),
        P("wt"),
        P("wt"),
        P(None, "wt"),
        P("wt"),
        P("wt", None),
        P("wt"),
    )
    return jax.shard_map(shards, mesh=mesh, in_specs=in_specs, out_specs=out_specs, check_vma=False)
```

```python
import functools

import jax
import jax.numpy as jnp
from jax import lax
from jax.experimental import pallas as pl
from jax.experimental.pallas import tpu as pltpu
from jax.sharding import PartitionSpec as P

HEAD_DIM = 64
BLOCK = 16
LEVELS = 10
FINE = 3
EPSILON = 1e-05
NEGATIVE = -1e30
LOG_TWO = 0.6931471805599453
LANES = 128
BF16 = jnp.bfloat16
F32 = jnp.float32


def dot(left, right, dims):
    return lax.dot_general(left, right, (dims, ((), ())), preferred_element_type=F32)


def dot_nn(left, right):
    return dot(left, right, ((1,), (0,)))


def dot_nt(left, right):
    return dot(left, right, ((1,), (1,)))


def dot_tn(left, right):
    return dot(left, right, ((0,), (0,)))


def norm_parts(source):
    centre = jnp.mean(source, axis=-1, keepdims=True)
    centred = source - centre
    variance = jnp.mean(centred * centred, axis=-1, keepdims=True)
    inverse = lax.rsqrt(variance + EPSILON)
    return centred * inverse, inverse


def norm_backward(upstream, normed, inverse, gain):
    scaled = upstream * gain
    first_mean = jnp.mean(scaled, axis=-1, keepdims=True)
    second_mean = jnp.mean(scaled * normed, axis=-1, keepdims=True)
    return inverse * (scaled - first_mean - normed * second_mean)


def iota(shape, axis):
    return lax.broadcasted_iota(jnp.int32, shape, axis)


class Geometry:
    def __init__(self, ctx, wt, tok_dev):
        self.ctx, self.wt, self.tok_dev = ctx, wt, tok_dev
        tokens = ctx * tok_dev
        self.levels = len([l for l in range(LEVELS) if BLOCK * 2**l < tokens])
        self.own_cells = [tok_dev // 2**l if l <= FINE else 0 for l in range(self.levels)]
        self.tile = tok_dev // 2
        self.tile_slots = [BLOCK + self.tile] + [BLOCK * 4 >> (l - 1) if l < FINE else BLOCK for l in range(1, self.levels)]
        self.slots = sum(self.tile_slots)
        self.slot_at = [sum(self.tile_slots[:l]) for l in range(self.levels + 1)]
        self.far = self.levels - (FINE + 2)
        self.near = FINE + 2


def pool_matrix():
    parts = []
    for level, count in ((1, 128), (2, 64), (3, 32)):
        hit = (iota((count, 256), 1) >> level) == iota((count, 256), 0)
        parts.append(jnp.where(hit, 1.0 / 2**level, 0.0))
    return jnp.concatenate(parts, axis=0).astype(BF16)


def coarse_matrix():
    row, column = iota((32, 32), 0), iota((32, 32), 1)
    out = jnp.zeros((32, 32), F32)
    first = 0
    for level, count in ((4, 16), (5, 8), (6, 4), (7, 2), (8, 1)):
        up = level - FINE
        hit = (row >= first) & (row < first + count) & ((column >> up) == row - first)
        out = jnp.where(hit, 1.0 / 2**up, out)
        first += count
    return out.astype(BF16)


def far_matrix(geo, me):
    parts = []
    first = 0
    for step in range(geo.far):
        up = step + 1
        each = BLOCK >> up
        row, column = iota((BLOCK, geo.ctx * BLOCK), 0), iota((BLOCK, geo.ctx * BLOCK), 1)
        group = (me >> up) - 1
        device = (group << up) + (row >> (4 - up))
        wanted = device * BLOCK + first + (row & (each - 1))
        parts.append(jnp.where((column == wanted) & (group >= 0), 1.0, 0.0))
        first += each
    return jnp.concatenate(parts, axis=0).astype(BF16)


def mask_bias(geo, me, segs, tile):
    first_pos = me * geo.tok_dev + tile * geo.tile
    seg_one = jnp.sum((segs < 1).astype(jnp.int32), axis=1, keepdims=True)
    seg_two = jnp.sum((segs < 2).astype(jnp.int32), axis=1, keepdims=True)
    position = first_pos + iota((1, geo.tile), 1)
    begins = jnp.where(position >= seg_two, seg_two, jnp.where(position >= seg_one, seg_one, 0))
    parts = []
    for level in range(geo.levels):
        size, shift = 2**level, level + 4
        count = geo.tile_slots[level]
        span = BLOCK * size
        if level <= FINE:
            base = first_pos - span
        else:
            base = (((me * geo.tok_dev) >> shift) - 1) << shift
        begin = base + size * iota((count, geo.tile), 0)
        lower = jnp.maximum(((position >> shift) - 1) << shift, begins)
        if level == 0:
            upper = position + 1
        else:
            upper = ((position >> (shift - 1)) - 1) << (shift - 1)
        valid = (begin >= lower) & (begin + size <= upper)
        parts.append(jnp.where(valid, level * LOG_TWO, NEGATIVE))
    return jnp.concatenate(parts, axis=0)


def both_heads(pair):
    lane = iota(pair.shape, 1)
    zero = jnp.zeros_like(pair)
    return jnp.concatenate([jnp.where(lane < HEAD_DIM, pair, zero), jnp.where(lane >= HEAD_DIM, pair, zero)], axis=0)


def own_lanes(stacked):
    rows = stacked.shape[0] // 2
    lane = iota((rows, stacked.shape[1]), 1)
    return jnp.where(lane < HEAD_DIM, stacked[:rows], stacked[rows:])


def project(w, n1, weights, extra, q, own, cells, near, far):
    out = dot_nn(n1[...], weights[0, w, :, : 3 * LANES])
    bias = extra[w, 1:2, :]
    q[w] = ((out[:, :LANES] + bias[:, :LANES]).astype(BF16) * 0.125).astype(BF16)
    kv = jnp.concatenate(
        [out[:, LANES : 2 * LANES], out[:, 2 * LANES :] + bias[:, LANES : 2 * LANES]], axis=1
    ).astype(BF16)
    own[w] = kv
    fine = dot_nn(pool_matrix(), kv).astype(BF16)
    cells[w] = fine
    rough = dot_nn(coarse_matrix(), fine[192:224]).astype(BF16)
    near[w, 0:16] = kv[240:256]
    near[w, 16:32] = fine[112:128]
    near[w, 32:48] = fine[176:192]
    near[w, 48:64] = fine[208:224]
    near[w, 64:80] = rough[0:16]
    far[w] = rough[16:32]


def tables(geo, w, pick, own, cells, near_in, far_in, table):
    blocks = far_in[:, w].reshape(geo.ctx * BLOCK, 2 * LANES)
    rough = dot_nn(pick, blocks).astype(BF16)
    at = geo.slot_at
    table[w, 0, 0:16] = near_in[w, 0:16]
    table[w, 0, 16:144] = own[w, 0:128]
    table[w, 1, 0:144] = own[w, 112:256]
    table[w, 0, at[1] : at[1] + 16] = near_in[w, 16:32]
    table[w, 0, at[1] + 16 : at[2]] = cells[w, 0:48]
    table[w, 1, at[1] : at[2]] = cells[w, 48:112]
    table[w, 0, at[2] : at[2] + 16] = near_in[w, 32:48]
    table[w, 0, at[2] + 16 : at[3]] = cells[w, 128:144]
    table[w, 1, at[2] : at[3]] = cells[w, 144:176]
    table[w, 0, at[3] : at[4]] = near_in[w, 48:64]
    table[w, 1, at[3] : at[4]] = cells[w, 192:208]
    for tile in (0, 1):
        table[w, tile, at[4] : at[5]] = near_in[w, 64:80]
        table[w, tile, at[5] :] = rough


def attend(geo, w, tile, q, table, bias, probs, mixed):
    rows = slice(tile * geo.tile, (tile + 1) * geo.tile)
    both = both_heads(q[w, rows, :])
    level_bias = bias[tile]
    scores = dot_nt(table[w, tile, :, :LANES], both)
    scores = scores + jnp.concatenate([level_bias, level_bias], axis=1)
    top = jnp.max(scores, axis=0, keepdims=True)
    exponent = jnp.exp(scores - top)
    total = jnp.sum(exponent, axis=0, keepdims=True)
    low = (exponent * (1.0 / total)).astype(BF16)
    probs[w, tile] = low
    mixed[w, rows, :] = own_lanes(dot_tn(low, table[w, tile, :, LANES:])).astype(BF16)


def attend_back(geo, w, tile, q, table, probs, d_mixed, d_queries, d_table):
    rows = slice(tile * geo.tile, (tile + 1) * geo.tile)
    both = both_heads(q[w, rows, :])
    d_both = both_heads(d_mixed[w, rows, :])
    low = probs[w, tile]
    d_probs = dot_nt(table[w, tile, :, LANES:], d_both)
    wide = low.astype(F32)
    product = wide * d_probs
    centre = jnp.sum(product, axis=0, keepdims=True)
    d_scores = (product - wide * centre).astype(BF16)
    d_table[w, tile, :, :LANES] = dot_nn(d_scores, both)
    d_table[w, tile, :, LANES:] = dot_nn(low, d_both)
    back = own_lanes(dot_tn(d_scores, table[w, tile, :, :LANES]))
    d_queries[w, rows, :] = (back * 0.125).astype(BF16)


def return_cells(geo, w, pick, d_table, near, far):
    at = geo.slot_at
    near[w, 0:16] = d_table[w, 0, 0:16].astype(BF16)
    near[w, 16:32] = d_table[w, 0, at[1] : at[1] + 16].astype(BF16)
    near[w, 32:48] = d_table[w, 0, at[2] : at[2] + 16].astype(BF16)
    near[w, 48:64] = d_table[w, 0, at[3] : at[4]].astype(BF16)
    near[w, 64:80] = (d_table[w, 0, at[4] : at[5]] + d_table[w, 1, at[4] : at[5]]).astype(BF16)
    rough = (d_table[w, 0, at[5] :] + d_table[w, 1, at[5] :]).astype(BF16)
    far[:, w] = dot_tn(pick, rough).astype(BF16).reshape(geo.ctx, BLOCK, 2 * LANES)


def own_gradients(geo, w, d_table, near_back, far_back):
    at = geo.slot_at
    first, second = d_table.at[w, 0], d_table.at[w, 1]
    back = near_back[w].astype(F32)
    tokens = jnp.concatenate(
        [first[16:128], first[128:144] + second[0:16], second[16:128], second[128:144] + back[0:16]], axis=0
    )
    far = jnp.sum(far_back[:, w].astype(F32), axis=0)
    rough = jnp.concatenate([back[64:80], far], axis=0)
    fine = dot_tn(coarse_matrix(), rough.astype(BF16))
    level3 = jnp.concatenate([second[at[3] : at[4]], back[48:64]], axis=0) + fine
    cells = jnp.concatenate(
        [
            first[at[1] + 16 : at[2]],
            second[at[1] : at[2]],
            back[16:32],
            first[at[2] + 16 : at[3]],
            second[at[2] : at[3]],
            back[32:48],
            level3,
        ],
        axis=0,
    )
    return tokens + dot_tn(pool_matrix(), cells.astype(BF16))


def feed(w, n2, weights, extra, hidden, slope, result):
    pre = dot_nn(n2[...], weights[1, w]) + extra[w, 0:1, :]
    gate = jax.nn.sigmoid(pre)
    hidden[w] = (pre * gate).astype(BF16)
    slope[w] = gate * (1.0 + pre * (1.0 - gate))
    result[...] += dot_nn(hidden[w], weights[2, w])


def feed_back(first, w, g2, weights, n2, hidden, slope, sums, grads, total):
    d_hidden = dot_nt(g2[...], weights[2, w]).astype(BF16).astype(F32)
    d_up = (d_hidden * slope[w]).astype(BF16)
    sums[w, 0:1, :] = jnp.sum(d_up.astype(F32), axis=0, keepdims=True)
    grads[2, w] = dot_tn(hidden[w], g2[...]).astype(BF16)
    grads[1, w] = dot_tn(n2[...], d_up).astype(BF16)
    part = dot_nt(d_up, weights[1, w])
    total[...] = part if first else total[...] + part


def put_sums(geo, sums, column, row):
    at, lanes = 2 + column // 4, slice(column % 4 * LANES, (column % 4 + 1) * LANES)
    for w in range(geo.wt):
        sums[w, at : at + 1, lanes] = row[:, w * LANES : (w + 1) * LANES]


def project_back(geo, first, w, weights, n1, d_queries, d_table, near_back, far_back, sums, grads, total):
    kv = own_gradients(geo, w, d_table, near_back, far_back).astype(BF16)
    d_qkv = jnp.concatenate([d_queries[w], kv], axis=1)
    sums[w, 1:2, :LANES] = jnp.sum(d_qkv[:, :LANES].astype(F32), axis=0, keepdims=True)
    sums[w, 1:2, LANES : 2 * LANES] = jnp.sum(d_qkv[:, 2 * LANES :].astype(F32), axis=0, keepdims=True)
    grads[0, w, :, : 3 * LANES] = dot_tn(n1[...], d_qkv).astype(BF16)
    part = dot_nt(d_qkv, weights[0, w, :, : 3 * LANES])
    total[...] = part if first else total[...] + part


def remote(source, target, sent, landed, device):
    return pltpu.make_async_remote_copy(source, target, sent, landed, device_id=device, device_id_type=pl.DeviceIdType.MESH)


class Plane:
    def __init__(self, ctx, c, rows):
        self.ctx, self.c = ctx, c
        self.bits = ctx.bit_length() - 1
        self.each = rows // ctx
        plane_bits = self.bits - 1
        half = plane_bits // 2
        plane, core = c // 2, c % 2
        turned = plane // 2**half + plane % 2**half * 2 ** (plane_bits - half)
        self.places = (plane + core * 2**plane_bits, turned + core * 2**plane_bits)
        self.masks = (
            [2 << s for s in range(plane_bits)] + [1],
            [2 << (s + half) % plane_bits for s in range(plane_bits)] + [1],
        )

    def place(self, order):
        if isinstance(order, int):
            return self.places[order]
        return jnp.where(order == 0, self.places[0], self.places[1])

    def partner(self, order, stage):
        if isinstance(order, int):
            return self.flip(self.masks[order][stage])
        return jnp.where(order == 0, self.flip(self.masks[0][stage]), self.flip(self.masks[1][stage]))

    def flip(self, mask):
        return self.c + mask * (1 - 2 * (self.c // mask % 2))

    def block(self, order, stage, other=False):
        index = self.place(order) // 2**stage
        if other:
            index = index + 1 - 2 * (index % 2)
        size = self.each * 2**stage
        return pl.ds(pl.multiple_of(index * size, size), size)


def fused(geo, *refs):
    (
        x_hbm, g_hbm, segs, n1g, n1b, q_hbm, q_bias, k_hbm, v_hbm, v_bias, o_hbm, out_bias, n2g, n2b,
        up_hbm, up_bias, down_hbm, down_bias,
        out_result, out_source, out_grads, out_sums,
        weights, extra, x, g2, o_own, n1, q, own, cells, near_send, far_send, near_in, far_in,
        table, bias, probs, mixed, middle, n2, hidden, slope, result, total, g1, d_mixed, d_queries, d_table,
        near_give, far_give, near_back, far_back, grads, sums, gathered, source_all,
        from_line, reduced, sums_in, sums_all, sums_got,
        load_sem, store_sem, zw_send, zw_recv, pw_send, pw_recv, ex_send, ex_recv, halo_send, halo_recv,
        far_s, far_r, back_send, back_recv, farb_s, farb_r, rs_send, rs_recv, zl_send, zl_recv,
        ag_send, ag_recv, out_send, out_recv, sm_send, sm_recv, sc_send, sc_recv,
        *landings,
    ) = refs
    C, W = geo.ctx, geo.wt
    c, z = lax.axis_index("ctx"), lax.axis_index("wt")
    plane = Plane(C, c, 512)
    B = plane.bits

    loads = [
        pltpu.make_async_copy(q_hbm, weights.at[0, z, :, pl.ds(0, LANES)], load_sem.at[0]),
        pltpu.make_async_copy(k_hbm, weights.at[0, z, :, pl.ds(LANES, LANES)], load_sem.at[1]),
        pltpu.make_async_copy(v_hbm, weights.at[0, z, :, pl.ds(2 * LANES, LANES)], load_sem.at[2]),
        pltpu.make_async_copy(o_hbm, o_own, load_sem.at[3]),
        pltpu.make_async_copy(up_hbm, weights.at[1, z], load_sem.at[4]),
        pltpu.make_async_copy(down_hbm, weights.at[2, z], load_sem.at[5]),
        pltpu.make_async_copy(x_hbm.at[z], x, load_sem.at[6]),
        pltpu.make_async_copy(g_hbm.at[z], g2, load_sem.at[7]),
    ]
    for copy in loads:
        copy.start()
    near_in[...] = jnp.zeros_like(near_in)
    far_in[...] = jnp.zeros_like(far_in)
    near_back[...] = jnp.zeros_like(near_back)
    far_back[...] = jnp.zeros_like(far_back)
    sums[...] = jnp.zeros_like(sums)
    extra[z] = jnp.zeros_like(extra[z])
    extra[z, 0:1, :] = up_bias[...]
    extra[z, 1:2, :LANES] = q_bias[...]
    extra[z, 1:2, LANES : 2 * LANES] = v_bias[...]

    barrier = pltpu.get_barrier_semaphore()
    for step in range(1, C):
        pl.semaphore_signal(barrier, inc=1, device_id=(lax.rem(c + step, C), z), device_id_type=pl.DeviceIdType.MESH)
    for step in range(1, W):
        pl.semaphore_signal(barrier, inc=1, device_id=(c, lax.rem(z + step, W)), device_id_type=pl.DeviceIdType.MESH)
    for copy in loads[:4]:
        copy.wait()
    weights[0, z, :, 3 * LANES :] = o_own[...].T
    pl.semaphore_wait(barrier, C + W - 2)

    def order_of(k, w):
        return (k + w) % 2

    def arrival(i):
        table_of = []
        for at in range(W):
            seen = []
            for step in range(1, W):
                seen += [w for w in (at - step, at + step) if 0 <= w < W]
            table_of.append(seen[i])
        w = jnp.int32(table_of[0])
        for at in range(1, W):
            w = jnp.where(z == at, table_of[at], w)
        return w

    arrivals = [arrival(i) for i in range(W - 1)]

    def weight_line(k, w, to):
        rows = plane.block(order_of(k, w), 0)
        return remote(weights.at[k, w, rows], weights.at[k, w, rows], zw_send.at[k, to], zw_recv.at[k, w], (c, to))

    def weight_first(k):
        for step in (1, 2, 3)[: W - 1]:
            for to, there in ((z - step, z >= step), (z + step, z + step < W)):

                @pl.when(there)
                def _():
                    weight_line(k, z, to).start()

    def weight_stage(k, w, s):
        order = order_of(k, w)
        rows = plane.block(order, s)
        return remote(
            weights.at[k, w, rows], weights.at[k, w, rows], pw_send.at[k, w, s], pw_recv.at[k, w, s],
            (plane.partner(order, s), z),
        )

    def weight_event(k, i, s):
        w = arrivals[i]
        if s == 0:
            weight_line(k, w, lax.rem(z + 1, W)).wait_recv()
        else:
            weight_stage(k, w, s - 1).wait_recv()
        if s < B:
            weight_stage(k, w, s).start()

    def weight_events(k, s):
        for i in range(W - 1):
            weight_event(k, i, s)

    def weight_drain(k):
        for step in range(1, W):
            to = lax.rem(z + step, W)
            weight_line(k, z, to).wait_send()
        for w in arrivals:
            for s in range(B):
                weight_stage(k, w, s).wait_send()

    def extra_copy(step):
        to = lax.rem(z + step, W)
        return remote(extra.at[z], extra.at[z], ex_send.at[step], ex_recv.at[step], (c, to))

    def extra_from(step):
        source = lax.rem(z + W - step, W)
        return remote(extra.at[source], extra.at[source], ex_send.at[step], ex_recv.at[step], (c, source))

    def halo(w, back):
        if back:
            return remote(near_give.at[w], near_back.at[w], back_send.at[w], back_recv.at[w], (c - 1, z))
        return remote(near_send.at[w], near_in.at[w], halo_send.at[w], halo_recv.at[w], (c + 1, z))

    def needs(source, target):
        need = jnp.bool_(False)
        for step in range(geo.far):
            size = 2 ** (step + 1)
            need = need | (target // size == source // size + 1)
        return need

    def far_copy(w, device, source):
        return remote(far_send.at[w], far_in.at[source, w], far_s.at[device, w], far_r.at[source, w], (device, z))

    def give_copy(w, device, source):
        return remote(
            far_give.at[device, w], far_back.at[source, w], farb_s.at[device, w], farb_r.at[source, w], (device, z)
        )

    def each_after(action):
        for step in range(1, C):
            device = jnp.minimum(c + step, C - 1)

            @pl.when((c + step < C) & needs(c, device))
            def _():
                action(device)

    def each_before(action):
        for step in range(1, C):
            device = jnp.maximum(c - step, 0)

            @pl.when((c - step >= 0) & needs(device, c))
            def _():
                action(device)

    def halo_start(w):
        @pl.when(c < C - 1)
        def _():
            halo(w, False).start()

        each_after(lambda device: far_copy(w, device, c).start())

    def halo_wait(w):
        @pl.when(c > 0)
        def _():
            halo(w, False).wait_recv()

        each_before(lambda device: far_copy(w, device, device).wait_recv())

    def give_start(w):
        @pl.when(c > 0)
        def _():
            halo(w, True).start()

        each_before(lambda device: give_copy(w, device, c).start())

    def give_wait(w):
        @pl.when(c < C - 1)
        def _():
            halo(w, True).wait_recv()

        each_after(lambda device: give_copy(w, device, device).wait_recv())

    first_three = [z] + arrivals

    def projection(w):
        project(w, n1, weights, extra, q, own, cells, near_send, far_send)
        halo_start(w)

    def attention(w):
        halo_wait(w)
        tables(geo, w, pick, own, cells, near_in, far_in, table)
        for tile in (0, 1):
            attend(geo, w, tile, q, table, bias, probs, mixed)

    weight_first(0)
    for step in range(1, W):
        extra_copy(step).start()
    loads[6].wait()
    normed, _ = norm_parts(x[...].astype(F32))
    n1[...] = (normed * n1g[...] + n1b[...]).astype(BF16)
    projection(z)
    bias[0] = mask_bias(geo, c, segs[pl.ds(z, 1), :], 0)
    bias[1] = mask_bias(geo, c, segs[pl.ds(z, 1), :], 1)
    pick = far_matrix(geo, c)
    weight_event(0, 0, 0)
    weight_event(0, 1, 0)
    weight_event(0, 0, 1)
    weight_event(0, 2, 0)
    loads[4].wait()
    weight_first(1)
    attention(z)
    weight_event(0, 1, 1)
    for step in range(1, W):
        extra_from(step).wait_recv()
    weight_event(0, 0, 2)
    weight_event(0, 2, 1)
    weight_events(1, 0)
    loads[5].wait()
    weight_first(2)
    for s in range(3, B + 1):
        weight_event(0, 0, s)
    projection(arrivals[0])
    weight_event(0, 1, 2)
    for s in range(3, B + 1):
        weight_event(0, 1, s)
    projection(arrivals[1])
    weight_event(0, 2, 2)
    weight_events(1, 1)
    for s in range(3, B + 1):
        weight_event(0, 2, s)
    projection(arrivals[2])
    attention(arrivals[0])
    weight_events(2, 0)
    attention(arrivals[1])
    weight_events(1, 2)
    attention(arrivals[2])
    weight_events(2, 1)
    for s in range(3, B + 1):
        weight_events(1, s)

    acc = x[...].astype(F32) + out_bias[...]
    for w in range(W):
        acc = acc + dot_nt(mixed[w], weights[0, w, :, 3 * LANES :])
    middle[...] = acc
    normed, _ = norm_parts(acc)
    n2[...] = (normed * n2g[...] + n2b[...]).astype(BF16)
    result[...] = acc + down_bias[...]
    feed(z, n2, weights, extra, hidden, slope, result)
    weight_events(2, 2)
    for i in range(W - 1):
        for s in range(3, B + 1):
            weight_event(2, i, s)
        feed(arrivals[i], n2, weights, extra, hidden, slope, result)
    gathered[z] = result[...].astype(BF16)

    def row_copy(at, w, to, relayed=False):
        rows = (gathered, source_all)[at]
        slot = w if relayed else to
        return remote(rows.at[w], rows.at[w], out_send.at[at, slot, int(relayed)], out_recv.at[at, w], (c, to))

    relays = W == 4
    inner = (z > 0) & (z < W - 1) if relays else jnp.bool_(False)
    across = jnp.where(z < W // 2, z + 2, z - 2)
    beside = W - 1 - z
    end = jnp.where(z < W // 2, 0, W - 1)

    def each_direct(action):
        for step in range(1, W):
            to = lax.rem(z + step, W)
            later = (z + to == W - 1) if relays else jnp.bool_(False)

            @pl.when(jnp.logical_not(later))
            def _():
                action(to)

    def rows_first(at):
        each_direct(lambda to: row_copy(at, z, to).start())

    def rows_relay(at):
        @pl.when(inner)
        def _():
            row_copy(at, across, end).wait_recv()
            row_copy(at, across, end, True).start()
            row_copy(at, z, beside).start()

    def rows_wait(at):
        for step in range(1, W):
            w = lax.rem(z + step, W)

            @pl.when(jnp.logical_not(inner & (w == across)))
            def _():
                row_copy(at, w, w).wait_recv()

    def rows_drain(at):
        each_direct(lambda to: row_copy(at, z, to).wait_send())

        @pl.when(inner)
        def _():
            row_copy(at, across, end, True).wait_send()
            row_copy(at, z, beside).wait_send()

    def reduce_copy(k, w, s):
        order = order_of(k, w)
        return remote(
            grads.at[k, w, plane.block(order, s, other=True)],
            landings[s].at[k, w],
            rs_send.at[k, w, s],
            rs_recv.at[k, w, s],
            (plane.partner(order, s), z),
        )

    def reduce_add(k, w, s):
        reduce_copy(k, w, s).wait_recv()
        rows = plane.block(order_of(k, w), s)
        grads[k, w, rows] = (grads[k, w, rows].astype(F32) + landings[s][k, w].astype(F32)).astype(BF16)
        if s > 0:
            reduce_copy(k, w, s - 1).start()
        else:
            line_send(k, w)

    def line_copy(k, w):
        rows = plane.block(order_of(k, w), 0)
        return remote(grads.at[k, w, rows], from_line.at[k, z], zl_send.at[k, w], zl_recv.at[k, z], (c, w))

    def line_send(k, w):
        @pl.when(w != z)
        def _():
            line_copy(k, w).start()

    def line_drain(k, w):
        @pl.when(w != z)
        def _():
            line_copy(k, w).wait_send()

    def own_rows(k):
        return plane.block(order_of(k, z), 0)

    def line_end(k):
        rows = own_rows(k)
        total_now = grads[k, z, rows].astype(F32)
        for step in range(1, W):
            source = lax.rem(z + step, W)
            remote(
                from_line.at[k, source], from_line.at[k, source], zl_send.at[k, source], zl_recv.at[k, source], (c, source)
            ).wait_recv()
            total_now = total_now + from_line[k, source].astype(F32)
        reduced[k, rows] = total_now.astype(BF16)
        gather_copy(k, 0).start()

    def gather_copy(k, s):
        order = order_of(k, z)
        rows = plane.block(order, s)
        return remote(reduced.at[k, rows], reduced.at[k, rows], ag_send.at[k, s], ag_recv.at[k, s], (plane.partner(order, s), z))

    def gather_next(k, s):
        gather_copy(k, s).wait_recv()
        if s + 1 < B:
            gather_copy(k, s + 1).start()

    rows_first(0)
    loads[7].wait()
    for w in range(W):
        feed_back(w == 0, w, g2, weights, n2, hidden, slope, sums, grads, total)
        reduce_copy(2, w, B - 1).start()
        reduce_copy(1, w, B - 1).start()
        if w > 0:
            reduce_add(2, w - 1, B - 1)
            reduce_add(1, w - 1, B - 1)
    normed, inverse = norm_parts(middle[...])
    d_normed = total[...]
    wide = g2[...].astype(F32)
    first = wide + norm_backward(d_normed, normed, inverse, n2g[...])
    g1[...] = first
    low = first.astype(BF16)
    reduce_add(2, W - 1, B - 1)
    reduce_add(1, W - 1, B - 1)
    for w in range(W):
        d_mixed[w] = dot_nn(low, weights[0, w, :, 3 * LANES :]).astype(BF16)
        grads[0, w, :, 3 * LANES :] = dot_tn(low, mixed[w]).astype(BF16)

    def reduce_both(w, s):
        reduce_add(2, w, s)
        reduce_add(1, w, s)

    def give(w):
        for tile in (0, 1):
            attend_back(geo, w, tile, q, table, probs, d_mixed, d_queries, d_table)
        return_cells(geo, w, pick, d_table, near_give, far_give)
        give_start(w)

    def take(w):
        give_wait(w)
        project_back(geo, w == 0, w, weights, n1, d_queries, d_table, near_back, far_back, sums, grads, total)
        reduce_copy(0, w, B - 1).start()

    give(0)
    give(1)
    for s in range(B - 2, 0, -1):
        reduce_both(0, s)
    give(2)
    give(3)
    for s in range(B - 2, 0, -1):
        reduce_both(1, s)
    put_sums(geo, sums, 2, jnp.sum(first, axis=0, keepdims=True))
    put_sums(geo, sums, 3, jnp.sum(d_normed * normed, axis=0, keepdims=True))
    put_sums(geo, sums, 4, jnp.sum(d_normed, axis=0, keepdims=True))
    put_sums(geo, sums, 5, jnp.sum(wide, axis=0, keepdims=True))
    take(0)
    take(1)
    for s in range(B - 2, 0, -1):
        reduce_both(2, s)
    reduce_both(0, 0)
    take(2)
    take(3)
    normed, inverse = norm_parts(x[...].astype(F32))
    d_normed = total[...]
    source_all[z] = (g1[...] + norm_backward(d_normed, normed, inverse, n1g[...])).astype(BF16)
    rows_relay(0)
    for s in range(B - 2, 0, -1):
        reduce_both(3, s)
    reduce_both(1, 0)
    for w in range(W):
        reduce_add(0, w, B - 1)
    put_sums(geo, sums, 0, jnp.sum(d_normed * normed, axis=0, keepdims=True))
    put_sums(geo, sums, 1, jnp.sum(d_normed, axis=0, keepdims=True))

    def sums_copy(step):
        to = lax.rem(z + step, W)
        return remote(sums.at[to], sums_in.at[step], sm_send.at[step], sm_recv.at[step], (c, to))

    def sums_stage(s):
        return remote(sums_all.at[s], sums_got.at[s], sc_send.at[s], sc_recv.at[s], (plane.flip(1 << s), z))

    for step in range(1, W):
        sums_copy(step).start()
    reduce_both(2, 0)
    reduce_both(3, 0)
    rows_first(1)
    for s in range(B - 2, 0, -1):
        for w in range(W):
            reduce_add(0, w, s)
    line_end(2)
    line_end(1)
    for w in range(W):
        reduce_add(0, w, 0)
    total_sums = sums[z]
    for step in range(1, W):
        sums_copy(step).wait_recv()
        total_sums = total_sums + sums_in[step]
    sums_all[0] = total_sums
    sums_stage(0).start()
    for s in range(B):
        sums_stage(s).wait_recv()
        sums_all[s + 1] = sums_all[s] + sums_got[s]
        if s + 1 < B:
            sums_stage(s + 1).start()
        gather_next(2, s)
        gather_next(1, s)
    rows_wait(0)
    rows_relay(1)
    line_end(0)
    stores = [
        pltpu.make_async_copy(gathered, out_result, store_sem.at[0]),
        pltpu.make_async_copy(source_all, out_source, store_sem.at[1]),
        pltpu.make_async_copy(sums_all.at[B], out_sums, store_sem.at[2]),
        pltpu.make_async_copy(reduced.at[1], out_grads.at[1], store_sem.at[3]),
        pltpu.make_async_copy(reduced.at[2], out_grads.at[2], store_sem.at[4]),
        pltpu.make_async_copy(reduced.at[0], out_grads.at[0], store_sem.at[5]),
    ]
    for at in (0, 2, 3, 4):
        stores[at].start()
    for s in range(B):
        gather_next(0, s)
    stores[5].start()
    rows_wait(1)
    stores[1].start()

    for k in range(3):
        weight_drain(k)
        for w in range(W):
            for s in range(B):
                reduce_copy(k, w, s).wait_send()
            line_drain(k, w)
        for s in range(B):
            gather_copy(k, s).wait_send()
    for at in (0, 1):
        rows_drain(at)
    for step in range(1, W):
        extra_copy(step).wait_send()
        sums_copy(step).wait_send()
    for s in range(B):
        sums_stage(s).wait_send()

    for w in range(W):

        @pl.when(c < C - 1)
        def _():
            halo(w, False).wait_send()

        @pl.when(c > 0)
        def _():
            halo(w, True).wait_send()

        each_after(lambda device: far_copy(w, device, c).wait_send())
        each_before(lambda device: give_copy(w, device, c).wait_send())
    for copy in stores:
        copy.wait()


def unpack(result, source, grads, sums, *outs):
    (
        layer_out, input_grad, d_n1g, d_n1b, d_q, d_qb, d_k, d_v, d_vb, d_o, d_ob, d_n2g, d_n2b, d_up, d_upb, d_down, d_db,
    ) = outs
    layer_out[...] = result[...].astype(F32)
    input_grad[...] = source[...].astype(F32)
    wide = grads[0].astype(F32)
    d_q[...] = wide[:, :LANES]
    d_k[...] = wide[:, LANES : 2 * LANES]
    d_v[...] = wide[:, 2 * LANES : 3 * LANES]
    d_o[...] = wide[:, 3 * LANES :].T
    d_up[...] = grads[1].astype(F32)
    d_down[...] = grads[2].astype(F32)
    for at, out in enumerate((d_n1g, d_n1b, d_ob, d_n2g, d_n2b, d_db)):
        row, lane = 2 + at // 4, at % 4 * LANES
        out[...] = sums[row : row + 1, lane : lane + LANES]
    d_qb[...] = sums[1:2, :LANES]
    d_vb[...] = sums[1:2, LANES : 2 * LANES]
    d_upb[...] = sums[0:1, :]


def shards(
    x_in,
    grad_out,
    seg_ids,
    norm1_gain,
    norm1_bias,
    q_weight,
    q_bias,
    k_weight,
    v_weight,
    v_bias,
    out_weight,
    out_bias,
    norm2_gain,
    norm2_bias,
    up_weight,
    up_bias,
    down_weight,
    down_bias,
):
    C, W = lax.axis_size("ctx"), lax.axis_size("wt")
    runs, T, width = x_in.shape
    hidden = up_weight.shape[1]
    geo = Geometry(C, W, T)
    S, B = geo.slots, C.bit_length() - 1
    each = width // C
    assert runs == W and hidden == width and q_weight.shape[1] == LANES and T == 256
    sds = jax.ShapeDtypeStruct
    vmem, dma = pltpu.VMEM, pltpu.SemaphoreType.DMA
    row = lambda v: v.reshape(1, -1)
    pair = 2 * LANES
    scratch = [
        vmem((3, W, width, width), BF16),
        vmem((W, 8, width), F32),
        vmem((T, width), BF16),
        vmem((T, width), BF16),
        vmem((LANES, width), BF16),
        vmem((T, width), BF16),
        vmem((W, T, LANES), BF16),
        vmem((W, T, pair), BF16),
        vmem((W, 224, pair), BF16),
        vmem((W, 80, pair), BF16),
        vmem((W, 16, pair), BF16),
        vmem((W, 80, pair), BF16),
        vmem((C, W, 16, pair), BF16),
        vmem((W, 2, S, pair), BF16),
        vmem((2, S, geo.tile), F32),
        vmem((W, 2, S, pair), BF16),
        vmem((W, T, LANES), BF16),
        vmem((T, width), F32),
        vmem((T, width), BF16),
        vmem((W, T, hidden), BF16),
        vmem((W, T, hidden), F32),
        vmem((T, width), F32),
        vmem((T, width), F32),
        vmem((T, width), F32),
        vmem((W, T, LANES), BF16),
        vmem((W, T, LANES), BF16),
        vmem((W, 2, S, pair), F32),
        vmem((W, 80, pair), BF16),
        vmem((C, W, 16, pair), BF16),
        vmem((W, 80, pair), BF16),
        vmem((C, W, 16, pair), BF16),
        vmem((3, W, width, width), BF16),
        vmem((W, 8, width), F32),
        vmem((W, T, width), BF16),
        vmem((W, T, width), BF16),
        vmem((3, W, each, width), BF16),
        vmem((3, width, width), BF16),
        vmem((W, 8, width), F32),
        vmem((B + 1, 8, width), F32),
        vmem((B, 8, width), F32),
        dma((8,)),
        dma((6,)),
        dma((3, W)),
        dma((3, W)),
        dma((3, W, B)),
        dma((3, W, B)),
        dma((W,)),
        dma((W,)),
        dma((W,)),
        dma((W,)),
        dma((C, W)),
        dma((C, W)),
        dma((W,)),
        dma((W,)),
        dma((C, W)),
        dma((C, W)),
        dma((3, W, B)),
        dma((3, W, B)),
        dma((3, W)),
        dma((3, W)),
        dma((3, B)),
        dma((3, B)),
        dma((2, W, 2)),
        dma((2, W)),
        dma((W,)),
        dma((W,)),
        dma((B,)),
        dma((B,)),
    ] + [vmem((3, W, each * 2**s, width), BF16) for s in range(B)]
    far, near = pl.BlockSpec(memory_space=pl.ANY), pl.BlockSpec(memory_space=pltpu.VMEM)
    result, source, grads, sums = pl.pallas_call(
        functools.partial(fused, geo),
        name="fused",
        out_shape=[sds((W, T, width), BF16), sds((W, T, width), BF16), sds((3, width, width), BF16), sds((8, width), F32)],
        in_specs=[far, far, near, near, near, far, near, far, far, near, far, near, near, near, far, near, far, near],
        out_specs=[far] * 4,
        scratch_shapes=scratch,
        compiler_params=pltpu.CompilerParams(collective_id=0, has_side_effects=True, vmem_limit_bytes=58 * 2**20),
    )(
        x_in, grad_out, seg_ids, row(norm1_gain), row(norm1_bias), q_weight, row(q_bias), k_weight, v_weight, row(v_bias),
        out_weight, row(out_bias), row(norm2_gain), row(norm2_bias), up_weight, row(up_bias), down_weight, row(down_bias),
    )
    part = width // W
    rows = lambda shape: pl.BlockSpec(shape, lambda i: (i, 0))
    still = lambda shape: pl.BlockSpec(shape, lambda i: (0, 0))
    one, wide = (sds((1, LANES), F32), still((1, LANES))), (sds((1, hidden), F32), still((1, hidden)))
    blocks = (sds((W, T, width), F32), pl.BlockSpec((1, T, width), lambda i: (i, 0, 0)))
    thin = (sds((width, LANES), F32), rows((part, LANES)))
    full = (sds((width, width), F32), rows((part, width)))
    turned = (sds((LANES, width), F32), pl.BlockSpec((LANES, part), lambda i: (0, i)))
    outs = [blocks, blocks, one, one, thin, one, thin, thin, one, turned, one, one, one, full, wide, full, one]
    values = pl.pallas_call(
        unpack,
        name="unpack",
        grid=(W,),
        out_shape=[o[0] for o in outs],
        in_specs=[blocks[1], blocks[1], pl.BlockSpec((3, part, width), lambda i: (0, i, 0)), still((8, width))],
        out_specs=[o[1] for o in outs],
    )(result, source, grads, sums)
    return tuple(v.reshape(-1) if v.shape[0] == 1 else v for v in values)


def solution(mesh):
    in_specs = (
        P(None, "ctx", None),
        P(None, "ctx", None),
        P(),
        P(),
        P(),
        P(None, "wt"),
        P("wt"),
        P(None, "wt"),
        P(None, "wt"),
        P("wt"),
        P("wt", None),
        P(),
        P(),
        P(),
        P(None, "wt"),
        P("wt"),
        P("wt", None),
        P(),
    )
    out_specs = (
        P(None, "ctx", None),
        P(None, "ctx", None),
        P("wt"),
        P("wt"),
        P(None, "wt"),
        P("wt"),
        P(None, "wt"),
        P(None, "wt"),
        P("wt"),
        P("wt", None),
        P("wt"),
        P("wt"),
        P("wt"),
        P(None, "wt"),
        P("wt"),
        P("wt", None),
        P("wt"),
    )
    return jax.shard_map(shards, mesh=mesh, in_specs=in_specs, out_specs=out_specs, check_vma=False)
```

```python
import functools

import jax
import jax.numpy as jnp
from jax import lax
from jax.experimental import pallas as pl
from jax.experimental.pallas import tpu as pltpu
from jax.sharding import PartitionSpec as P

HEAD_DIM = 64
BLOCK = 16
LEVELS = 10
FINE = 3
EPSILON = 1e-05
NEGATIVE = -1e30
LOG_TWO = 0.6931471805599453
LANES = 128
BF16 = jnp.bfloat16
F32 = jnp.float32


def dot(left, right, dims):
    return lax.dot_general(left, right, (dims, ((), ())), preferred_element_type=F32)


def dot_nn(left, right):
    return dot(left, right, ((1,), (0,)))


def dot_nt(left, right):
    return dot(left, right, ((1,), (1,)))


def dot_tn(left, right):
    return dot(left, right, ((0,), (0,)))


def norm_parts(source):
    centre = jnp.mean(source, axis=-1, keepdims=True)
    centred = source - centre
    variance = jnp.mean(centred * centred, axis=-1, keepdims=True)
    inverse = lax.rsqrt(variance + EPSILON)
    return centred * inverse, inverse


def norm_backward(upstream, normed, inverse, gain):
    scaled = upstream * gain
    first_mean = jnp.mean(scaled, axis=-1, keepdims=True)
    second_mean = jnp.mean(scaled * normed, axis=-1, keepdims=True)
    return inverse * (scaled - first_mean - normed * second_mean)


def iota(shape, axis):
    return lax.broadcasted_iota(jnp.int32, shape, axis)


class Geometry:
    def __init__(self, ctx, wt, tok_dev):
        self.ctx, self.wt, self.tok_dev = ctx, wt, tok_dev
        tokens = ctx * tok_dev
        self.levels = len([l for l in range(LEVELS) if BLOCK * 2**l < tokens])
        self.own_cells = [tok_dev // 2**l if l <= FINE else 0 for l in range(self.levels)]
        self.tile = tok_dev // 2
        self.tile_slots = [BLOCK + self.tile] + [BLOCK * 4 >> (l - 1) if l < FINE else BLOCK for l in range(1, self.levels)]
        self.slots = sum(self.tile_slots)
        self.slot_at = [sum(self.tile_slots[:l]) for l in range(self.levels + 1)]
        self.far = self.levels - (FINE + 2)
        self.near = FINE + 2


def pool_matrix():
    parts = []
    for level, count in ((1, 128), (2, 64), (3, 32)):
        hit = (iota((count, 256), 1) >> level) == iota((count, 256), 0)
        parts.append(jnp.where(hit, 1.0 / 2**level, 0.0))
    return jnp.concatenate(parts, axis=0).astype(BF16)


def coarse_matrix():
    row, column = iota((32, 32), 0), iota((32, 32), 1)
    out = jnp.zeros((32, 32), F32)
    first = 0
    for level, count in ((4, 16), (5, 8), (6, 4), (7, 2), (8, 1)):
        up = level - FINE
        hit = (row >= first) & (row < first + count) & ((column >> up) == row - first)
        out = jnp.where(hit, 1.0 / 2**up, out)
        first += count
    return out.astype(BF16)


def far_matrix(geo, me):
    parts = []
    first = 0
    for step in range(geo.far):
        up = step + 1
        each = BLOCK >> up
        row, column = iota((BLOCK, geo.ctx * BLOCK), 0), iota((BLOCK, geo.ctx * BLOCK), 1)
        group = (me >> up) - 1
        device = (group << up) + (row >> (4 - up))
        wanted = device * BLOCK + first + (row & (each - 1))
        parts.append(jnp.where((column == wanted) & (group >= 0), 1.0, 0.0))
        first += each
    return jnp.concatenate(parts, axis=0).astype(BF16)


def mask_bias(geo, me, segs, tile):
    first_pos = me * geo.tok_dev + tile * geo.tile
    seg_one = jnp.sum((segs < 1).astype(jnp.int32), axis=1, keepdims=True)
    seg_two = jnp.sum((segs < 2).astype(jnp.int32), axis=1, keepdims=True)
    position = first_pos + iota((1, geo.tile), 1)
    begins = jnp.where(position >= seg_two, seg_two, jnp.where(position >= seg_one, seg_one, 0))
    parts = []
    for level in range(geo.levels):
        size, shift = 2**level, level + 4
        count = geo.tile_slots[level]
        span = BLOCK * size
        if level <= FINE:
            base = first_pos - span
        else:
            base = (((me * geo.tok_dev) >> shift) - 1) << shift
        begin = base + size * iota((count, geo.tile), 0)
        lower = jnp.maximum(((position >> shift) - 1) << shift, begins)
        if level == 0:
            upper = position + 1
        else:
            upper = ((position >> (shift - 1)) - 1) << (shift - 1)
        valid = (begin >= lower) & (begin + size <= upper)
        parts.append(jnp.where(valid, level * LOG_TWO, NEGATIVE))
    return jnp.concatenate(parts, axis=0)


def both_heads(pair):
    lane = iota(pair.shape, 1)
    zero = jnp.zeros_like(pair)
    return jnp.concatenate([jnp.where(lane < HEAD_DIM, pair, zero), jnp.where(lane >= HEAD_DIM, pair, zero)], axis=0)


def own_lanes(stacked):
    rows = stacked.shape[0] // 2
    lane = iota((rows, stacked.shape[1]), 1)
    return jnp.where(lane < HEAD_DIM, stacked[:rows], stacked[rows:])


def project(w, n1, weights, extra, q, own, cells, near, far):
    out = dot_nn(n1[...], weights[0][w])
    bias = extra[w, 1:2, :]
    q[w] = ((out[:, :LANES] + bias[:, :LANES]).astype(BF16) * 0.125).astype(BF16)
    kv = jnp.concatenate(
        [out[:, LANES : 2 * LANES], out[:, 2 * LANES :] + bias[:, LANES : 2 * LANES]], axis=1
    ).astype(BF16)
    own[w] = kv
    fine = dot_nn(pool_matrix(), kv).astype(BF16)
    cells[w] = fine
    rough = dot_nn(coarse_matrix(), fine[192:224]).astype(BF16)
    near[w, 0:16] = kv[240:256]
    near[w, 16:32] = fine[112:128]
    near[w, 32:48] = fine[176:192]
    near[w, 48:64] = fine[208:224]
    near[w, 64:80] = rough[0:16]
    far[w] = rough[16:32]


def tables(geo, w, pick, own, cells, near_in, far_in, table):
    blocks = far_in[:, w].reshape(geo.ctx * BLOCK, 2 * LANES)
    rough = dot_nn(pick, blocks).astype(BF16)
    at = geo.slot_at
    table[w, 0, 0:16] = near_in[w, 0:16]
    table[w, 0, 16:144] = own[w, 0:128]
    table[w, 1, 0:144] = own[w, 112:256]
    table[w, 0, at[1] : at[1] + 16] = near_in[w, 16:32]
    table[w, 0, at[1] + 16 : at[2]] = cells[w, 0:48]
    table[w, 1, at[1] : at[2]] = cells[w, 48:112]
    table[w, 0, at[2] : at[2] + 16] = near_in[w, 32:48]
    table[w, 0, at[2] + 16 : at[3]] = cells[w, 128:144]
    table[w, 1, at[2] : at[3]] = cells[w, 144:176]
    table[w, 0, at[3] : at[4]] = near_in[w, 48:64]
    table[w, 1, at[3] : at[4]] = cells[w, 192:208]
    for tile in (0, 1):
        table[w, tile, at[4] : at[5]] = near_in[w, 64:80]
        table[w, tile, at[5] :] = rough


def attend(geo, w, tile, q, table, bias, probs, mixed):
    rows = slice(tile * geo.tile, (tile + 1) * geo.tile)
    both = both_heads(q[w, rows, :])
    level_bias = bias[tile]
    scores = dot_nt(table[w, tile, :, :LANES], both)
    scores = scores + jnp.concatenate([level_bias, level_bias], axis=1)
    top = jnp.max(scores, axis=0, keepdims=True)
    exponent = jnp.exp(scores - top)
    total = jnp.sum(exponent, axis=0, keepdims=True)
    low = (exponent * (1.0 / total)).astype(BF16)
    probs[w, tile] = low
    mixed[w, rows, :] = own_lanes(dot_tn(low, table[w, tile, :, LANES:])).astype(BF16)


def attend_back(geo, w, tile, q, table, probs, d_mixed, d_queries, d_table):
    rows = slice(tile * geo.tile, (tile + 1) * geo.tile)
    both = both_heads(q[w, rows, :])
    d_both = both_heads(d_mixed[w, rows, :])
    low = probs[w, tile]
    d_probs = dot_nt(table[w, tile, :, LANES:], d_both)
    wide = low.astype(F32)
    product = wide * d_probs
    centre = jnp.sum(product, axis=0, keepdims=True)
    d_scores = (product - wide * centre).astype(BF16)
    d_table[w, tile, :, :LANES] = dot_nn(d_scores, both)
    d_table[w, tile, :, LANES:] = dot_nn(low, d_both)
    back = own_lanes(dot_tn(d_scores, table[w, tile, :, :LANES]))
    d_queries[w, rows, :] = (back * 0.125).astype(BF16)


def return_cells(geo, w, pick, d_table, near, far):
    at = geo.slot_at
    near[w, 0:16] = d_table[w, 0, 0:16].astype(BF16)
    near[w, 16:32] = d_table[w, 0, at[1] : at[1] + 16].astype(BF16)
    near[w, 32:48] = d_table[w, 0, at[2] : at[2] + 16].astype(BF16)
    near[w, 48:64] = d_table[w, 0, at[3] : at[4]].astype(BF16)
    near[w, 64:80] = (d_table[w, 0, at[4] : at[5]] + d_table[w, 1, at[4] : at[5]]).astype(BF16)
    rough = (d_table[w, 0, at[5] :] + d_table[w, 1, at[5] :]).astype(BF16)
    far[:, w] = dot_tn(pick, rough).astype(BF16).reshape(geo.ctx, BLOCK, 2 * LANES)


def own_gradients(geo, w, d_table, near_back, far_back):
    at = geo.slot_at
    first, second = d_table.at[w, 0], d_table.at[w, 1]
    back = near_back[w].astype(F32)
    tokens = jnp.concatenate(
        [first[16:128], first[128:144] + second[0:16], second[16:128], second[128:144] + back[0:16]], axis=0
    )
    far = jnp.sum(far_back[:, w].astype(F32), axis=0)
    rough = jnp.concatenate([back[64:80], far], axis=0)
    fine = dot_tn(coarse_matrix(), rough.astype(BF16))
    level3 = jnp.concatenate([second[at[3] : at[4]], back[48:64]], axis=0) + fine
    cells = jnp.concatenate(
        [
            first[at[1] + 16 : at[2]],
            second[at[1] : at[2]],
            back[16:32],
            first[at[2] + 16 : at[3]],
            second[at[2] : at[3]],
            back[32:48],
            level3,
        ],
        axis=0,
    )
    return tokens + dot_tn(pool_matrix(), cells.astype(BF16))


def feed(w, n2, weights, extra, hidden, slope, result):
    pre = dot_nn(n2[...], weights[1][w]) + extra[w, 0:1, :]
    gate = jax.nn.sigmoid(pre)
    hidden[w] = (pre * gate).astype(BF16)
    slope[w] = gate * (1.0 + pre * (1.0 - gate))
    result[...] += dot_nn(hidden[w], weights[2][w])


def feed_back(first, w, g2, weights, n2, hidden, slope, sums, grads, total):
    d_hidden = dot_nt(g2[...], weights[2][w]).astype(BF16).astype(F32)
    d_up = (d_hidden * slope[w]).astype(BF16)
    sums[w, 0:1, :] = jnp.sum(d_up.astype(F32), axis=0, keepdims=True)
    grads[2][w] = dot_tn(hidden[w], g2[...]).astype(BF16)
    grads[1][w] = dot_tn(n2[...], d_up).astype(BF16)
    part = dot_nt(d_up, weights[1][w])
    total[...] = part if first else total[...] + part


def put_sums(geo, sums, column, row):
    at, lanes = 2 + column // 4, slice(column % 4 * LANES, (column % 4 + 1) * LANES)
    for w in range(geo.wt):
        sums[w, at : at + 1, lanes] = row[:, w * LANES : (w + 1) * LANES]


def project_back(geo, first, w, weights, n1, d_queries, d_table, near_back, far_back, sums, grads, total):
    kv = own_gradients(geo, w, d_table, near_back, far_back).astype(BF16)
    d_qkv = jnp.concatenate([d_queries[w], kv], axis=1)
    sums[w, 1:2, :LANES] = jnp.sum(d_qkv[:, :LANES].astype(F32), axis=0, keepdims=True)
    sums[w, 1:2, LANES : 2 * LANES] = jnp.sum(d_qkv[:, 2 * LANES :].astype(F32), axis=0, keepdims=True)
    grads[0][w] = dot_tn(n1[...], d_qkv).astype(BF16)
    part = dot_nt(d_qkv, weights[0][w])
    total[...] = part if first else total[...] + part


def remote(source, target, sent, landed, device):
    return pltpu.make_async_remote_copy(source, target, sent, landed, device_id=device, device_id_type=pl.DeviceIdType.MESH)


class Plane:
    def __init__(self, ctx, c, rows):
        self.ctx, self.c = ctx, c
        self.bits = ctx.bit_length() - 1
        self.each = rows // ctx
        plane_bits = self.bits - 1
        half = plane_bits // 2
        self.plane_bits, self.half = plane_bits, half
        self.places = self.places_of(c)
        self.masks = (
            [2 << s for s in range(plane_bits)] + [1],
            [2 << (s + half) % plane_bits for s in range(plane_bits)] + [1],
        )

    def places_of(self, device):
        plane, core = device // 2, device % 2
        turned = plane // 2**self.half + plane % 2**self.half * 2 ** (self.plane_bits - self.half)
        top = core * 2**self.plane_bits
        return plane + top, turned + top

    def place(self, order, device=None):
        places = self.places if device is None else self.places_of(device)
        if isinstance(order, int):
            return places[order]
        return jnp.where(order == 0, places[0], places[1])

    def partner(self, order, stage):
        if isinstance(order, int):
            return self.flip(self.masks[order][stage])
        return jnp.where(order == 0, self.flip(self.masks[0][stage]), self.flip(self.masks[1][stage]))

    def flip(self, mask):
        return self.c + mask * (1 - 2 * (self.c // mask % 2))

    def flips(self, bits):
        device = self.c
        for s in range(self.bits):
            if bits >> s & 1:
                device = device + (1 << s) * (1 - 2 * (self.c // (1 << s) % 2))
        return device

    def block(self, order, stage, other=False, device=None):
        index = self.place(order, device) // 2**stage
        if other:
            index = index + 1 - 2 * (index % 2)
        size = self.each * 2**stage
        return pl.ds(pl.multiple_of(index * size, size), size)


SCHEDULE = (
    ("send_shards", 1), ("masks",), ("send_shards", 0), ("event", 1, 0, 0), ("first_norm",), ("projection", 0),
    ("send_shards", 3), ("event", 0, 0, 0), ("event", 1, 1, 0), ("event", 0, 0, 1), ("event", 0, 1, 0),
    ("event", 0, 2, 0), ("send_shards", 2), ("event", 3, 0, 0), ("event", 1, 2, 0), ("event", 1, 1, 1),
    ("send_biases",), ("event", 0, 2, 1), ("event", 1, 0, 1), ("event", 0, 0, 2), ("event", 0, 1, 1),
    ("event", 3, 1, 0), ("event", 0, 0, 3), ("event", 2, 0, 0), ("event", 2, 0, 1), ("event", 2, 1, 0),
    ("event", 2, 1, 1), ("event", 0, 1, 2), ("attention", 0), ("event", 3, 1, 1), ("event", 3, 1, 2),
    ("wait_biases",), ("event", 3, 0, 1), ("projection", 1), ("event", 0, 2, 2), ("event", 3, 2, 0),
    ("event", 1, 1, 2), ("event", 3, 1, 3), ("event", 0, 1, 3), ("projection", 2), ("event", 0, 2, 3),
    ("event", 3, 0, 2), ("event", 2, 0, 2), ("projection", 3), ("event", 1, 0, 2), ("event", 3, 2, 1),
    ("event", 3, 2, 2), ("event", 3, 0, 3), ("event", 1, 0, 3), ("event", 2, 2, 0), ("event", 2, 1, 2),
    ("attention", 1), ("event", 2, 2, 1), ("event", 1, 2, 1), ("attention", 2), ("event", 3, 2, 3), ("attention", 3),
    ("event", 2, 1, 3), ("second_norm",), ("forth", 0), ("back", 0), ("halve", 2, 0), ("halve", 1, 0),
    ("event", 2, 0, 3), ("forth", 1), ("event", 2, 2, 2), ("back", 1), ("halve", 1, 1), ("event", 1, 2, 2),
    ("halve", 2, 1), ("add", 1, 0, 2), ("event", 1, 1, 3), ("forth", 2), ("event", 2, 2, 3), ("add", 1, 1, 2),
    ("event", 1, 2, 3), ("forth", 3), ("layer_rows",), ("add", 2, 1, 2), ("rows_first", 1), ("add", 2, 0, 2),
    ("back", 3), ("halve", 1, 3), ("back", 2), ("second_back",), ("out_back", 3), ("out_back", 1), ("out_back", 0),
    ("halve", 3, 0), ("halve", 2, 2), ("give", 1), ("out_back", 2), ("rows_first", 0), ("give", 0), ("halve", 3, 1),
    ("give", 3), ("halve", 3, 3), ("halve", 2, 3), ("give", 2), ("add", 3, 1, 2), ("halve", 1, 2), ("add", 3, 3, 2),
    ("take", 1), ("rows_relay", 1, 0), ("add", 2, 2, 2), ("add", 2, 0, 1), ("halve", 0, 1), ("add", 1, 2, 2),
    ("take", 0), ("halve", 0, 0), ("rows_relay", 1, 1), ("add", 1, 3, 2), ("take", 3), ("halve", 0, 3),
    ("halve", 3, 2), ("take", 2), ("halve", 0, 2), ("source",), ("rows_first", 2), ("rows_relay", 0, 1),
    ("add", 2, 2, 1), ("add", 3, 0, 2), ("add", 1, 0, 1), ("add", 3, 2, 2), ("add", 1, 1, 1), ("add", 2, 3, 2),
    ("add", 1, 3, 1), ("add", 1, 2, 1), ("add", 2, 1, 1), ("rows_relay", 0, 0), ("add", 3, 1, 1), ("send_sums",),
    ("add", 3, 2, 1), ("rows_relay", 2, 0), ("add", 2, 2, 0), ("add", 1, 1, 0), ("add", 2, 3, 1), ("add", 0, 2, 2),
    ("add", 0, 0, 2), ("add", 3, 0, 1), ("add", 0, 1, 2), ("add", 1, 2, 0), ("add", 1, 3, 0), ("add", 0, 3, 2),
    ("add", 3, 2, 0), ("rows_relay", 2, 1), ("add", 3, 3, 1), ("add", 0, 0, 1), ("add", 3, 1, 0), ("add", 3, 0, 0),
    ("add", 2, 3, 0), ("add", 1, 0, 0), ("line_over", 1), ("add", 2, 1, 0), ("add", 0, 1, 1), ("add", 0, 3, 1),
    ("add", 3, 3, 0), ("add", 0, 2, 1), ("add", 0, 0, 0), ("add_sums", 0), ("line_over", 3), ("add", 2, 0, 0),
    ("rows_wait", 1), ("line_over", 2), ("line_pass", 1), ("add", 0, 1, 0), ("add", 0, 3, 0), ("line_end", 1),
    ("gather", 1, 0), ("add", 0, 2, 0), ("line_pass", 2), ("line_over", 0), ("gather", 1, 1), ("line_pass", 3),
    ("rows_first", 3), ("add_sums", 1), ("line_end", 3), ("gather", 3, 0), ("line_end", 2), ("gather", 2, 0),
    ("gather", 1, 2), ("add_sums", 2), ("line_pass", 0), ("line_end", 0), ("gather", 0, 0), ("gather", 3, 1),
    ("gather", 2, 1), ("gather", 0, 1), ("rows_relay", 3, 0), ("gather", 2, 2), ("rows_wait", 2), ("gather", 1, 3),
    ("rows_relay", 3, 1), ("gather", 3, 2), ("gather", 2, 3), ("gather", 0, 2), ("gather", 3, 3), ("add_sums", 3),
    ("store", 2), ("rows_wait", 0), ("store", 6), ("gather", 0, 3), ("rows_wait", 3), ("store", 1), ("store", 5),
    ("store", 0), ("store", 3), ("store", 4),
)
FIRST_STAGE = (0, 0, 1, 1)


def fused(geo, *refs):
    (
        x_hbm, g_hbm, segs, n1g, n1b, q_hbm, q_bias, k_hbm, v_hbm, v_bias, o_hbm, out_bias, n2g, n2b,
        up_hbm, up_bias, down_hbm, down_bias,
        out_result, out_source, out_a, out_u, out_d, out_o, out_sums,
        w_a, w_u, w_d, w_o, extra, x, g2, o_own, n1, q, own, cells, near_send, far_send, near_in, far_in,
        table, bias, probs, mixed, middle, n2, hidden, slope, result, total, g1, d_mixed, d_queries, d_table,
        g1_low, near_give, far_give, near_back, far_back, g_a, g_u, g_d, g_o, sums, gathered, source_all,
        line_a, line_u, line_d, line_o, end_a, end_u, end_d, end_o, in_a, in_u, in_d, in_o, r_a, r_u, r_d, r_o, sums_in, sums_all, sums_got,
        load_sem, store_sem, zw_send, zw_recv, pw_send, pw_recv, ex_send, ex_recv, halo_send, halo_recv,
        far_s, far_r, back_send, back_recv, farb_s, farb_r, rs_send, rs_recv, zl_send, zl_recv, zx_recv, zy_recv,
        ag_send, ag_recv, out_send, out_recv, sm_send, sm_recv, sc_send, sc_recv,
        *landings,
    ) = refs
    weights, grads, reduced = (w_a, w_u, w_d, w_o), (g_a, g_u, g_d, g_o), (r_a, r_u, r_d, r_o)
    from_line, from_end, from_inner = (line_a, line_u, line_d, line_o), (end_a, end_u, end_d, end_o), (in_a, in_u, in_d, in_o)
    C, W = geo.ctx, geo.wt
    c, z = lax.axis_index("ctx"), lax.axis_index("wt")
    plane = Plane(C, c, 512)
    B = plane.bits

    loads = [
        pltpu.make_async_copy(q_hbm, weights[0].at[z, :, pl.ds(0, LANES)], load_sem.at[0]),
        pltpu.make_async_copy(k_hbm, weights[0].at[z, :, pl.ds(LANES, LANES)], load_sem.at[1]),
        pltpu.make_async_copy(v_hbm, weights[0].at[z, :, pl.ds(2 * LANES, LANES)], load_sem.at[2]),
        pltpu.make_async_copy(o_hbm, o_own, load_sem.at[3]),
        pltpu.make_async_copy(up_hbm, weights[1].at[z], load_sem.at[4]),
        pltpu.make_async_copy(down_hbm, weights[2].at[z], load_sem.at[5]),
        pltpu.make_async_copy(x_hbm.at[z], x, load_sem.at[6]),
        pltpu.make_async_copy(g_hbm.at[z], g2, load_sem.at[7]),
    ]
    for copy in loads:
        copy.start()
    near_in[...] = jnp.zeros_like(near_in)
    far_in[...] = jnp.zeros_like(far_in)
    near_back[...] = jnp.zeros_like(near_back)
    far_back[...] = jnp.zeros_like(far_back)
    sums[...] = jnp.zeros_like(sums)
    extra[z] = jnp.zeros_like(extra[z])
    extra[z, 0:1, :] = up_bias[...]
    extra[z, 1:2, :LANES] = q_bias[...]
    extra[z, 1:2, LANES : 2 * LANES] = v_bias[...]

    barrier = pltpu.get_barrier_semaphore()
    for step in range(1, C):
        pl.semaphore_signal(barrier, inc=1, device_id=(lax.rem(c + step, C), z), device_id_type=pl.DeviceIdType.MESH)
    for step in range(1, W):
        pl.semaphore_signal(barrier, inc=1, device_id=(c, lax.rem(z + step, W)), device_id_type=pl.DeviceIdType.MESH)
    for copy in loads[:4]:
        copy.wait()
    weights[3][z] = o_own[...].T
    pl.semaphore_wait(barrier, C + W - 2)

    def order_of(k, w):
        return (k + w) % 2

    relays = W == 4
    inner = (z > 0) & (z < W - 1) if relays else jnp.bool_(False)
    across = jnp.where(z < W // 2, z + 2, z - 2)
    beside = W - 1 - z
    end = jnp.where(z < W // 2, 0, W - 1)
    near_inner = jnp.where(z < W // 2, 1, W - 2)

    def arrival(i, relayed):
        table_of = []
        for at in range(W):
            seen = []
            for step in range(1, W):
                seen += [w for w in (at - step, at + step) if 0 <= w < W]
            if relayed and 0 < at < W - 1:
                seen = [at - 1, at + 2, at + 1] if at < W // 2 else [at + 1, at - 2, at - 1]
            table_of.append(seen[i])
        w = jnp.int32(table_of[0])
        for at in range(1, W):
            w = jnp.where(z == at, table_of[at], w)
        return w

    relayed_of = (False, relays, relays, relays)
    first_stage = FIRST_STAGE if B > 2 else (0, 0, 0, 0)
    arrivals_of = [[arrival(i, relayed) for i in range(W - 1)] for relayed in relayed_of]
    arrivals = arrivals_of[0]

    def each_direct(action, relayed=relays):
        for step in range(1, W):
            to = lax.rem(z + step, W)
            later = (z + to == W - 1) if relayed else jnp.bool_(False)

            @pl.when(jnp.logical_not(later))
            def _():
                action(to)

    def weight_line(k, w, to, relayed=False):
        rows = plane.block(order_of(k, w), first_stage[k])
        slot = w if relayed else to
        return remote(
            weights[k].at[w, rows], weights[k].at[w, rows], zw_send.at[k, slot, int(relayed)], zw_recv.at[k, w], (c, to)
        )

    def weight_first(k):
        each_direct(lambda to: weight_line(k, z, to).start(), relayed_of[k])

    def weight_copy(k, w, j, s, landing=False):
        order = order_of(k, w)
        device = plane.partner(order, s)
        seen = device if landing else None
        if j < 0:
            rows = plane.block(order, first_stage[k], device=seen)
        else:
            rows = plane.block(order, j, other=True, device=seen)
        at = s * (s + 1) // 2 + j + 1
        block = weights[k].at[w, rows]
        return remote(block, block, pw_send.at[k, w, at], pw_recv.at[k, w, at], (device, z))

    def held_at(k, s):
        return [-1, *range(first_stage[k], s)] if s >= first_stage[k] else []

    def weight_event(k, i, s):
        w = arrivals_of[k][i]
        if s == 0:
            weight_line(k, w, lax.rem(z + 1, W)).wait_recv()
            if i == 1 and relayed_of[k]:

                @pl.when(inner)
                def _():
                    weight_line(k, w, end, True).start()
                    weight_line(k, z, beside).start()

            for later in range(first_stage[k], B):
                weight_copy(k, w, -1, later).start()
        else:
            for j in held_at(k, s - 1):
                weight_copy(k, w, j, s - 1, True).wait_recv()
            if s > first_stage[k]:
                for later in range(s, B):
                    weight_copy(k, w, s - 1, later).start()

    def weight_drain(k):
        each_direct(lambda to: weight_line(k, z, to).wait_send(), relayed_of[k])
        if relayed_of[k]:

            @pl.when(inner)
            def _():
                weight_line(k, across, end, True).wait_send()
                weight_line(k, z, beside).wait_send()

        for w in arrivals:
            for s in range(B):
                for j in held_at(k, s):
                    weight_copy(k, w, j, s).wait_send()

    def extra_copy(step):
        to = lax.rem(z + step, W)
        return remote(extra.at[z], extra.at[z], ex_send.at[step], ex_recv.at[step], (c, to))

    def extra_from(step):
        source = lax.rem(z + W - step, W)
        return remote(extra.at[source], extra.at[source], ex_send.at[step], ex_recv.at[step], (c, source))

    def halo(w, back):
        if back:
            return remote(near_give.at[w], near_back.at[w], back_send.at[w], back_recv.at[w], (c - 1, z))
        return remote(near_send.at[w], near_in.at[w], halo_send.at[w], halo_recv.at[w], (c + 1, z))

    def needs(source, target):
        need = jnp.bool_(False)
        for step in range(geo.far):
            size = 2 ** (step + 1)
            need = need | (target // size == source // size + 1)
        return need

    def far_copy(w, device, source):
        return remote(far_send.at[w], far_in.at[source, w], far_s.at[device, w], far_r.at[source, w], (device, z))

    def give_copy(w, device, source):
        return remote(
            far_give.at[device, w], far_back.at[source, w], farb_s.at[device, w], farb_r.at[source, w], (device, z)
        )

    def each_after(action):
        for step in range(1, C):
            device = jnp.minimum(c + step, C - 1)

            @pl.when((c + step < C) & needs(c, device))
            def _():
                action(device)

    def each_before(action):
        for step in range(1, C):
            device = jnp.maximum(c - step, 0)

            @pl.when((c - step >= 0) & needs(device, c))
            def _():
                action(device)

    def halo_start(w):
        @pl.when(c < C - 1)
        def _():
            halo(w, False).start()

        each_after(lambda device: far_copy(w, device, c).start())

    def halo_wait(w):
        @pl.when(c > 0)
        def _():
            halo(w, False).wait_recv()

        each_before(lambda device: far_copy(w, device, device).wait_recv())

    def give_start(w):
        @pl.when(c > 0)
        def _():
            halo(w, True).start()

        each_before(lambda device: give_copy(w, device, c).start())

    def give_wait(w):
        @pl.when(c < C - 1)
        def _():
            halo(w, True).wait_recv()

        each_after(lambda device: give_copy(w, device, device).wait_recv())

    def row_copy(part, w, to, relayed=False):
        rows = (gathered, source_all)[part // 2].at[w, pl.ds(part % 2 * geo.tile, geo.tile)]
        slot = w if relayed else to
        return remote(rows, rows, out_send.at[part, slot, int(relayed)], out_recv.at[part, w], (c, to))

    def each_beside(action):
        for step in range(1, W):
            to = lax.rem(z + step, W)
            if relays:
                skip = (z + to == W - 1) & jnp.logical_not(inner) | inner & (to == across)
            else:
                skip = jnp.bool_(False)

            @pl.when(jnp.logical_not(skip))
            def _():
                action(to)

    def rows_first(part):
        each_beside(lambda to: row_copy(part, z, to).start())

    def rows_relay(part, far):
        w = across if far else beside

        @pl.when(inner)
        def _():
            row_copy(part, w, end).wait_recv()
            row_copy(part, w, end, True).start()

    def rows_wait(part):
        for step in range(1, W):
            w = lax.rem(z + step, W)

            @pl.when(jnp.logical_not(inner) | (w == end))
            def _():
                row_copy(part, w, w).wait_recv()

    def rows_drain(part):
        each_beside(lambda to: row_copy(part, z, to).wait_send())

        @pl.when(inner)
        def _():
            row_copy(part, across, end, True).wait_send()
            row_copy(part, beside, end, True).wait_send()

    def reduce_copy(k, w, s):
        order = order_of(k, w)
        return remote(
            grads[k].at[w, plane.block(order, s, other=True)],
            landings[4 * s + k].at[w],
            rs_send.at[k, w, s],
            rs_recv.at[k, w, s],
            (plane.partner(order, s), z),
        )

    def reduce_add(k, w, s):
        reduce_copy(k, w, s).wait_recv()
        rows = plane.block(order_of(k, w), s)
        grads[k][w, rows] = (grads[k][w, rows].astype(F32) + landings[4 * s + k][w].astype(F32)).astype(BF16)
        if s > 0:
            reduce_copy(k, w, s - 1).start()
        else:
            line_send(k, w)

    def line_copy(k, w, way=None):
        rows = plane.block(order_of(k, w), 0)
        if way == "end":
            return remote(grads[k].at[w, rows], from_end[k], zl_send.at[k, w], zx_recv.at[k], (c, near_inner))
        if way == "inner":
            return remote(grads[k].at[w, rows], from_inner[k], zl_send.at[k, w], zy_recv.at[k], (c, beside))
        return remote(grads[k].at[w, rows], from_line[k].at[z], zl_send.at[k, w], zl_recv.at[k, z], (c, w))

    def line_send(k, w):
        over = jnp.logical_not(inner) & (w == beside) if relays else jnp.bool_(False)
        waits = inner & ((w == across) | (w == end))

        @pl.when(over)
        def _():
            line_copy(k, w, "end").start()

        @pl.when((w != z) & jnp.logical_not(over | waits))
        def _():
            line_copy(k, w).start()

    def line_add(k, w, landed):
        rows = plane.block(order_of(k, w), 0)
        grads[k][w, rows] = (grads[k][w, rows].astype(F32) + landed[k][...].astype(F32)).astype(BF16)

    def line_over(k):
        @pl.when(inner)
        def _():
            line_copy(k, across, "end").wait_recv()
            line_add(k, across, from_end)
            line_copy(k, across, "inner").start()

    def line_pass(k):
        @pl.when(inner)
        def _():
            line_copy(k, across, "inner").wait_recv()
            line_add(k, end, from_inner)
            line_copy(k, end).start()

    def line_drain(k, w):
        @pl.when(w != z)
        def _():
            line_copy(k, w).wait_send()

    def own_rows(k):
        return plane.block(order_of(k, z), 0)

    def line_end(k):
        rows = own_rows(k)
        total_now = grads[k][z, rows].astype(F32)
        for step in range(1, W):
            source = lax.rem(z + step, W)
            block = from_line[k].at[source]
            comes = inner | (source == near_inner) if relays else jnp.bool_(True)

            @pl.when(comes)
            def _():
                remote(block, block, zl_send.at[k, source], zl_recv.at[k, source], (c, source)).wait_recv()

            total_now = total_now + jnp.where(comes, from_line[k][source].astype(F32), 0.0)
        reduced[k][rows] = total_now.astype(BF16)

    def gather_copy(k, j, s):
        order = order_of(k, z)
        rows = plane.block(order, 0) if j < 0 else plane.block(order, j, other=True)
        at = s * (s + 1) // 2 + j + 1
        block = reduced[k].at[rows]
        return remote(block, block, ag_send.at[k, at], ag_recv.at[k, at], (plane.partner(order, s), z))

    def gather_landing(k, j, s):
        order = order_of(k, z)
        device = plane.partner(order, s)
        rows = plane.block(order, 0, device=device) if j < 0 else plane.block(order, j, other=True, device=device)
        at = s * (s + 1) // 2 + j + 1
        block = reduced[k].at[rows]
        return remote(block, block, ag_send.at[k, at], ag_recv.at[k, at], (device, z))

    def gather_event(k, s):
        if s > 0:
            for j in range(-1, s - 1):
                gather_landing(k, j, s - 1).wait_recv()
        for later in range(s, B):
            gather_copy(k, s - 1, later).start()

    def gather_drain(k):
        for s in range(B):
            for j in range(-1, s):
                gather_copy(k, j, s).wait_send()

    held = {}
    shard_of = [z] + arrivals
    feed_of = [z] + arrivals_of[2]
    turn = [w for step in range((W + 1) // 2) for w in dict.fromkeys((step, W - 1 - step))]

    def send_shards(k):
        for at in {1: (4,), 2: (5,)}.get(k, ()):
            loads[at].wait()
        weight_first(k)

    def send_biases():
        for step in range(1, W):
            extra_copy(step).start()

    def wait_biases():
        for step in range(1, W):
            extra_from(step).wait_recv()

    def first_norm():
        loads[6].wait()
        normed, _ = norm_parts(x[...].astype(F32))
        n1[...] = (normed * n1g[...] + n1b[...]).astype(BF16)

    def masks():
        bias[0] = mask_bias(geo, c, segs[pl.ds(z, 1), :], 0)
        bias[1] = mask_bias(geo, c, segs[pl.ds(z, 1), :], 1)
        held["pick"] = far_matrix(geo, c)

    def projection(i):
        w = shard_of[i]
        project(w, n1, weights, extra, q, own, cells, near_send, far_send)
        halo_start(w)

    def attention(i):
        w = shard_of[i]
        halo_wait(w)
        tables(geo, w, held["pick"], own, cells, near_in, far_in, table)
        for tile in (0, 1):
            attend(geo, w, tile, q, table, bias, probs, mixed)

    def event(k, i, s):
        for stage in {0: [0], 1: [1], 2: range(2, B), 3: [B]}[s]:
            weight_event(k, i, stage)

    def second_norm():
        loads[7].wait()
        acc = x[...].astype(F32) + out_bias[...]
        for w in range(W):
            acc = acc + dot_nt(mixed[w], weights[3][w])
        middle[...] = acc
        normed, _ = norm_parts(acc)
        n2[...] = (normed * n2g[...] + n2b[...]).astype(BF16)
        result[...] = acc + down_bias[...]

    def forth(i):
        feed(feed_of[i], n2, weights, extra, hidden, slope, result)

    def layer_rows():
        gathered[z] = result[...].astype(BF16)

    def back(i):
        first = "total" not in held
        held["total"] = True
        feed_back(first, feed_of[i], g2, weights, n2, hidden, slope, sums, grads, total)

    def shard(k, i):
        return feed_of[i] if k in (1, 2) else turn[i]

    def halve(k, i):
        reduce_copy(k, shard(k, i), B - 1).start()

    def add(k, i, s):
        for stage in {2: [B - 1], 1: range(B - 2, 0, -1), 0: [0]}[s]:
            reduce_add(k, shard(k, i), stage)

    def second_back():
        hat, inverse = norm_parts(middle[...])
        d_normed = total[...]
        wide = g2[...].astype(F32)
        first = wide + norm_backward(d_normed, hat, inverse, n2g[...])
        g1[...] = first
        g1_low[...] = first.astype(BF16)
        put_sums(geo, sums, 2, jnp.sum(first, axis=0, keepdims=True))
        put_sums(geo, sums, 3, jnp.sum(d_normed * hat, axis=0, keepdims=True))
        put_sums(geo, sums, 4, jnp.sum(d_normed, axis=0, keepdims=True))
        put_sums(geo, sums, 5, jnp.sum(wide, axis=0, keepdims=True))
        del held["total"]

    def out_back(i):
        w = turn[i]
        d_mixed[w] = dot_nn(g1_low[...], weights[3][w]).astype(BF16)
        grads[3][w] = dot_tn(g1_low[...], mixed[w]).astype(BF16)

    def give(i):
        w = turn[i]
        for tile in (0, 1):
            attend_back(geo, w, tile, q, table, probs, d_mixed, d_queries, d_table)
        return_cells(geo, w, held["pick"], d_table, near_give, far_give)
        give_start(w)

    def take(i):
        w = turn[i]
        give_wait(w)
        first = "total" not in held
        held["total"] = True
        project_back(geo, first, w, weights, n1, d_queries, d_table, near_back, far_back, sums, grads, total)

    def source():
        normed, inverse = norm_parts(x[...].astype(F32))
        d_normed = total[...]
        source_all[z] = (g1[...] + norm_backward(d_normed, normed, inverse, n1g[...])).astype(BF16)
        put_sums(geo, sums, 0, jnp.sum(d_normed * normed, axis=0, keepdims=True))
        put_sums(geo, sums, 1, jnp.sum(d_normed, axis=0, keepdims=True))

    def sums_copy(step):
        to = lax.rem(z + step, W)
        return remote(sums.at[to], sums_in.at[step], sm_send.at[step], sm_recv.at[step], (c, to))

    def sums_stage(s):
        return remote(sums_all.at[s], sums_got.at[s], sc_send.at[s], sc_recv.at[s], (plane.flip(1 << s), z))

    def send_sums():
        for step in range(1, W):
            sums_copy(step).start()

    def add_sums(s):
        if s == 0:
            total_sums = sums[z]
            for step in range(1, W):
                sums_copy(step).wait_recv()
                total_sums = total_sums + sums_in[step]
            sums_all[0] = total_sums
            sums_stage(0).start()
        for stage in {0: [], 1: [0], 2: range(1, B - 1), 3: [B - 1]}[s]:
            sums_stage(stage).wait_recv()
            sums_all[stage + 1] = sums_all[stage] + sums_got[stage]
            if stage + 1 < B:
                sums_stage(stage + 1).start()

    def gather(k, s):
        for stage in {0: [0], 1: [1], 2: range(2, B), 3: [B]}[s]:
            gather_event(k, stage)

    stores = [
        pltpu.make_async_copy(gathered, out_result, store_sem.at[0]),
        pltpu.make_async_copy(source_all, out_source, store_sem.at[1]),
        pltpu.make_async_copy(sums_all.at[B], out_sums, store_sem.at[2]),
        pltpu.make_async_copy(r_a, out_a, store_sem.at[3]),
        pltpu.make_async_copy(r_u, out_u, store_sem.at[4]),
        pltpu.make_async_copy(r_d, out_d, store_sem.at[5]),
        pltpu.make_async_copy(r_o, out_o, store_sem.at[6]),
    ]

    def store(i):
        stores[i].start()

    steps = {
        step.__name__: step
        for step in (
            send_shards, send_biases, wait_biases, first_norm, masks, projection, attention, event, second_norm, forth,
            layer_rows, back, halve, add, second_back, out_back, give, take, source, send_sums, add_sums, gather, store,
            rows_first, rows_relay, rows_wait, line_over, line_pass, line_end,
        )
    }
    for name, *args in SCHEDULE:
        steps[name](*args)

    for k in range(4):
        weight_drain(k)
        for w in range(W):
            for s in range(B):
                reduce_copy(k, w, s).wait_send()
            line_drain(k, w)
        gather_drain(k)
    for part in range(4):
        rows_drain(part)
    for step in range(1, W):
        extra_copy(step).wait_send()
        sums_copy(step).wait_send()
    for s in range(B):
        sums_stage(s).wait_send()

    for w in range(W):

        @pl.when(c < C - 1)
        def _():
            halo(w, False).wait_send()

        @pl.when(c > 0)
        def _():
            halo(w, True).wait_send()

        each_after(lambda device: far_copy(w, device, c).wait_send())
        each_before(lambda device: give_copy(w, device, c).wait_send())
    for copy in stores:
        copy.wait()


def unpack(result, source, grads_a, grads_u, grads_d, grads_o, sums, *outs):
    (
        layer_out, input_grad, d_n1g, d_n1b, d_q, d_qb, d_k, d_v, d_vb, d_o, d_ob, d_n2g, d_n2b, d_up, d_upb, d_down, d_db,
    ) = outs
    layer_out[...] = result[...].astype(F32)
    input_grad[...] = source[...].astype(F32)
    d_q[...] = grads_a[:, :LANES].astype(F32)
    d_k[...] = grads_a[:, LANES : 2 * LANES].astype(F32)
    d_v[...] = grads_a[:, 2 * LANES :].astype(F32)
    d_o[...] = grads_o[...].astype(F32).T
    d_up[...] = grads_u[...].astype(F32)
    d_down[...] = grads_d[...].astype(F32)
    for at, out in enumerate((d_n1g, d_n1b, d_ob, d_n2g, d_n2b, d_db)):
        row, lane = 2 + at // 4, at % 4 * LANES
        out[...] = sums[row : row + 1, lane : lane + LANES]
    d_qb[...] = sums[1:2, :LANES]
    d_vb[...] = sums[1:2, LANES : 2 * LANES]
    d_upb[...] = sums[0:1, :]


def shards(
    x_in,
    grad_out,
    seg_ids,
    norm1_gain,
    norm1_bias,
    q_weight,
    q_bias,
    k_weight,
    v_weight,
    v_bias,
    out_weight,
    out_bias,
    norm2_gain,
    norm2_bias,
    up_weight,
    up_bias,
    down_weight,
    down_bias,
):
    C, W = lax.axis_size("ctx"), lax.axis_size("wt")
    runs, T, width = x_in.shape
    hidden = up_weight.shape[1]
    geo = Geometry(C, W, T)
    S, B = geo.slots, C.bit_length() - 1
    each = width // C
    assert runs == W and hidden == width and q_weight.shape[1] == LANES and T == 256
    sds = jax.ShapeDtypeStruct
    vmem, dma = pltpu.VMEM, pltpu.SemaphoreType.DMA
    row = lambda v: v.reshape(1, -1)
    pair = 2 * LANES
    wide_of = (3 * LANES, hidden, width, LANES)
    scratch = [
        *[vmem((W, width, n), BF16) for n in wide_of],
        vmem((W, 8, width), F32),
        vmem((T, width), BF16),
        vmem((T, width), BF16),
        vmem((LANES, width), BF16),
        vmem((T, width), BF16),
        vmem((W, T, LANES), BF16),
        vmem((W, T, pair), BF16),
        vmem((W, 224, pair), BF16),
        vmem((W, 80, pair), BF16),
        vmem((W, 16, pair), BF16),
        vmem((W, 80, pair), BF16),
        vmem((C, W, 16, pair), BF16),
        vmem((W, 2, S, pair), BF16),
        vmem((2, S, geo.tile), F32),
        vmem((W, 2, S, pair), BF16),
        vmem((W, T, LANES), BF16),
        vmem((T, width), F32),
        vmem((T, width), BF16),
        vmem((W, T, hidden), BF16),
        vmem((W, T, hidden), F32),
        vmem((T, width), F32),
        vmem((T, width), F32),
        vmem((T, width), F32),
        vmem((W, T, LANES), BF16),
        vmem((W, T, LANES), BF16),
        vmem((W, 2, S, pair), F32),
        vmem((T, width), BF16),
        vmem((W, 80, pair), BF16),
        vmem((C, W, 16, pair), BF16),
        vmem((W, 80, pair), BF16),
        vmem((C, W, 16, pair), BF16),
        *[vmem((W, width, n), BF16) for n in wide_of],
        vmem((W, 8, width), F32),
        vmem((W, T, width), BF16),
        vmem((W, T, width), BF16),
        *[vmem((W, each, n), BF16) for n in wide_of],
        *[vmem((each, n), BF16) for n in wide_of],
        *[vmem((each, n), BF16) for n in wide_of],
        *[vmem((width, n), BF16) for n in wide_of],
        vmem((W, 8, width), F32),
        vmem((B + 1, 8, width), F32),
        vmem((B, 8, width), F32),
        dma((8,)),
        dma((7,)),
        dma((4, W, 2)),
        dma((4, W)),
        dma((4, W, B * (B + 1) // 2)),
        dma((4, W, B * (B + 1) // 2)),
        dma((W,)),
        dma((W,)),
        dma((W,)),
        dma((W,)),
        dma((C, W)),
        dma((C, W)),
        dma((W,)),
        dma((W,)),
        dma((C, W)),
        dma((C, W)),
        dma((4, W, B)),
        dma((4, W, B)),
        dma((4, W)),
        dma((4, W)),
        dma((4,)),
        dma((4,)),
        dma((4, B * (B + 1) // 2)),
        dma((4, B * (B + 1) // 2)),
        dma((4, W, 2)),
        dma((4, W)),
        dma((W,)),
        dma((W,)),
        dma((B,)),
        dma((B,)),
    ] + [vmem((W, each * 2**s, n), BF16) for s in range(B) for n in wide_of]
    far, near = pl.BlockSpec(memory_space=pl.ANY), pl.BlockSpec(memory_space=pltpu.VMEM)
    result, source, d_a, d_u, d_d, d_o, sums = pl.pallas_call(
        functools.partial(fused, geo),
        name="fused",
        out_shape=[sds((W, T, width), BF16), sds((W, T, width), BF16), *[sds((width, n), BF16) for n in wide_of], sds((8, width), F32)],
        in_specs=[far, far, near, near, near, far, near, far, far, near, far, near, near, near, far, near, far, near],
        out_specs=[far] * 7,
        scratch_shapes=scratch,
        compiler_params=pltpu.CompilerParams(collective_id=0, has_side_effects=True, vmem_limit_bytes=58 * 2**20),
    )(
        x_in, grad_out, seg_ids, row(norm1_gain), row(norm1_bias), q_weight, row(q_bias), k_weight, v_weight, row(v_bias),
        out_weight, row(out_bias), row(norm2_gain), row(norm2_bias), up_weight, row(up_bias), down_weight, row(down_bias),
    )
    part, half = width // 2, W // 2
    rows = lambda shape: pl.BlockSpec(shape, lambda i: (i, 0))
    still = lambda shape: pl.BlockSpec(shape, lambda i: (0, 0))
    one, wide = (sds((1, LANES), F32), still((1, LANES))), (sds((1, hidden), F32), still((1, hidden)))
    blocks = (sds((W, T, width), F32), pl.BlockSpec((half, T, width), lambda i: (i, 0, 0)))
    thin = (sds((width, LANES), F32), rows((part, LANES)))
    full = (sds((width, width), F32), rows((part, width)))
    turned = (sds((LANES, width), F32), pl.BlockSpec((LANES, part), lambda i: (0, i)))
    outs = [blocks, blocks, one, one, thin, one, thin, thin, one, turned, one, one, one, full, wide, full, one]
    values = pl.pallas_call(
        unpack,
        name="unpack",
        grid=(2,),
        out_shape=[o[0] for o in outs],
        in_specs=[blocks[1], blocks[1], *[rows((part, n)) for n in wide_of], still((8, width))],
        out_specs=[o[1] for o in outs],
    )(result, source, d_a, d_u, d_d, d_o, sums)
    return tuple(v.reshape(-1) if v.shape[0] == 1 else v for v in values)


def solution(mesh):
    in_specs = (
        P(None, "ctx", None),
        P(None, "ctx", None),
        P(),
        P(),
        P(),
        P(None, "wt"),
        P("wt"),
        P(None, "wt"),
        P(None, "wt"),
        P("wt"),
        P("wt", None),
        P(),
        P(),
        P(),
        P(None, "wt"),
        P("wt"),
        P("wt", None),
        P(),
    )
    out_specs = (
        P(None, "ctx", None),
        P(None, "ctx", None),
        P("wt"),
        P("wt"),
        P(None, "wt"),
        P("wt"),
        P(None, "wt"),
        P(None, "wt"),
        P("wt"),
        P("wt", None),
        P("wt"),
        P("wt"),
        P("wt"),
        P(None, "wt"),
        P("wt"),
        P("wt", None),
        P("wt"),
    )
    return jax.shard_map(shards, mesh=mesh, in_specs=in_specs, out_specs=out_specs, check_vma=False)
```

```python
import functools

import jax
import jax.numpy as jnp
from jax import lax
from jax.experimental import pallas as pl
from jax.experimental.pallas import tpu as pltpu
from jax.sharding import PartitionSpec as P

HEAD_DIM = 64
BLOCK = 16
LEVELS = 10
FINE = 3
EPSILON = 1e-05
NEGATIVE = -1e30
LOG_TWO = 0.6931471805599453
LANES = 128
BF16 = jnp.bfloat16
F32 = jnp.float32


def dot(left, right, dims):
    return lax.dot_general(left, right, (dims, ((), ())), preferred_element_type=F32)


def dot_nn(left, right):
    return dot(left, right, ((1,), (0,)))


def dot_nt(left, right):
    return dot(left, right, ((1,), (1,)))


def dot_tn(left, right):
    return dot(left, right, ((0,), (0,)))


def norm_parts(source):
    centre = jnp.mean(source, axis=-1, keepdims=True)
    centred = source - centre
    variance = jnp.mean(centred * centred, axis=-1, keepdims=True)
    inverse = lax.rsqrt(variance + EPSILON)
    return centred * inverse, inverse


def norm_backward(upstream, normed, inverse, gain):
    scaled = upstream * gain
    first_mean = jnp.mean(scaled, axis=-1, keepdims=True)
    second_mean = jnp.mean(scaled * normed, axis=-1, keepdims=True)
    return inverse * (scaled - first_mean - normed * second_mean)


def iota(shape, axis):
    return lax.broadcasted_iota(jnp.int32, shape, axis)


class Geometry:
    def __init__(self, ctx, wt, tok_dev):
        self.ctx, self.wt, self.tok_dev = ctx, wt, tok_dev
        tokens = ctx * tok_dev
        self.levels = len([l for l in range(LEVELS) if BLOCK * 2**l < tokens])
        self.own_cells = [tok_dev // 2**l if l <= FINE else 0 for l in range(self.levels)]
        self.tile = tok_dev // 2
        self.tile_slots = [BLOCK + self.tile] + [BLOCK * 4 >> (l - 1) if l < FINE else BLOCK for l in range(1, self.levels)]
        self.slots = sum(self.tile_slots)
        self.slot_at = [sum(self.tile_slots[:l]) for l in range(self.levels + 1)]
        self.far = self.levels - (FINE + 2)
        self.near = FINE + 2


def pool_matrix():
    parts = []
    for level, count in ((1, 128), (2, 64), (3, 32)):
        hit = (iota((count, 256), 1) >> level) == iota((count, 256), 0)
        parts.append(jnp.where(hit, 1.0 / 2**level, 0.0))
    return jnp.concatenate(parts, axis=0).astype(BF16)


def coarse_matrix():
    row, column = iota((32, 32), 0), iota((32, 32), 1)
    out = jnp.zeros((32, 32), F32)
    first = 0
    for level, count in ((4, 16), (5, 8), (6, 4), (7, 2), (8, 1)):
        up = level - FINE
        hit = (row >= first) & (row < first + count) & ((column >> up) == row - first)
        out = jnp.where(hit, 1.0 / 2**up, out)
        first += count
    return out.astype(BF16)


def far_matrix(geo, me):
    parts = []
    first = 0
    for step in range(geo.far):
        up = step + 1
        each = BLOCK >> up
        row, column = iota((BLOCK, geo.ctx * BLOCK), 0), iota((BLOCK, geo.ctx * BLOCK), 1)
        group = (me >> up) - 1
        device = (group << up) + (row >> (4 - up))
        wanted = device * BLOCK + first + (row & (each - 1))
        parts.append(jnp.where((column == wanted) & (group >= 0), 1.0, 0.0))
        first += each
    return jnp.concatenate(parts, axis=0).astype(BF16)


def mask_bias(geo, me, segs, tile):
    first_pos = me * geo.tok_dev + tile * geo.tile
    seg_one = jnp.sum((segs < 1).astype(jnp.int32), axis=1, keepdims=True)
    seg_two = jnp.sum((segs < 2).astype(jnp.int32), axis=1, keepdims=True)
    position = first_pos + iota((1, geo.tile), 1)
    begins = jnp.where(position >= seg_two, seg_two, jnp.where(position >= seg_one, seg_one, 0))
    parts = []
    for level in range(geo.levels):
        size, shift = 2**level, level + 4
        count = geo.tile_slots[level]
        span = BLOCK * size
        if level <= FINE:
            base = first_pos - span
        else:
            base = (((me * geo.tok_dev) >> shift) - 1) << shift
        begin = base + size * iota((count, geo.tile), 0)
        lower = jnp.maximum(((position >> shift) - 1) << shift, begins)
        if level == 0:
            upper = position + 1
        else:
            upper = ((position >> (shift - 1)) - 1) << (shift - 1)
        valid = (begin >= lower) & (begin + size <= upper)
        parts.append(jnp.where(valid, level * LOG_TWO, NEGATIVE))
    return jnp.concatenate(parts, axis=0)


def both_heads(pair):
    lane = iota(pair.shape, 1)
    zero = jnp.zeros_like(pair)
    return jnp.concatenate([jnp.where(lane < HEAD_DIM, pair, zero), jnp.where(lane >= HEAD_DIM, pair, zero)], axis=0)


def own_lanes(stacked):
    rows = stacked.shape[0] // 2
    lane = iota((rows, stacked.shape[1]), 1)
    return jnp.where(lane < HEAD_DIM, stacked[:rows], stacked[rows:])


def project(w, n1, weights, extra, q, own, cells, near, far):
    out = dot_nn(n1[...], weights[0][w])
    bias = extra[w, 1:2, :]
    q[w] = ((out[:, :LANES] + bias[:, :LANES]).astype(BF16) * 0.125).astype(BF16)
    kv = jnp.concatenate(
        [out[:, LANES : 2 * LANES], out[:, 2 * LANES :] + bias[:, LANES : 2 * LANES]], axis=1
    ).astype(BF16)
    own[w] = kv
    fine = dot_nn(pool_matrix(), kv).astype(BF16)
    cells[w] = fine
    rough = dot_nn(coarse_matrix(), fine[192:224]).astype(BF16)
    near[w, 0:16] = kv[240:256]
    near[w, 16:32] = fine[112:128]
    near[w, 32:48] = fine[176:192]
    near[w, 48:64] = fine[208:224]
    near[w, 64:80] = rough[0:16]
    far[w] = rough[16:32]


def tables(geo, w, pick, own, cells, near_in, far_in, table):
    blocks = far_in[:, w].reshape(geo.ctx * BLOCK, 2 * LANES)
    rough = dot_nn(pick, blocks).astype(BF16)
    at = geo.slot_at
    table[w, 0, 0:16] = near_in[w, 0:16]
    table[w, 0, 16:144] = own[w, 0:128]
    table[w, 1, 0:144] = own[w, 112:256]
    table[w, 0, at[1] : at[1] + 16] = near_in[w, 16:32]
    table[w, 0, at[1] + 16 : at[2]] = cells[w, 0:48]
    table[w, 1, at[1] : at[2]] = cells[w, 48:112]
    table[w, 0, at[2] : at[2] + 16] = near_in[w, 32:48]
    table[w, 0, at[2] + 16 : at[3]] = cells[w, 128:144]
    table[w, 1, at[2] : at[3]] = cells[w, 144:176]
    table[w, 0, at[3] : at[4]] = near_in[w, 48:64]
    table[w, 1, at[3] : at[4]] = cells[w, 192:208]
    for tile in (0, 1):
        table[w, tile, at[4] : at[5]] = near_in[w, 64:80]
        table[w, tile, at[5] :] = rough


def attend(geo, w, tile, q, table, bias, probs, mixed):
    rows = slice(tile * geo.tile, (tile + 1) * geo.tile)
    both = both_heads(q[w, rows, :])
    level_bias = bias[tile]
    scores = dot_nt(table[w, tile, :, :LANES], both)
    scores = scores + jnp.concatenate([level_bias, level_bias], axis=1)
    top = jnp.max(scores, axis=0, keepdims=True)
    exponent = jnp.exp(scores - top)
    total = jnp.sum(exponent, axis=0, keepdims=True)
    low = (exponent * (1.0 / total)).astype(BF16)
    probs[w, tile] = low
    mixed[w, rows, :] = own_lanes(dot_tn(low, table[w, tile, :, LANES:])).astype(BF16)


def attend_back(geo, w, tile, q, table, probs, d_mixed, d_queries, d_table):
    rows = slice(tile * geo.tile, (tile + 1) * geo.tile)
    both = both_heads(q[w, rows, :])
    d_both = both_heads(d_mixed[w, rows, :])
    low = probs[w, tile]
    d_probs = dot_nt(table[w, tile, :, LANES:], d_both)
    wide = low.astype(F32)
    product = wide * d_probs
    centre = jnp.sum(product, axis=0, keepdims=True)
    d_scores = (product - wide * centre).astype(BF16)
    d_table[w, tile, :, :LANES] = dot_nn(d_scores, both)
    d_table[w, tile, :, LANES:] = dot_nn(low, d_both)
    back = own_lanes(dot_tn(d_scores, table[w, tile, :, :LANES]))
    d_queries[w, rows, :] = (back * 0.125).astype(BF16)


def return_cells(geo, w, pick, d_table, near, far):
    at = geo.slot_at
    near[w, 0:16] = d_table[w, 0, 0:16].astype(BF16)
    near[w, 16:32] = d_table[w, 0, at[1] : at[1] + 16].astype(BF16)
    near[w, 32:48] = d_table[w, 0, at[2] : at[2] + 16].astype(BF16)
    near[w, 48:64] = d_table[w, 0, at[3] : at[4]].astype(BF16)
    near[w, 64:80] = (d_table[w, 0, at[4] : at[5]] + d_table[w, 1, at[4] : at[5]]).astype(BF16)
    rough = (d_table[w, 0, at[5] :] + d_table[w, 1, at[5] :]).astype(BF16)
    far[:, w] = dot_tn(pick, rough).astype(BF16).reshape(geo.ctx, BLOCK, 2 * LANES)


def own_gradients(geo, w, d_table, near_back, far_back):
    at = geo.slot_at
    first, second = d_table.at[w, 0], d_table.at[w, 1]
    back = near_back[w].astype(F32)
    tokens = jnp.concatenate(
        [first[16:128], first[128:144] + second[0:16], second[16:128], second[128:144] + back[0:16]], axis=0
    )
    far = jnp.sum(far_back[:, w].astype(F32), axis=0)
    rough = jnp.concatenate([back[64:80], far], axis=0)
    fine = dot_tn(coarse_matrix(), rough.astype(BF16))
    level3 = jnp.concatenate([second[at[3] : at[4]], back[48:64]], axis=0) + fine
    cells = jnp.concatenate(
        [
            first[at[1] + 16 : at[2]],
            second[at[1] : at[2]],
            back[16:32],
            first[at[2] + 16 : at[3]],
            second[at[2] : at[3]],
            back[32:48],
            level3,
        ],
        axis=0,
    )
    return tokens + dot_tn(pool_matrix(), cells.astype(BF16))


def feed(w, n2, weights, extra, hidden, slope, result):
    pre = dot_nn(n2[...], weights[1][w]) + extra[w, 0:1, :]
    gate = jax.nn.sigmoid(pre)
    hidden[w] = (pre * gate).astype(BF16)
    slope[w] = gate * (1.0 + pre * (1.0 - gate))
    result[...] += dot_nn(hidden[w], weights[2][w])


def feed_back(first, w, g2, weights, n2, hidden, slope, sums, grads, total):
    d_hidden = dot_nt(g2[...], weights[2][w]).astype(BF16).astype(F32)
    d_up = (d_hidden * slope[w]).astype(BF16)
    sums[w, 0:1, :] = jnp.sum(d_up.astype(F32), axis=0, keepdims=True)
    grads[2][w] = dot_tn(hidden[w], g2[...]).astype(BF16)
    grads[1][w] = dot_tn(n2[...], d_up).astype(BF16)
    part = dot_nt(d_up, weights[1][w])
    total[...] = part if first else total[...] + part


def put_sums(geo, sums, column, row):
    at, lanes = 2 + column // 4, slice(column % 4 * LANES, (column % 4 + 1) * LANES)
    for w in range(geo.wt):
        sums[w, at : at + 1, lanes] = row[:, w * LANES : (w + 1) * LANES]


def project_back(geo, first, w, weights, n1, d_queries, d_table, near_back, far_back, sums, grads, total):
    kv = own_gradients(geo, w, d_table, near_back, far_back).astype(BF16)
    d_qkv = jnp.concatenate([d_queries[w], kv], axis=1)
    sums[w, 1:2, :LANES] = jnp.sum(d_qkv[:, :LANES].astype(F32), axis=0, keepdims=True)
    sums[w, 1:2, LANES : 2 * LANES] = jnp.sum(d_qkv[:, 2 * LANES :].astype(F32), axis=0, keepdims=True)
    grads[0][w] = dot_tn(n1[...], d_qkv).astype(BF16)
    part = dot_nt(d_qkv, weights[0][w])
    total[...] = part if first else total[...] + part


def remote(source, target, sent, landed, device):
    return pltpu.make_async_remote_copy(source, target, sent, landed, device_id=device, device_id_type=pl.DeviceIdType.MESH)


class Plane:
    def __init__(self, ctx, c, rows):
        self.ctx, self.c = ctx, c
        self.bits = ctx.bit_length() - 1
        self.each = rows // ctx
        plane_bits = self.bits - 1
        half = plane_bits // 2
        self.plane_bits, self.half = plane_bits, half
        self.places = self.places_of(c)
        self.masks = (
            [2 << s for s in range(plane_bits)] + [1],
            [2 << (s + half) % plane_bits for s in range(plane_bits)] + [1],
        )

    def places_of(self, device):
        plane, core = device // 2, device % 2
        turned = plane // 2**self.half + plane % 2**self.half * 2 ** (self.plane_bits - self.half)
        top = core * 2**self.plane_bits
        return plane + top, turned + top

    def place(self, order, device=None):
        places = self.places if device is None else self.places_of(device)
        if isinstance(order, int):
            return places[order]
        return jnp.where(order == 0, places[0], places[1])

    def partner(self, order, stage):
        if isinstance(order, int):
            return self.flip(self.masks[order][stage])
        return jnp.where(order == 0, self.flip(self.masks[0][stage]), self.flip(self.masks[1][stage]))

    def flip(self, mask):
        return self.c + mask * (1 - 2 * (self.c // mask % 2))

    def flips(self, bits):
        device = self.c
        for s in range(self.bits):
            if bits >> s & 1:
                device = device + (1 << s) * (1 - 2 * (self.c // (1 << s) % 2))
        return device

    def block(self, order, stage, other=False, device=None):
        index = self.place(order, device) // 2**stage
        if other:
            index = index + 1 - 2 * (index % 2)
        size = self.each * 2**stage
        return pl.ds(pl.multiple_of(index * size, size), size)


SCHEDULE = (
    ("send_shards", 0), ("send_shards", 1), ("first_norm",), ("event", 0, 1, 0), ("send_shards", 3), ("send_biases",),
    ("projection", 0), ("event", 1, 0, 0), ("event", 0, 0, 0), ("event", 1, 1, 0), ("event", 1, 0, 1),
    ("event", 0, 0, 1), ("masks",), ("send_shards", 2), ("event", 3, 0, 0), ("event", 3, 0, 1), ("event", 0, 2, 0),
    ("event", 1, 1, 1), ("event", 3, 1, 0), ("event", 1, 2, 0), ("attention", 0), ("event", 0, 1, 1),
    ("event", 0, 1, 2), ("event", 0, 2, 1), ("event", 3, 0, 2), ("event", 1, 2, 1), ("wait_biases",),
    ("event", 2, 0, 0), ("event", 0, 0, 2), ("event", 3, 2, 0), ("event", 0, 0, 3), ("projection", 1),
    ("event", 3, 2, 1), ("event", 2, 1, 0), ("event", 2, 1, 1), ("event", 0, 1, 3), ("event", 2, 0, 1),
    ("event", 0, 2, 2), ("event", 0, 2, 3), ("event", 3, 2, 2), ("projection", 3), ("event", 1, 0, 2),
    ("event", 1, 0, 3), ("projection", 2), ("event", 1, 1, 2), ("event", 3, 1, 1), ("event", 3, 1, 2),
    ("attention", 1), ("event", 3, 2, 3), ("event", 1, 1, 3), ("event", 3, 1, 3), ("event", 2, 2, 0),
    ("event", 3, 0, 3), ("event", 1, 2, 2), ("event", 2, 1, 2), ("attention", 3), ("event", 1, 2, 3),
    ("event", 2, 0, 2), ("attention", 2), ("second_norm",), ("forth", 0), ("event", 2, 1, 3), ("back", 0),
    ("halve", 1, 0), ("event", 2, 0, 3), ("forth", 1), ("halve", 2, 0), ("forth", 2), ("event", 2, 2, 1),
    ("event", 2, 2, 2), ("back", 2), ("halve", 2, 2), ("add", 1, 0, 2), ("back", 1), ("event", 2, 2, 3), ("forth", 3),
    ("layer_rows",), ("add", 2, 0, 2), ("rows_first", 0), ("back", 3), ("second_back",), ("out_back", 0),
    ("halve", 3, 0), ("out_back", 2), ("halve", 2, 3), ("give", 0), ("rows_first", 1), ("halve", 1, 3),
    ("out_back", 3), ("halve", 3, 3), ("give", 2), ("give", 3), ("halve", 1, 2), ("out_back", 1), ("give", 1),
    ("add", 3, 0, 2), ("add", 3, 3, 2), ("take", 0), ("add", 1, 2, 2), ("add", 1, 3, 2), ("rows_relay", 0, 0),
    ("add", 2, 2, 2), ("halve", 3, 2), ("take", 3), ("halve", 0, 3), ("add", 2, 3, 2), ("add", 2, 0, 1), ("take", 2),
    ("halve", 1, 1), ("halve", 2, 1), ("take", 1), ("halve", 3, 1), ("rows_relay", 0, 1), ("add", 3, 3, 1),
    ("source",), ("send_sums",), ("rows_first", 2), ("add", 1, 1, 2), ("halve", 0, 0), ("rows_relay", 1, 0),
    ("add", 3, 2, 2), ("add", 3, 0, 1), ("add", 1, 2, 1), ("add", 3, 1, 2), ("add", 1, 3, 1), ("add", 2, 3, 1),
    ("add", 2, 1, 2), ("halve", 0, 1), ("add", 0, 3, 2), ("add", 3, 0, 0), ("add", 0, 1, 2), ("add", 1, 2, 0),
    ("add", 1, 3, 0), ("add", 3, 2, 1), ("add", 3, 1, 1), ("rows_relay", 2, 0), ("add", 1, 0, 1), ("halve", 0, 2),
    ("add", 1, 1, 1), ("add", 2, 3, 0), ("add", 2, 1, 1), ("rows_relay", 1, 1), ("add", 3, 2, 0), ("add", 2, 2, 1),
    ("add", 0, 0, 2), ("add", 1, 0, 0), ("add", 3, 3, 0), ("add", 1, 1, 0), ("line_over", 1), ("add_sums", 0),
    ("add_sums", 1), ("add", 2, 0, 0), ("rows_relay", 2, 1), ("add", 2, 1, 0), ("add", 0, 3, 1), ("add", 0, 2, 2),
    ("add", 2, 2, 0), ("add", 3, 1, 0), ("line_over", 2), ("rows_wait", 1), ("add", 0, 0, 1), ("add", 0, 1, 1),
    ("line_pass", 1), ("rows_first", 3), ("line_pass", 2), ("add", 0, 2, 1), ("add_sums", 2), ("add_sums", 3),
    ("add", 0, 1, 0), ("add", 0, 0, 0), ("line_end", 1), ("gather", 1, 0), ("store", 2), ("line_end", 2),
    ("gather", 2, 0), ("line_end", 3), ("add", 0, 2, 0), ("gather", 3, 0), ("add", 0, 3, 0), ("rows_relay", 3, 1),
    ("gather", 1, 1), ("gather", 2, 1), ("line_end", 0), ("rows_relay", 3, 0), ("gather", 0, 0), ("rows_wait", 0),
    ("store", 0), ("gather", 3, 1), ("rows_wait", 2), ("gather", 2, 2), ("gather", 2, 3), ("gather", 3, 2),
    ("gather", 1, 2), ("gather", 0, 1), ("gather", 1, 3), ("store", 6), ("store", 5), ("gather", 0, 2), ("store", 3),
    ("rows_wait", 3), ("store", 1), ("store", 4),
)
FIRST_STAGE = (0, 0, 1, 1)
WAYS = (1, 1, 1, 1)


def fused(geo, *refs):
    (
        x_hbm, g_hbm, segs_hbm, n1g_hbm, n1b_hbm, q_hbm, q_bias_hbm, k_hbm, v_hbm, v_bias_hbm, o_hbm, out_bias_hbm,
        n2g_hbm, n2b_hbm, up_hbm, up_bias_hbm, down_hbm, down_bias_hbm,
        out_result, out_source, out_a, out_u, out_d, out_o, out_sums,
        segs, n1g, n1b, q_bias, v_bias, out_bias, n2g, n2b, up_bias, down_bias,
        w_a, w_u, w_d, w_o, extra, x, g2, o_own, n1, q, own, cells, near_send, far_send, near_in, far_in,
        table, bias, probs, mixed, middle, n2, hidden, slope, result, total, g1, d_mixed, d_queries, d_table,
        g1_low, near_give, far_give, near_back, far_back, g_a, g_u, g_d, g_o, sums, gathered, source_all,
        line_a, line_u, line_d, line_o, end_a, end_u, end_d, end_o, in_a, in_u, in_d, in_o, r_a, r_u, r_d, r_o, sums_in, sums_all, sums_got,
        load_sem, small_sem, store_sem, zw_send, zw_recv, pw_send, pw_recv, ex_send, ex_recv, halo_send, halo_recv,
        far_s, far_r, back_send, back_recv, farb_s, farb_r, rs_send, rs_recv, zl_send, zl_recv, zx_recv, zy_recv,
        ag_send, ag_recv, gp_send, gp_recv, gc_send, gc_recv, out_send, out_recv, sm_send, sm_recv, sc_send, sc_recv,
        *landings,
    ) = refs
    weights, grads, reduced = (w_a, w_u, w_d, w_o), (g_a, g_u, g_d, g_o), (r_a, r_u, r_d, r_o)
    from_line, from_end, from_inner = (line_a, line_u, line_d, line_o), (end_a, end_u, end_d, end_o), (in_a, in_u, in_d, in_o)
    C, W = geo.ctx, geo.wt
    c, z = lax.axis_index("ctx"), lax.axis_index("wt")
    plane = Plane(C, c, 512)
    B = plane.bits

    loads = [
        pltpu.make_async_copy(q_hbm, weights[0].at[z, :, pl.ds(0, LANES)], load_sem.at[0]),
        pltpu.make_async_copy(k_hbm, weights[0].at[z, :, pl.ds(LANES, LANES)], load_sem.at[1]),
        pltpu.make_async_copy(v_hbm, weights[0].at[z, :, pl.ds(2 * LANES, LANES)], load_sem.at[2]),
        pltpu.make_async_copy(o_hbm, o_own, load_sem.at[3]),
        pltpu.make_async_copy(up_hbm, weights[1].at[z], load_sem.at[4]),
        pltpu.make_async_copy(down_hbm, weights[2].at[z], load_sem.at[5]),
        pltpu.make_async_copy(x_hbm.at[z], x, load_sem.at[6]),
        pltpu.make_async_copy(g_hbm.at[z], g2, load_sem.at[7]),
    ]
    small = [
        pltpu.make_async_copy(source, target, small_sem.at[at])
        for at, (source, target) in enumerate(
            (
                (q_bias_hbm, q_bias), (v_bias_hbm, v_bias), (up_bias_hbm, up_bias), (n1g_hbm, n1g), (n1b_hbm, n1b),
                (segs_hbm, segs), (out_bias_hbm, out_bias), (n2g_hbm, n2g), (n2b_hbm, n2b), (down_bias_hbm, down_bias),
            )
        )
    ]

    for copy in loads + small:
        copy.start()
    near_in[...] = jnp.zeros_like(near_in)
    far_in[...] = jnp.zeros_like(far_in)
    near_back[...] = jnp.zeros_like(near_back)
    far_back[...] = jnp.zeros_like(far_back)

    barrier = pltpu.get_barrier_semaphore()
    for step in range(1, C):
        pl.semaphore_signal(barrier, inc=1, device_id=(lax.rem(c + step, C), z), device_id_type=pl.DeviceIdType.MESH)
    for step in range(1, W):
        pl.semaphore_signal(barrier, inc=1, device_id=(c, lax.rem(z + step, W)), device_id_type=pl.DeviceIdType.MESH)
    sums[...] = jnp.zeros_like(sums)
    extra[z] = jnp.zeros_like(extra[z])
    pl.semaphore_wait(barrier, C + W - 2)

    def order_of(k, w):
        return (k + w) % 2

    relays = W == 4
    inner = (z > 0) & (z < W - 1) if relays else jnp.bool_(False)
    across = jnp.where(z < W // 2, z + 2, z - 2)
    beside = W - 1 - z
    end = jnp.where(z < W // 2, 0, W - 1)
    near_inner = jnp.where(z < W // 2, 1, W - 2)

    def arrival(i, way):
        table_of = []
        for at in range(W):
            seen = []
            for step in range(1, W):
                seen += [w for w in (at - step, at + step) if 0 <= w < W]
            if way == 1 and 0 < at < W - 1:
                seen = [at - 1, at + 2, at + 1] if at < W // 2 else [at + 1, at - 2, at - 1]
            if way == 2 and 0 < at < W - 1:
                seen = [at - 1, at + 1, at + 2] if at < W // 2 else [at + 1, at - 1, at - 2]
            table_of.append(seen[i])
        w = jnp.int32(table_of[0])
        for at in range(1, W):
            w = jnp.where(z == at, table_of[at], w)
        return w

    ways = WAYS if relays else (0, 0, 0, 0)
    first_stage = FIRST_STAGE if B > 2 else (0, 0, 0, 0)
    arrivals_of = [[arrival(i, way) for i in range(W - 1)] for way in ways]
    arrivals = arrivals_of[0]

    def each_direct(action, way):
        for step in range(1, W):
            for to, there in ((z - step, z >= step), (z + step, z + step < W)):
                skip = jnp.bool_(False)
                if way == 1:
                    skip = z + to == W - 1
                if way == 2:
                    skip = (z + to == W - 1) & jnp.logical_not(inner) | inner & (to == across)

                @pl.when(there & jnp.logical_not(skip))
                def _():
                    action(to)

    def weight_line(k, w, to, relayed=False, own=False):
        rows = plane.block(order_of(k, w), first_stage[k])
        slot = w if relayed else to
        mine = {1: up_hbm, 2: down_hbm}.get(k) if own else None
        return remote(
            weights[k].at[w, rows] if mine is None else mine.at[rows], weights[k].at[w, rows], zw_send.at[k, slot, int(relayed)], zw_recv.at[k, w], (c, to)
        )

    def weight_first(k):
        each_direct(lambda to: weight_line(k, z, to, own=True).start(), ways[k])

    def weight_copy(k, w, j, s, landing=False):
        order = order_of(k, w)
        device = plane.partner(order, s)
        seen = device if landing else None
        if j < 0:
            rows = plane.block(order, first_stage[k], device=seen)
        else:
            rows = plane.block(order, j, other=True, device=seen)
        at = s * (s + 1) // 2 + j + 1
        block = weights[k].at[w, rows]
        return remote(block, block, pw_send.at[k, w, at], pw_recv.at[k, w, at], (device, z))

    def held_at(k, s):
        return [-1, *range(first_stage[k], s)] if s >= first_stage[k] else []

    def weight_event(k, i, s):
        w = arrivals_of[k][i]
        if s == 0:
            weight_line(k, w, lax.rem(z + 1, W)).wait_recv()
            if i == 1 and ways[k] == 1:

                @pl.when(inner)
                def _():
                    weight_line(k, w, end, True).start()
                    weight_line(k, z, beside, own=True).start()

            if i > 0 and ways[k] == 2:

                @pl.when(inner)
                def _():
                    weight_line(k, w, end, True).start()

            for later in range(first_stage[k], B):
                weight_copy(k, w, -1, later).start()
        else:
            for j in held_at(k, s - 1):
                weight_copy(k, w, j, s - 1, True).wait_recv()
            if s > first_stage[k]:
                for later in range(s, B):
                    weight_copy(k, w, s - 1, later).start()

    def weight_drain(k):
        each_direct(lambda to: weight_line(k, z, to, own=True).wait_send(), ways[k])
        if ways[k]:

            @pl.when(inner)
            def _():
                weight_line(k, across, end, True).wait_send()
                if ways[k] == 1:
                    weight_line(k, z, beside, own=True).wait_send()
                else:
                    weight_line(k, beside, end, True).wait_send()

        for w in arrivals:
            for s in range(B):
                for j in held_at(k, s):
                    weight_copy(k, w, j, s).wait_send()

    def extra_copy(step):
        to = lax.rem(z + step, W)
        return remote(extra.at[z], extra.at[z], ex_send.at[step], ex_recv.at[step], (c, to))

    def extra_from(step):
        source = lax.rem(z + W - step, W)
        return remote(extra.at[source], extra.at[source], ex_send.at[step], ex_recv.at[step], (c, source))

    def halo(w, back):
        if back:
            return remote(near_give.at[w], near_back.at[w], back_send.at[w], back_recv.at[w], (c - 1, z))
        return remote(near_send.at[w], near_in.at[w], halo_send.at[w], halo_recv.at[w], (c + 1, z))

    def needs(source, target):
        need = jnp.bool_(False)
        for step in range(geo.far):
            size = 2 ** (step + 1)
            need = need | (target // size == source // size + 1)
        return need

    def far_copy(w, device, source):
        return remote(far_send.at[w], far_in.at[source, w], far_s.at[device, w], far_r.at[source, w], (device, z))

    def give_copy(w, device, source):
        return remote(
            far_give.at[device, w], far_back.at[source, w], farb_s.at[device, w], farb_r.at[source, w], (device, z)
        )

    def each_after(action):
        for step in range(1, C):
            device = jnp.minimum(c + step, C - 1)

            @pl.when((c + step < C) & needs(c, device))
            def _():
                action(device)

    def each_before(action):
        for step in range(1, C):
            device = jnp.maximum(c - step, 0)

            @pl.when((c - step >= 0) & needs(device, c))
            def _():
                action(device)

    def halo_start(w):
        @pl.when(c < C - 1)
        def _():
            halo(w, False).start()

        each_after(lambda device: far_copy(w, device, c).start())

    def halo_wait(w):
        @pl.when(c > 0)
        def _():
            halo(w, False).wait_recv()

        each_before(lambda device: far_copy(w, device, device).wait_recv())

    def give_start(w):
        @pl.when(c > 0)
        def _():
            halo(w, True).start()

        each_before(lambda device: give_copy(w, device, c).start())

    def give_wait(w):
        @pl.when(c < C - 1)
        def _():
            halo(w, True).wait_recv()

        each_after(lambda device: give_copy(w, device, device).wait_recv())

    def row_copy(part, w, to, relayed=False):
        rows = (gathered, source_all)[part // 2].at[w, pl.ds(part % 2 * geo.tile, geo.tile)]
        slot = w if relayed else to
        return remote(rows, rows, out_send.at[part, slot, int(relayed)], out_recv.at[part, w], (c, to))

    def rows_first(part):
        each_direct(lambda to: row_copy(part, z, to).start(), 2 if relays else 0)

    def rows_relay(part, far):
        w = across if far else beside

        @pl.when(inner)
        def _():
            row_copy(part, w, end).wait_recv()
            row_copy(part, w, end, True).start()

    def rows_wait(part):
        for step in range(1, W):
            w = lax.rem(z + step, W)

            @pl.when(jnp.logical_not(inner) | (w == end))
            def _():
                row_copy(part, w, w).wait_recv()

    def rows_drain(part):
        each_direct(lambda to: row_copy(part, z, to).wait_send(), 2 if relays else 0)

        @pl.when(inner)
        def _():
            row_copy(part, across, end, True).wait_send()
            row_copy(part, beside, end, True).wait_send()

    def reduce_copy(k, w, s):
        order = order_of(k, w)
        return remote(
            grads[k].at[w, plane.block(order, s, other=True)],
            landings[4 * s + k].at[w],
            rs_send.at[k, w, s],
            rs_recv.at[k, w, s],
            (plane.partner(order, s), z),
        )

    def reduce_add(k, w, s):
        reduce_copy(k, w, s).wait_recv()
        rows = plane.block(order_of(k, w), s)
        grads[k][w, rows] = (grads[k][w, rows].astype(F32) + landings[4 * s + k][w].astype(F32)).astype(BF16)
        if s > 0:
            reduce_copy(k, w, s - 1).start()
        else:
            line_send(k, w)

    def line_copy(k, w, way=None):
        rows = plane.block(order_of(k, w), 0)
        if way == "end":
            return remote(grads[k].at[w, rows], from_end[k], zl_send.at[k, w], zx_recv.at[k], (c, near_inner))
        if way == "inner":
            return remote(grads[k].at[w, rows], from_inner[k], zl_send.at[k, w], zy_recv.at[k], (c, beside))
        return remote(grads[k].at[w, rows], from_line[k].at[z], zl_send.at[k, w], zl_recv.at[k, z], (c, w))

    chained = (False, relays, relays, False)

    def line_send(k, w):
        over = jnp.logical_not(inner) & (w == beside) if chained[k] else jnp.bool_(False)
        waits = inner & ((w == across) | (w == end)) if chained[k] else jnp.bool_(False)

        @pl.when(over)
        def _():
            line_copy(k, w, "end").start()

        @pl.when((w != z) & jnp.logical_not(over | waits))
        def _():
            line_copy(k, w).start()

    def line_add(k, w, landed):
        rows = plane.block(order_of(k, w), 0)
        grads[k][w, rows] = (grads[k][w, rows].astype(F32) + landed[k][...].astype(F32)).astype(BF16)

    def line_over(k):
        @pl.when(inner)
        def _():
            line_copy(k, across, "end").wait_recv()
            line_add(k, across, from_end)
            line_copy(k, across, "inner").start()

    def line_pass(k):
        @pl.when(inner)
        def _():
            line_copy(k, across, "inner").wait_recv()
            line_add(k, end, from_inner)
            line_copy(k, end).start()

    def line_drain(k, w):
        @pl.when(w != z)
        def _():
            line_copy(k, w).wait_send()

    def own_rows(k):
        return plane.block(order_of(k, z), 0)

    def line_end(k):
        rows = own_rows(k)
        total_now = grads[k][z, rows].astype(F32)
        for step in range(1, W):
            source = lax.rem(z + step, W)
            block = from_line[k].at[source]
            comes = inner | (source == near_inner) if chained[k] else jnp.bool_(True)

            @pl.when(comes)
            def _():
                remote(block, block, zl_send.at[k, source], zl_recv.at[k, source], (c, source)).wait_recv()

            total_now = total_now + jnp.where(comes, from_line[k][source].astype(F32), 0.0)
        reduced[k][rows] = total_now.astype(BF16)

    def gather_copy(k, j, s):
        order = order_of(k, z)
        rows = plane.block(order, 0) if j < 0 else plane.block(order, j, other=True)
        at = s * (s + 1) // 2 + j + 1
        block = reduced[k].at[rows]
        return remote(block, block, ag_send.at[k, at], ag_recv.at[k, at], (plane.partner(order, s), z))

    def gather_landing(k, j, s):
        order = order_of(k, z)
        device = plane.partner(order, s)
        rows = plane.block(order, 0, device=device) if j < 0 else plane.block(order, j, other=True, device=device)
        at = s * (s + 1) // 2 + j + 1
        block = reduced[k].at[rows]
        return remote(block, block, ag_send.at[k, at], ag_recv.at[k, at], (device, z))

    def gather_plane(k, offset, landing=False):
        device = plane.flips(2 * offset)
        block = reduced[k].at[plane.block(order_of(k, z), 0, device=device if landing else None)]
        return remote(block, block, gp_send.at[k, offset], gp_recv.at[k, offset], (device, z))

    def gather_core(k, offset, landing=False):
        block = reduced[k].at[plane.block(order_of(k, z), 0, device=plane.flips(2 * offset + int(landing)))]
        return remote(block, block, gc_send.at[k, offset], gc_recv.at[k, offset], (plane.flips(1), z))

    straight = (True, False, False, True)

    def gather_event(k, s):
        if straight[k]:
            offsets = range(1, C // 2) if s < 2 else range(C // 2)
            for offset in offsets:
                if s == 0:
                    gather_plane(k, offset).start()
                elif s == 1:
                    gather_plane(k, offset, True).wait_recv()
                    gather_core(k, offset).start()
                elif s == 2:
                    gather_core(k, offset, True).wait_recv()
            if s == 0:
                gather_core(k, 0).start()
            return
        if s > 0:
            for j in range(-1, s - 1):
                gather_landing(k, j, s - 1).wait_recv()
        for later in range(s, B):
            gather_copy(k, s - 1, later).start()

    def gather_drain(k):
        if straight[k]:
            for offset in range(C // 2):
                if offset:
                    gather_plane(k, offset).wait_send()
                gather_core(k, offset).wait_send()
            return
        for s in range(B):
            for j in range(-1, s):
                gather_copy(k, j, s).wait_send()

    held = {}
    shard_of = [z] + arrivals
    feed_of = [z] + arrivals_of[2]
    turn = [w for step in range((W + 1) // 2) for w in dict.fromkeys((step, W - 1 - step))]

    def send_shards(k):
        for at in {0: (0, 1, 2), 3: (3,)}.get(k, ()):
            loads[at].wait()
        if k == 3:
            weights[3][z] = o_own[...].T
        weight_first(k)

    def send_biases():
        for at in (0, 1, 2):
            small[at].wait()
        extra[z, 0:1, :] = up_bias[...]
        extra[z, 1:2, :LANES] = q_bias[...]
        extra[z, 1:2, LANES : 2 * LANES] = v_bias[...]
        for step in range(1, W):
            extra_copy(step).start()

    def wait_biases():
        for step in range(1, W):
            extra_from(step).wait_recv()

    def first_norm():
        loads[6].wait()
        small[3].wait()
        small[4].wait()
        normed, _ = norm_parts(x[...].astype(F32))
        n1[...] = (normed * n1g[...] + n1b[...]).astype(BF16)

    def masks():
        small[5].wait()
        bias[0] = mask_bias(geo, c, segs[pl.ds(z, 1), :], 0)
        bias[1] = mask_bias(geo, c, segs[pl.ds(z, 1), :], 1)
        held["pick"] = far_matrix(geo, c)

    def projection(i):
        w = shard_of[i]
        project(w, n1, weights, extra, q, own, cells, near_send, far_send)
        halo_start(w)

    def attention(i):
        w = shard_of[i]
        halo_wait(w)
        tables(geo, w, held["pick"], own, cells, near_in, far_in, table)
        for tile in (0, 1):
            attend(geo, w, tile, q, table, bias, probs, mixed)

    def event(k, i, s):
        for stage in {0: [0], 1: [1], 2: range(2, B), 3: [B]}[s]:
            weight_event(k, i, stage)

    def second_norm():
        for at in (4, 5, 7):
            loads[at].wait()
        for at in range(6, 10):
            small[at].wait()
        acc = x[...].astype(F32) + out_bias[...]
        for w in range(W):
            acc = acc + dot_nt(mixed[w], weights[3][w])
        middle[...] = acc
        normed, _ = norm_parts(acc)
        n2[...] = (normed * n2g[...] + n2b[...]).astype(BF16)
        result[...] = acc + down_bias[...]

    def forth(i):
        feed(feed_of[i], n2, weights, extra, hidden, slope, result)

    def layer_rows():
        gathered[z] = result[...].astype(BF16)

    def back(i):
        first = "total" not in held
        held["total"] = True
        feed_back(first, feed_of[i], g2, weights, n2, hidden, slope, sums, grads, total)

    def shard(k, i):
        return feed_of[i] if k in (1, 2) else turn[i]

    def halve(k, i):
        reduce_copy(k, shard(k, i), B - 1).start()

    def add(k, i, s):
        for stage in {2: [B - 1], 1: range(B - 2, 0, -1), 0: [0]}[s]:
            reduce_add(k, shard(k, i), stage)

    def second_back():
        hat, inverse = norm_parts(middle[...])
        d_normed = total[...]
        wide = g2[...].astype(F32)
        first = wide + norm_backward(d_normed, hat, inverse, n2g[...])
        g1[...] = first
        g1_low[...] = first.astype(BF16)
        put_sums(geo, sums, 2, jnp.sum(first, axis=0, keepdims=True))
        put_sums(geo, sums, 3, jnp.sum(d_normed * hat, axis=0, keepdims=True))
        put_sums(geo, sums, 4, jnp.sum(d_normed, axis=0, keepdims=True))
        put_sums(geo, sums, 5, jnp.sum(wide, axis=0, keepdims=True))
        del held["total"]

    def out_back(i):
        w = turn[i]
        d_mixed[w] = dot_nn(g1_low[...], weights[3][w]).astype(BF16)
        grads[3][w] = dot_tn(g1_low[...], mixed[w]).astype(BF16)

    def give(i):
        w = turn[i]
        for tile in (0, 1):
            attend_back(geo, w, tile, q, table, probs, d_mixed, d_queries, d_table)
        return_cells(geo, w, held["pick"], d_table, near_give, far_give)
        give_start(w)

    def take(i):
        w = turn[i]
        give_wait(w)
        first = "total" not in held
        held["total"] = True
        project_back(geo, first, w, weights, n1, d_queries, d_table, near_back, far_back, sums, grads, total)

    def source():
        normed, inverse = norm_parts(x[...].astype(F32))
        d_normed = total[...]
        source_all[z] = (g1[...] + norm_backward(d_normed, normed, inverse, n1g[...])).astype(BF16)
        put_sums(geo, sums, 0, jnp.sum(d_normed * normed, axis=0, keepdims=True))
        put_sums(geo, sums, 1, jnp.sum(d_normed, axis=0, keepdims=True))

    def sums_copy(step):
        to = lax.rem(z + step, W)
        return remote(sums.at[to], sums_in.at[step], sm_send.at[step], sm_recv.at[step], (c, to))

    def sums_stage(s):
        return remote(sums_all.at[s], sums_got.at[s], sc_send.at[s], sc_recv.at[s], (plane.flip(1 << s), z))

    def send_sums():
        for step in range(1, W):
            sums_copy(step).start()

    def add_sums(s):
        if s == 0:
            total_sums = sums[z]
            for step in range(1, W):
                sums_copy(step).wait_recv()
                total_sums = total_sums + sums_in[step]
            sums_all[0] = total_sums
            sums_stage(0).start()
        for stage in {0: [], 1: [0], 2: range(1, B - 1), 3: [B - 1]}[s]:
            sums_stage(stage).wait_recv()
            sums_all[stage + 1] = sums_all[stage] + sums_got[stage]
            if stage + 1 < B:
                sums_stage(stage + 1).start()

    def gather(k, s):
        for stage in {0: [0], 1: [1], 2: range(2, B), 3: [B]}[s]:
            gather_event(k, stage)

    stores = [
        pltpu.make_async_copy(gathered, out_result, store_sem.at[0]),
        pltpu.make_async_copy(source_all, out_source, store_sem.at[1]),
        pltpu.make_async_copy(sums_all.at[B], out_sums, store_sem.at[2]),
        pltpu.make_async_copy(r_a, out_a, store_sem.at[3]),
        pltpu.make_async_copy(r_u, out_u, store_sem.at[4]),
        pltpu.make_async_copy(r_d, out_d, store_sem.at[5]),
        pltpu.make_async_copy(r_o, out_o, store_sem.at[6]),
    ]

    def store(i):
        stores[i].start()

    steps = {
        step.__name__: step
        for step in (
            send_shards, send_biases, wait_biases, first_norm, masks, projection, attention, event, second_norm, forth,
            layer_rows, back, halve, add, second_back, out_back, give, take, source, send_sums, add_sums, gather, store,
            rows_first, rows_relay, rows_wait, line_over, line_pass, line_end,
        )
    }
    for name, *args in SCHEDULE:
        steps[name](*args)

    for k in range(4):
        weight_drain(k)
        for w in range(W):
            for s in range(B):
                reduce_copy(k, w, s).wait_send()
            line_drain(k, w)
        gather_drain(k)
    for part in range(4):
        rows_drain(part)
    for step in range(1, W):
        extra_copy(step).wait_send()
        sums_copy(step).wait_send()
    for s in range(B):
        sums_stage(s).wait_send()

    for w in range(W):

        @pl.when(c < C - 1)
        def _():
            halo(w, False).wait_send()

        @pl.when(c > 0)
        def _():
            halo(w, True).wait_send()

        each_after(lambda device: far_copy(w, device, c).wait_send())
        each_before(lambda device: give_copy(w, device, c).wait_send())
    for copy in stores:
        copy.wait()


def unpack(
    result_in, source_in, a_in, u_in, d_in, o_in, sums_in,
    result_out, source_out, d_n1g, d_n1b, d_q, d_qb, d_k, d_v, d_vb, d_o, d_ob, d_n2g, d_n2b, d_up, d_upb, d_down, d_db,
    result, source, a, u, d, o, sums, result_f, source_f, a_f, o_f, u_f, d_f, row_f, load_sem, store_sem,
):
    runs = result.shape[0]
    pairs = [(result_in.at[m], result.at[m]) for m in range(runs)] + [(source_in.at[m], source.at[m]) for m in range(runs)]
    pairs += [(a_in, a), (u_in, u), (d_in, d), (o_in, o), (sums_in, sums)]
    loads = [pltpu.make_async_copy(*pair, load_sem.at[at]) for at, pair in enumerate(pairs)]
    for copy in loads:
        copy.start()
    stores = []

    def put(held, target):
        copy = pltpu.make_async_copy(held, target, store_sem.at[len(stores)])
        copy.start()
        stores.append(copy)

    for m in range(runs):
        loads[m].wait()
        result_f[m] = result[m].astype(F32)
        put(result_f.at[m], result_out.at[m])
    for m in range(runs):
        loads[runs + m].wait()
        source_f[m] = source[m].astype(F32)
        put(source_f.at[m], source_out.at[m])
    loads[2 * runs].wait()
    for at, target in enumerate((d_q, d_k, d_v)):
        a_f[at] = a[:, at * LANES : (at + 1) * LANES].astype(F32)
        put(a_f.at[at], target)
    loads[2 * runs + 1].wait()
    u_f[...] = u[...].astype(F32)
    put(u_f, d_up)
    loads[2 * runs + 2].wait()
    d_f[...] = d[...].astype(F32)
    put(d_f, d_down)
    loads[2 * runs + 3].wait()
    o_f[...] = o[...].astype(F32).T
    put(o_f, d_o)
    loads[2 * runs + 4].wait()
    for at, target in enumerate((d_n1g, d_n1b, d_ob, d_n2g, d_n2b, d_db)):
        row, lane = 2 + at // 4, at % 4 * LANES
        row_f[at, :, :LANES] = sums[row : row + 1, lane : lane + LANES]
        put(row_f.at[at, :, pl.ds(0, LANES)], target)
    for at, target in ((6, d_qb), (7, d_vb)):
        row_f[at, :, :LANES] = sums[1:2, (at - 6) * LANES : (at - 5) * LANES]
        put(row_f.at[at, :, pl.ds(0, LANES)], target)
    row_f[8] = sums[0:1, :]
    put(row_f.at[8], d_upb)
    for copy in stores:
        copy.wait()


def shards(
    x_in,
    grad_out,
    seg_ids,
    norm1_gain,
    norm1_bias,
    q_weight,
    q_bias,
    k_weight,
    v_weight,
    v_bias,
    out_weight,
    out_bias,
    norm2_gain,
    norm2_bias,
    up_weight,
    up_bias,
    down_weight,
    down_bias,
):
    C, W = lax.axis_size("ctx"), lax.axis_size("wt")
    runs, T, width = x_in.shape
    hidden = up_weight.shape[1]
    geo = Geometry(C, W, T)
    S, B = geo.slots, C.bit_length() - 1
    each = width // C
    assert runs == W and hidden == width and q_weight.shape[1] == LANES and T == 256
    sds = jax.ShapeDtypeStruct
    vmem, dma = pltpu.VMEM, pltpu.SemaphoreType.DMA
    row = lambda v: v.reshape(1, -1)
    pair = 2 * LANES
    wide_of = (3 * LANES, hidden, width, LANES)
    scratch = [
        vmem(seg_ids.shape, jnp.int32),
        *[vmem((1, n), F32) for n in (width, width, LANES, LANES, width, width, width, hidden, width)],
        *[vmem((W, width, n), BF16) for n in wide_of],
        vmem((W, 8, width), F32),
        vmem((T, width), BF16),
        vmem((T, width), BF16),
        vmem((LANES, width), BF16),
        vmem((T, width), BF16),
        vmem((W, T, LANES), BF16),
        vmem((W, T, pair), BF16),
        vmem((W, 224, pair), BF16),
        vmem((W, 80, pair), BF16),
        vmem((W, 16, pair), BF16),
        vmem((W, 80, pair), BF16),
        vmem((C, W, 16, pair), BF16),
        vmem((W, 2, S, pair), BF16),
        vmem((2, S, geo.tile), F32),
        vmem((W, 2, S, pair), BF16),
        vmem((W, T, LANES), BF16),
        vmem((T, width), F32),
        vmem((T, width), BF16),
        vmem((W, T, hidden), BF16),
        vmem((W, T, hidden), F32),
        vmem((T, width), F32),
        vmem((T, width), F32),
        vmem((T, width), F32),
        vmem((W, T, LANES), BF16),
        vmem((W, T, LANES), BF16),
        vmem((W, 2, S, pair), F32),
        vmem((T, width), BF16),
        vmem((W, 80, pair), BF16),
        vmem((C, W, 16, pair), BF16),
        vmem((W, 80, pair), BF16),
        vmem((C, W, 16, pair), BF16),
        *[vmem((W, width, n), BF16) for n in wide_of],
        vmem((W, 8, width), F32),
        vmem((W, T, width), BF16),
        vmem((W, T, width), BF16),
        *[vmem((W, each, n), BF16) for n in wide_of],
        *[vmem((each, n), BF16) for n in wide_of],
        *[vmem((each, n), BF16) for n in wide_of],
        *[vmem((width, n), BF16) for n in wide_of],
        vmem((W, 8, width), F32),
        vmem((B + 1, 8, width), F32),
        vmem((B, 8, width), F32),
        dma((8,)),
        dma((10,)),
        dma((7,)),
        dma((4, W, 2)),
        dma((4, W)),
        dma((4, W, B * (B + 1) // 2)),
        dma((4, W, B * (B + 1) // 2)),
        dma((W,)),
        dma((W,)),
        dma((W,)),
        dma((W,)),
        dma((C, W)),
        dma((C, W)),
        dma((W,)),
        dma((W,)),
        dma((C, W)),
        dma((C, W)),
        dma((4, W, B)),
        dma((4, W, B)),
        dma((4, W)),
        dma((4, W)),
        dma((4,)),
        dma((4,)),
        dma((4, B * (B + 1) // 2)),
        dma((4, B * (B + 1) // 2)),
        dma((4, C // 2)),
        dma((4, C // 2)),
        dma((4, C // 2)),
        dma((4, C // 2)),
        dma((4, W, 2)),
        dma((4, W)),
        dma((W,)),
        dma((W,)),
        dma((B,)),
        dma((B,)),
    ] + [vmem((W, each * 2**s, n), BF16) for s in range(B) for n in wide_of]
    far = pl.BlockSpec(memory_space=pl.ANY)
    result, source, d_a, d_u, d_d, d_o, sums = pl.pallas_call(
        functools.partial(fused, geo),
        name="fused",
        out_shape=[sds((W, T, width), BF16), sds((W, T, width), BF16), *[sds((width, n), BF16) for n in wide_of], sds((8, width), F32)],
        in_specs=[far] * 18,
        out_specs=[far] * 7,
        scratch_shapes=scratch,
        compiler_params=pltpu.CompilerParams(collective_id=0, has_side_effects=True, vmem_limit_bytes=58 * 2**20),
    )(
        x_in, grad_out, seg_ids, row(norm1_gain), row(norm1_bias), q_weight, row(q_bias), k_weight, v_weight, row(v_bias),
        out_weight, row(out_bias), row(norm2_gain), row(norm2_bias), up_weight, row(up_bias), down_weight, row(down_bias),
    )
    one, thin, full = (1, LANES), (width, LANES), (width, width)
    shapes = [(W, T, width)] * 2 + [one, one, thin, one, thin, thin, one, (LANES, width), one, one, one, full, (1, hidden), full, one]
    values = pl.pallas_call(
        unpack,
        name="unpack",
        out_shape=[sds(shape, F32) for shape in shapes],
        in_specs=[far] * 7,
        out_specs=[far] * 17,
        scratch_shapes=[
            vmem((W, T, width), BF16),
            vmem((W, T, width), BF16),
            *[vmem((width, n), BF16) for n in wide_of],
            vmem((8, width), F32),
            vmem((W, T, width), F32),
            vmem((W, T, width), F32),
            vmem((3, width, LANES), F32),
            vmem((LANES, width), F32),
            vmem(full, F32),
            vmem(full, F32),
            vmem((9, 1, hidden), F32),
            dma((2 * W + 5,)),
            dma((2 * W + 15,)),
        ],
        compiler_params=pltpu.CompilerParams(vmem_limit_bytes=58 * 2**20),
    )(result, source, d_a, d_u, d_d, d_o, sums)
    return tuple(v.reshape(-1) if v.shape[0] == 1 else v for v in values)


def solution(mesh):
    in_specs = (
        P(None, "ctx", None),
        P(None, "ctx", None),
        P(),
        P(),
        P(),
        P(None, "wt"),
        P("wt"),
        P(None, "wt"),
        P(None, "wt"),
        P("wt"),
        P("wt", None),
        P(),
        P(),
        P(),
        P(None, "wt"),
        P("wt"),
        P("wt", None),
        P(),
    )
    out_specs = (
        P(None, "ctx", None),
        P(None, "ctx", None),
        P("wt"),
        P("wt"),
        P(None, "wt"),
        P("wt"),
        P(None, "wt"),
        P(None, "wt"),
        P("wt"),
        P("wt", None),
        P("wt"),
        P("wt"),
        P("wt"),
        P(None, "wt"),
        P("wt"),
        P("wt", None),
        P("wt"),
    )
    return jax.shard_map(shards, mesh=mesh, in_specs=in_specs, out_specs=out_specs, check_vma=False)
```

```python
import functools

import jax
import jax.numpy as jnp
from jax import lax
from jax.experimental import pallas as pl
from jax.experimental.pallas import tpu as pltpu
from jax.sharding import PartitionSpec as P

HEAD_DIM = 64
BLOCK = 16
LEVELS = 10
FINE = 3
EPSILON = 1e-05
NEGATIVE = -1e30
LOG_TWO = 0.6931471805599453
LANES = 128
BF16 = jnp.bfloat16
F32 = jnp.float32


def dot(left, right, dims):
    return lax.dot_general(left, right, (dims, ((), ())), preferred_element_type=F32)


def dot_nn(left, right):
    return dot(left, right, ((1,), (0,)))


def dot_nt(left, right):
    return dot(left, right, ((1,), (1,)))


def dot_tn(left, right):
    return dot(left, right, ((0,), (0,)))


def norm_parts(source):
    centre = jnp.mean(source, axis=-1, keepdims=True)
    centred = source - centre
    variance = jnp.mean(centred * centred, axis=-1, keepdims=True)
    inverse = lax.rsqrt(variance + EPSILON)
    return centred * inverse, inverse


def norm_backward(upstream, normed, inverse, gain):
    scaled = upstream * gain
    first_mean = jnp.mean(scaled, axis=-1, keepdims=True)
    second_mean = jnp.mean(scaled * normed, axis=-1, keepdims=True)
    return inverse * (scaled - first_mean - normed * second_mean)


def iota(shape, axis):
    return lax.broadcasted_iota(jnp.int32, shape, axis)


class Geometry:
    def __init__(self, ctx, wt, tok_dev):
        self.ctx, self.wt, self.tok_dev = ctx, wt, tok_dev
        tokens = ctx * tok_dev
        self.levels = len([l for l in range(LEVELS) if BLOCK * 2**l < tokens])
        self.own_cells = [tok_dev // 2**l if l <= FINE else 0 for l in range(self.levels)]
        self.tile = tok_dev // 2
        self.tile_slots = [BLOCK + self.tile] + [BLOCK * 4 >> (l - 1) if l < FINE else BLOCK for l in range(1, self.levels)]
        self.slots = sum(self.tile_slots)
        self.slot_at = [sum(self.tile_slots[:l]) for l in range(self.levels + 1)]
        self.far = self.levels - (FINE + 2)
        self.near = FINE + 2


def pool_matrix():
    parts = []
    for level, count in ((1, 128), (2, 64), (3, 32)):
        hit = (iota((count, 256), 1) >> level) == iota((count, 256), 0)
        parts.append(jnp.where(hit, 1.0 / 2**level, 0.0))
    return jnp.concatenate(parts, axis=0).astype(BF16)


def coarse_matrix():
    row, column = iota((32, 32), 0), iota((32, 32), 1)
    out = jnp.zeros((32, 32), F32)
    first = 0
    for level, count in ((4, 16), (5, 8), (6, 4), (7, 2), (8, 1)):
        up = level - FINE
        hit = (row >= first) & (row < first + count) & ((column >> up) == row - first)
        out = jnp.where(hit, 1.0 / 2**up, out)
        first += count
    return out.astype(BF16)


def far_matrix(geo, me):
    parts = []
    first = 0
    for step in range(geo.far):
        up = step + 1
        each = BLOCK >> up
        row, column = iota((BLOCK, geo.ctx * BLOCK), 0), iota((BLOCK, geo.ctx * BLOCK), 1)
        group = (me >> up) - 1
        device = (group << up) + (row >> (4 - up))
        wanted = device * BLOCK + first + (row & (each - 1))
        parts.append(jnp.where((column == wanted) & (group >= 0), 1.0, 0.0))
        first += each
    return jnp.concatenate(parts, axis=0).astype(BF16)


def mask_bias(geo, me, segs, tile):
    first_pos = me * geo.tok_dev + tile * geo.tile
    seg_one = jnp.sum((segs < 1).astype(jnp.int32), axis=1, keepdims=True)
    seg_two = jnp.sum((segs < 2).astype(jnp.int32), axis=1, keepdims=True)
    position = first_pos + iota((1, geo.tile), 1)
    begins = jnp.where(position >= seg_two, seg_two, jnp.where(position >= seg_one, seg_one, 0))
    parts = []
    for level in range(geo.levels):
        size, shift = 2**level, level + 4
        count = geo.tile_slots[level]
        span = BLOCK * size
        if level <= FINE:
            base = first_pos - span
        else:
            base = (((me * geo.tok_dev) >> shift) - 1) << shift
        begin = base + size * iota((count, geo.tile), 0)
        lower = jnp.maximum(((position >> shift) - 1) << shift, begins)
        if level == 0:
            upper = position + 1
        else:
            upper = ((position >> (shift - 1)) - 1) << (shift - 1)
        valid = (begin >= lower) & (begin + size <= upper)
        parts.append(jnp.where(valid, level * LOG_TWO, NEGATIVE))
    return jnp.concatenate(parts, axis=0)


def both_heads(pair):
    lane = iota(pair.shape, 1)
    zero = jnp.zeros_like(pair)
    return jnp.concatenate([jnp.where(lane < HEAD_DIM, pair, zero), jnp.where(lane >= HEAD_DIM, pair, zero)], axis=0)


def own_lanes(stacked):
    rows = stacked.shape[0] // 2
    lane = iota((rows, stacked.shape[1]), 1)
    return jnp.where(lane < HEAD_DIM, stacked[:rows], stacked[rows:])


def project(w, n1, weights, extra, q, own, cells, near, far):
    out = dot_nn(n1[...], weights[0][w])
    bias = extra[w, 1:2, :]
    q[w] = ((out[:, :LANES] + bias[:, :LANES]).astype(BF16) * 0.125).astype(BF16)
    kv = jnp.concatenate(
        [out[:, LANES : 2 * LANES], out[:, 2 * LANES :] + bias[:, LANES : 2 * LANES]], axis=1
    ).astype(BF16)
    own[w] = kv
    fine = dot_nn(pool_matrix(), kv).astype(BF16)
    cells[w] = fine
    rough = dot_nn(coarse_matrix(), fine[192:224]).astype(BF16)
    near[w, 0:16] = kv[240:256]
    near[w, 16:32] = fine[112:128]
    near[w, 32:48] = fine[176:192]
    near[w, 48:64] = fine[208:224]
    near[w, 64:80] = rough[0:16]
    far[w] = rough[16:32]


def tables(geo, w, pick, own, cells, near_in, far_in, table):
    blocks = far_in[:, w].reshape(geo.ctx * BLOCK, 2 * LANES)
    rough = dot_nn(pick, blocks).astype(BF16)
    at = geo.slot_at
    table[w, 0, 0:16] = near_in[w, 0:16]
    table[w, 0, 16:144] = own[w, 0:128]
    table[w, 1, 0:144] = own[w, 112:256]
    table[w, 0, at[1] : at[1] + 16] = near_in[w, 16:32]
    table[w, 0, at[1] + 16 : at[2]] = cells[w, 0:48]
    table[w, 1, at[1] : at[2]] = cells[w, 48:112]
    table[w, 0, at[2] : at[2] + 16] = near_in[w, 32:48]
    table[w, 0, at[2] + 16 : at[3]] = cells[w, 128:144]
    table[w, 1, at[2] : at[3]] = cells[w, 144:176]
    table[w, 0, at[3] : at[4]] = near_in[w, 48:64]
    table[w, 1, at[3] : at[4]] = cells[w, 192:208]
    for tile in (0, 1):
        table[w, tile, at[4] : at[5]] = near_in[w, 64:80]
        table[w, tile, at[5] :] = rough


def attend(geo, w, tile, q, table, bias, probs, mixed):
    rows = slice(tile * geo.tile, (tile + 1) * geo.tile)
    both = both_heads(q[w, rows, :])
    level_bias = bias[tile]
    scores = dot_nt(table[w, tile, :, :LANES], both)
    scores = scores + jnp.concatenate([level_bias, level_bias], axis=1)
    top = jnp.max(scores, axis=0, keepdims=True)
    exponent = jnp.exp(scores - top)
    total = jnp.sum(exponent, axis=0, keepdims=True)
    low = (exponent * (1.0 / total)).astype(BF16)
    probs[w, tile] = low
    mixed[w, rows, :] = own_lanes(dot_tn(low, table[w, tile, :, LANES:])).astype(BF16)


def attend_back(geo, w, tile, q, table, probs, d_mixed, d_queries, d_table):
    rows = slice(tile * geo.tile, (tile + 1) * geo.tile)
    both = both_heads(q[w, rows, :])
    d_both = both_heads(d_mixed[w, rows, :])
    low = probs[w, tile]
    d_probs = dot_nt(table[w, tile, :, LANES:], d_both)
    wide = low.astype(F32)
    product = wide * d_probs
    centre = jnp.sum(product, axis=0, keepdims=True)
    d_scores = (product - wide * centre).astype(BF16)
    d_table[w, tile, :, :LANES] = dot_nn(d_scores, both)
    d_table[w, tile, :, LANES:] = dot_nn(low, d_both)
    back = own_lanes(dot_tn(d_scores, table[w, tile, :, :LANES]))
    d_queries[w, rows, :] = (back * 0.125).astype(BF16)


def return_cells(geo, w, pick, d_table, near, far):
    at = geo.slot_at
    near[w, 0:16] = d_table[w, 0, 0:16].astype(BF16)
    near[w, 16:32] = d_table[w, 0, at[1] : at[1] + 16].astype(BF16)
    near[w, 32:48] = d_table[w, 0, at[2] : at[2] + 16].astype(BF16)
    near[w, 48:64] = d_table[w, 0, at[3] : at[4]].astype(BF16)
    near[w, 64:80] = (d_table[w, 0, at[4] : at[5]] + d_table[w, 1, at[4] : at[5]]).astype(BF16)
    rough = (d_table[w, 0, at[5] :] + d_table[w, 1, at[5] :]).astype(BF16)
    far[:, w] = dot_tn(pick, rough).astype(BF16).reshape(geo.ctx, BLOCK, 2 * LANES)


def own_gradients(geo, w, d_table, near_back, far_back):
    at = geo.slot_at
    first, second = d_table.at[w, 0], d_table.at[w, 1]
    back = near_back[w].astype(F32)
    tokens = jnp.concatenate(
        [first[16:128], first[128:144] + second[0:16], second[16:128], second[128:144] + back[0:16]], axis=0
    )
    far = jnp.sum(far_back[:, w].astype(F32), axis=0)
    rough = jnp.concatenate([back[64:80], far], axis=0)
    fine = dot_tn(coarse_matrix(), rough.astype(BF16))
    level3 = jnp.concatenate([second[at[3] : at[4]], back[48:64]], axis=0) + fine
    cells = jnp.concatenate(
        [
            first[at[1] + 16 : at[2]],
            second[at[1] : at[2]],
            back[16:32],
            first[at[2] + 16 : at[3]],
            second[at[2] : at[3]],
            back[32:48],
            level3,
        ],
        axis=0,
    )
    return tokens + dot_tn(pool_matrix(), cells.astype(BF16))


def feed(w, n2, weights, extra, hidden, slope, result):
    pre = dot_nn(n2[...], weights[1][w]) + extra[w, 0:1, :]
    gate = jax.nn.sigmoid(pre)
    hidden[w] = (pre * gate).astype(BF16)
    slope[w] = gate * (1.0 + pre * (1.0 - gate))
    result[...] += dot_nn(hidden[w], weights[2][w])


def feed_back(first, w, g2, weights, n2, hidden, slope, sums, grads, total):
    d_hidden = dot_nt(g2[...], weights[2][w]).astype(BF16).astype(F32)
    d_up = (d_hidden * slope[w]).astype(BF16)
    sums[w, 0:1, :] = jnp.sum(d_up.astype(F32), axis=0, keepdims=True)
    grads[2][w] = dot_tn(hidden[w], g2[...]).astype(BF16)
    grads[1][w] = dot_tn(n2[...], d_up).astype(BF16)
    part = dot_nt(d_up, weights[1][w])
    total[...] = part if first else total[...] + part


def put_sums(geo, sums, column, row):
    at, lanes = 2 + column // 4, slice(column % 4 * LANES, (column % 4 + 1) * LANES)
    for w in range(geo.wt):
        sums[w, at : at + 1, lanes] = row[:, w * LANES : (w + 1) * LANES]


def project_back(geo, first, w, weights, n1, d_queries, d_table, near_back, far_back, sums, grads, total):
    kv = own_gradients(geo, w, d_table, near_back, far_back).astype(BF16)
    d_qkv = jnp.concatenate([d_queries[w], kv], axis=1)
    sums[w, 1:2, :LANES] = jnp.sum(d_qkv[:, :LANES].astype(F32), axis=0, keepdims=True)
    sums[w, 1:2, LANES : 2 * LANES] = jnp.sum(d_qkv[:, 2 * LANES :].astype(F32), axis=0, keepdims=True)
    grads[0][w] = dot_tn(n1[...], d_qkv).astype(BF16)
    part = dot_nt(d_qkv, weights[0][w])
    total[...] = part if first else total[...] + part


def remote(source, target, sent, landed, device):
    return pltpu.make_async_remote_copy(source, target, sent, landed, device_id=device, device_id_type=pl.DeviceIdType.MESH)


class Plane:
    def __init__(self, ctx, c, rows):
        self.ctx, self.c = ctx, c
        self.bits = ctx.bit_length() - 1
        self.each = rows // ctx
        plane_bits = self.bits - 1
        half = plane_bits // 2
        self.plane_bits, self.half = plane_bits, half
        self.places = self.places_of(c)
        self.masks = (
            [2 << s for s in range(plane_bits)] + [1],
            [2 << (s + half) % plane_bits for s in range(plane_bits)] + [1],
        )

    def places_of(self, device):
        plane, core = device // 2, device % 2
        turned = plane // 2**self.half + plane % 2**self.half * 2 ** (self.plane_bits - self.half)
        top = core * 2**self.plane_bits
        return plane + top, turned + top

    def place(self, order, device=None):
        places = self.places if device is None else self.places_of(device)
        if isinstance(order, int):
            return places[order]
        return jnp.where(order == 0, places[0], places[1])

    def partner(self, order, stage):
        if isinstance(order, int):
            return self.flip(self.masks[order][stage])
        return jnp.where(order == 0, self.flip(self.masks[0][stage]), self.flip(self.masks[1][stage]))

    def flip(self, mask):
        return self.c + mask * (1 - 2 * (self.c // mask % 2))

    def flips(self, bits):
        device = self.c
        for s in range(self.bits):
            if bits >> s & 1:
                device = device + (1 << s) * (1 - 2 * (self.c // (1 << s) % 2))
        return device

    def block(self, order, stage, other=False, device=None):
        index = self.place(order, device) // 2**stage
        if other:
            index = index + 1 - 2 * (index % 2)
        size = self.each * 2**stage
        return pl.ds(pl.multiple_of(index * size, size), size)


SCHEDULE = (
    ("send_shards", 0), ("first_norm",), ("send_shards", 1), ("send_shards", 3), ("event", 0, 0, 0),
    ("event", 0, 1, 0), ("event", 1, 0, 0), ("event", 0, 0, 1), ("event", 3, 0, 0), ("send_biases",),
    ("projection", 0), ("event", 1, 1, 0), ("event", 0, 2, 0), ("event", 3, 1, 0), ("event", 3, 1, 1), ("masks",),
    ("event", 1, 0, 1), ("send_shards", 2), ("event", 0, 0, 2), ("event", 1, 2, 0), ("event", 0, 1, 1),
    ("event", 3, 1, 2), ("event", 0, 2, 1), ("event", 1, 1, 1), ("wait_biases",), ("attention", 0),
    ("event", 0, 0, 3), ("projection", 1), ("event", 3, 2, 0), ("event", 1, 1, 2), ("event", 2, 0, 0),
    ("event", 2, 0, 1), ("event", 2, 1, 0), ("event", 2, 1, 1), ("event", 0, 1, 2), ("event", 0, 2, 2),
    ("event", 1, 0, 2), ("event", 1, 0, 3), ("event", 0, 2, 3), ("projection", 3), ("event", 3, 0, 1),
    ("event", 0, 1, 3), ("event", 3, 2, 1), ("event", 3, 2, 2), ("event", 1, 2, 1), ("projection", 2),
    ("event", 2, 1, 2), ("event", 2, 2, 0), ("event", 2, 0, 2), ("event", 3, 0, 2), ("event", 3, 0, 3),
    ("event", 3, 1, 3), ("attention", 1), ("attention", 3), ("event", 3, 2, 3), ("attention", 2), ("second_norm",),
    ("event", 2, 0, 3), ("forth", 1), ("event", 2, 2, 1), ("event", 2, 2, 2), ("event", 2, 1, 3), ("event", 1, 2, 2),
    ("forth", 0), ("back", 0), ("halve", 1, 0), ("halve", 2, 0), ("event", 2, 2, 3), ("event", 1, 1, 3),
    ("event", 1, 2, 3), ("forth", 2), ("back", 2), ("halve", 1, 2), ("forth", 3), ("layer_rows",), ("rows_first", 0),
    ("back", 1), ("add", 1, 0, 2), ("add", 2, 0, 2), ("back", 3), ("second_back",), ("halve", 2, 3), ("out_back", 1),
    ("rows_first", 1), ("halve", 2, 1), ("out_back", 0), ("give", 0), ("out_back", 2), ("give", 2), ("out_back", 3),
    ("give", 1), ("give", 3), ("halve", 3, 0), ("halve", 1, 1), ("add", 3, 0, 2), ("add", 1, 1, 2), ("halve", 1, 3),
    ("add", 1, 2, 2), ("add", 2, 3, 2), ("rows_relay", 0, 0), ("take", 0), ("add", 1, 3, 2), ("add", 2, 1, 2),
    ("take", 1), ("take", 2), ("take", 3), ("add", 1, 2, 1), ("rows_relay", 1, 0), ("halve", 0, 2), ("halve", 2, 2),
    ("source",), ("rows_first", 2), ("settle", 0), ("settle", 3), ("settle", 20), ("add", 2, 3, 1), ("add", 3, 0, 1),
    ("add", 1, 3, 1), ("add", 1, 0, 1), ("rows_relay", 0, 1), ("send_sums",), ("halve", 3, 1), ("add", 3, 1, 2),
    ("add", 2, 0, 1), ("add", 0, 2, 2), ("settle", 1), ("add", 3, 0, 0), ("rows_relay", 1, 1), ("halve", 3, 2),
    ("add", 2, 2, 2), ("add", 2, 3, 0), ("halve", 0, 0), ("add", 1, 3, 0), ("add", 3, 2, 2), ("halve", 0, 1),
    ("add", 3, 1, 1), ("add", 1, 1, 1), ("halve", 3, 3), ("add", 3, 3, 2), ("add", 1, 0, 0), ("halve", 0, 3),
    ("add", 2, 1, 1), ("add", 0, 0, 2), ("add", 1, 2, 0), ("add", 2, 0, 0), ("settle", 2), ("settle", 23),
    ("add", 2, 2, 1), ("rows_relay", 2, 1), ("add", 3, 1, 0), ("add", 1, 1, 0), ("line_over", 1), ("add", 3, 3, 1),
    ("add_sums", 0), ("add", 0, 1, 2), ("add", 0, 2, 1), ("add", 2, 1, 0), ("settle", 22), ("add", 2, 2, 0),
    ("line_over", 2), ("add_sums", 1), ("add", 3, 2, 1), ("rows_first", 3), ("add", 0, 2, 0), ("line_pass", 1),
    ("line_pass", 2), ("add", 0, 3, 2), ("add", 0, 1, 1), ("add", 0, 0, 1), ("rows_relay", 2, 0), ("add_sums", 2),
    ("settle", 5), ("settle", 6), ("settle", 16), ("settle", 17), ("add", 0, 1, 0), ("add", 0, 3, 1),
    ("add", 0, 0, 0), ("add", 3, 3, 0), ("line_end", 1), ("gather", 1, 0), ("add", 3, 2, 0), ("line_end", 2),
    ("gather", 2, 0), ("add", 0, 3, 0), ("settle", 9), ("settle", 10), ("settle", 7), ("gather", 2, 1),
    ("gather", 1, 1), ("rows_relay", 3, 0), ("rows_wait", 2), ("line_end", 3), ("gather", 3, 0), ("rows_relay", 3, 1),
    ("settle", 4), ("line_end", 0), ("gather", 0, 0), ("gather", 2, 2), ("gather", 1, 2), ("gather", 3, 1),
    ("settle", 18), ("settle", 11), ("gather", 0, 1), ("rows_wait", 0), ("settle", 21), ("settle", 8),
    ("gather", 3, 2), ("add_sums", 3), ("store", 2), ("gather", 1, 3), ("rows_wait", 1), ("store", 0),
    ("rows_wait", 3), ("store", 1), ("store", 6), ("gather", 2, 3), ("store", 5), ("store", 4), ("settle", 13),
    ("settle", 14), ("gather", 0, 2), ("store", 3), ("settle", 12), ("settle", 15), ("settle", 19),
)
FIRST_STAGE = (0, 0, 1, 1)
WAYS = (1, 1, 1, 1)


def fused(geo, *refs):
    (
        x_hbm, g_hbm, segs_hbm, n1g_hbm, n1b_hbm, q_hbm, q_bias_hbm, k_hbm, v_hbm, v_bias_hbm, o_hbm, out_bias_hbm,
        n2g_hbm, n2b_hbm, up_hbm, up_bias_hbm, down_hbm, down_bias_hbm,
        out_result, out_source, out_a, out_u, out_d, out_o, out_sums,
        segs, n1g, n1b, q_bias, v_bias, out_bias, n2g, n2b, up_bias, down_bias,
        w_a, w_u, w_d, w_o, extra, x, g2, o_own, n1, q, own, cells, near_send, far_send, near_in, far_in,
        table, bias, probs, mixed, middle, n2, hidden, slope, result, total, g1, d_mixed, d_queries, d_table,
        g1_low, near_give, far_give, near_back, far_back, g_a, g_u, g_d, g_o, sums, gathered, source_all,
        line_a, line_u, line_d, line_o, end_a, end_u, end_d, end_o, in_a, in_u, in_d, in_o, r_a, r_u, r_d, r_o, sums_in, sums_all, sums_got,
        load_sem, small_sem, store_sem, zw_send, zw_recv, pw_send, pw_recv, ex_send, ex_recv, halo_send, halo_recv,
        far_s, far_r, back_send, back_recv, rs_send, rs_recv, zl_send, zl_recv, zx_recv, zy_recv,
        ag_send, ag_recv, gp_send, gp_recv, gc_send, gc_recv, out_send, out_recv, sm_send, sm_recv, sc_send, sc_recv,
        *landings,
    ) = refs
    weights, grads, reduced = (w_a, w_u, w_d, w_o), (g_a, g_u, g_d, g_o), (r_a, r_u, r_d, r_o)
    from_line, from_end, from_inner = (line_a, line_u, line_d, line_o), (end_a, end_u, end_d, end_o), (in_a, in_u, in_d, in_o)
    C, W = geo.ctx, geo.wt
    c, z = lax.axis_index("ctx"), lax.axis_index("wt")
    plane = Plane(C, c, 512)
    B = plane.bits

    loads = [
        pltpu.make_async_copy(q_hbm, weights[0].at[z, :, pl.ds(0, LANES)], load_sem.at[0]),
        pltpu.make_async_copy(k_hbm, weights[0].at[z, :, pl.ds(LANES, LANES)], load_sem.at[1]),
        pltpu.make_async_copy(v_hbm, weights[0].at[z, :, pl.ds(2 * LANES, LANES)], load_sem.at[2]),
        pltpu.make_async_copy(o_hbm, o_own, load_sem.at[3]),
        pltpu.make_async_copy(up_hbm, weights[1].at[z], load_sem.at[4]),
        pltpu.make_async_copy(down_hbm, weights[2].at[z], load_sem.at[5]),
        pltpu.make_async_copy(x_hbm.at[z], x, load_sem.at[6]),
        pltpu.make_async_copy(g_hbm.at[z], g2, load_sem.at[7]),
    ]
    small = [
        pltpu.make_async_copy(source, target, small_sem.at[at])
        for at, (source, target) in enumerate(
            (
                (q_bias_hbm, q_bias), (v_bias_hbm, v_bias), (up_bias_hbm, up_bias), (n1g_hbm, n1g), (n1b_hbm, n1b),
                (segs_hbm, segs), (out_bias_hbm, out_bias), (n2g_hbm, n2g), (n2b_hbm, n2b), (down_bias_hbm, down_bias),
            )
        )
    ]

    for copy in loads + small:
        copy.start()
    near_in[...] = jnp.zeros_like(near_in)
    far_in[...] = jnp.zeros_like(far_in)
    near_back[...] = jnp.zeros_like(near_back)
    far_back[...] = jnp.zeros_like(far_back)

    barrier = pltpu.get_barrier_semaphore()
    for step in range(1, C):
        pl.semaphore_signal(barrier, inc=1, device_id=(lax.rem(c + step, C), z), device_id_type=pl.DeviceIdType.MESH)
    for step in range(1, W):
        pl.semaphore_signal(barrier, inc=1, device_id=(c, lax.rem(z + step, W)), device_id_type=pl.DeviceIdType.MESH)
    sums[...] = jnp.zeros_like(sums)
    extra[z] = jnp.zeros_like(extra[z])
    pl.semaphore_wait(barrier, C + W - 2)

    def order_of(k, w):
        return (k + w) % 2

    relays = W == 4
    inner = (z > 0) & (z < W - 1) if relays else jnp.bool_(False)
    across = jnp.where(z < W // 2, z + 2, z - 2)
    beside = W - 1 - z
    end = jnp.where(z < W // 2, 0, W - 1)
    near_inner = jnp.where(z < W // 2, 1, W - 2)

    def arrival(i, way):
        table_of = []
        for at in range(W):
            seen = []
            for step in range(1, W):
                seen += [w for w in (at - step, at + step) if 0 <= w < W]
            if way == 1 and 0 < at < W - 1:
                seen = [at - 1, at + 2, at + 1] if at < W // 2 else [at + 1, at - 2, at - 1]
            if way == 2 and 0 < at < W - 1:
                seen = [at - 1, at + 1, at + 2] if at < W // 2 else [at + 1, at - 1, at - 2]
            table_of.append(seen[i])
        w = jnp.int32(table_of[0])
        for at in range(1, W):
            w = jnp.where(z == at, table_of[at], w)
        return w

    ways = WAYS if relays else (0, 0, 0, 0)
    first_stage = FIRST_STAGE if B > 2 else (0, 0, 0, 0)
    arrivals_of = [[arrival(i, way) for i in range(W - 1)] for way in ways]
    arrivals = arrivals_of[0]

    def each_direct(action, way):
        for step in range(1, W):
            for to, there in ((z - step, z >= step), (z + step, z + step < W)):
                skip = jnp.bool_(False)
                if way == 1:
                    skip = z + to == W - 1
                if way == 2:
                    skip = (z + to == W - 1) & jnp.logical_not(inner) | inner & (to == across)

                @pl.when(there & jnp.logical_not(skip))
                def _():
                    action(to)

    def weight_line(k, w, to, relayed=False, own=False):
        rows = plane.block(order_of(k, w), first_stage[k])
        slot = jnp.where(w == across, z, across) if relayed else to
        mine = {1: up_hbm, 2: down_hbm}.get(k) if own else None
        return remote(
            weights[k].at[w, rows] if mine is None else mine.at[rows], weights[k].at[w, rows], zw_send.at[k, slot], zw_recv.at[k, w], (c, to)
        )

    def weight_first(k):
        each_direct(lambda to: weight_line(k, z, to, own=True).start(), ways[k])

    def held_at(k, s):
        return [-1, *range(first_stage[k], s)] if s >= first_stage[k] else []

    plane_slots = {}
    for k in range(4):
        for s in range(B):
            for j in held_at(k, s):
                plane_slots[k, j, s] = len(plane_slots)

    def weight_copy(k, w, j, s, landing=False):
        order = order_of(k, w)
        device = plane.partner(order, s)
        seen = device if landing else None
        if j < 0:
            rows = plane.block(order, first_stage[k], device=seen)
        else:
            rows = plane.block(order, j, other=True, device=seen)
        at, rank = plane_slots[k, j, s], lax.rem(w - z + W, W) - 1
        block = weights[k].at[w, rows]
        return remote(block, block, pw_send.at[at, rank], pw_recv.at[at, rank], (device, z))

    def weight_event(k, i, s):
        w = arrivals_of[k][i]
        if s == 0:
            weight_line(k, w, lax.rem(z + 1, W)).wait_recv()
            if i == 1 and ways[k] == 1:

                @pl.when(inner)
                def _():
                    weight_line(k, w, end, True).start()
                    weight_line(k, z, beside, own=True).start()

            if i > 0 and ways[k] == 2:

                @pl.when(inner)
                def _():
                    weight_line(k, w, end, True).start()

            for later in range(first_stage[k], B):
                weight_copy(k, w, -1, later).start()
        else:
            for j in held_at(k, s - 1):
                weight_copy(k, w, j, s - 1, True).wait_recv()
            if s > first_stage[k]:
                for later in range(s, B):
                    weight_copy(k, w, s - 1, later).start()

    def weight_drain(k):
        each_direct(lambda to: weight_line(k, z, to, own=True).wait_send(), ways[k])
        if ways[k]:

            @pl.when(inner)
            def _():
                weight_line(k, across, end, True).wait_send()
                if ways[k] == 1:
                    weight_line(k, z, beside, own=True).wait_send()
                else:
                    weight_line(k, beside, end, True).wait_send()

        for w in arrivals:
            for s in range(B):
                for j in held_at(k, s):
                    weight_copy(k, w, j, s).wait_send()

    def extra_copy(step):
        to = lax.rem(z + step, W)
        return remote(extra.at[z], extra.at[z], ex_send.at[step], ex_recv.at[step], (c, to))

    def extra_from(step):
        source = lax.rem(z + W - step, W)
        return remote(extra.at[source], extra.at[source], ex_send.at[step], ex_recv.at[step], (c, source))

    def halo(w, back):
        if back:
            return remote(near_give.at[w], near_back.at[w], back_send.at[w], back_recv.at[w], (c - 1, z))
        return remote(near_send.at[w], near_in.at[w], halo_send.at[w], halo_recv.at[w], (c + 1, z))

    def needs(source, target):
        need = jnp.bool_(False)
        for step in range(geo.far):
            size = 2 ** (step + 1)
            need = need | (target // size == source // size + 1)
        return need

    def far_copy(w, device, source):
        return remote(far_send.at[w], far_in.at[source, w], far_s.at[device, w], far_r.at[source, w], (device, z))

    def give_copy(w, device, source):
        return remote(
            far_give.at[device, w], far_back.at[source, w], far_s.at[device, w], far_r.at[source, w], (device, z)
        )

    def each_after(action):
        for step in range(1, C):
            device = jnp.minimum(c + step, C - 1)

            @pl.when((c + step < C) & needs(c, device))
            def _():
                action(device)

    def each_before(action):
        for step in range(1, C):
            device = jnp.maximum(c - step, 0)

            @pl.when((c - step >= 0) & needs(device, c))
            def _():
                action(device)

    def halo_start(w):
        @pl.when(c < C - 1)
        def _():
            halo(w, False).start()

        each_after(lambda device: far_copy(w, device, c).start())

    def halo_wait(w):
        @pl.when(c > 0)
        def _():
            halo(w, False).wait_recv()

        each_before(lambda device: far_copy(w, device, device).wait_recv())

    def give_start(w):
        @pl.when(c > 0)
        def _():
            halo(w, True).start()

        each_before(lambda device: give_copy(w, device, c).start())

    def give_wait(w):
        @pl.when(c < C - 1)
        def _():
            halo(w, True).wait_recv()

        each_after(lambda device: give_copy(w, device, device).wait_recv())

    def row_copy(part, w, to, relayed=False):
        rows = (gathered, source_all)[part // 2].at[w, pl.ds(part % 2 * geo.tile, geo.tile)]
        slot = jnp.where(w == across, across, z) if relayed else to
        return remote(rows, rows, out_send.at[part, slot], out_recv.at[part, w], (c, to))

    def rows_first(part):
        each_direct(lambda to: row_copy(part, z, to).start(), 2 if relays else 0)

    def rows_relay(part, far):
        w = across if far else beside

        @pl.when(inner)
        def _():
            row_copy(part, w, end).wait_recv()
            row_copy(part, w, end, True).start()

    def rows_wait(part):
        for step in range(1, W):
            w = lax.rem(z + step, W)

            @pl.when(jnp.logical_not(inner) | (w == end))
            def _():
                row_copy(part, w, w).wait_recv()

    def rows_drain(part):
        each_direct(lambda to: row_copy(part, z, to).wait_send(), 2 if relays else 0)

        @pl.when(inner)
        def _():
            row_copy(part, across, end, True).wait_send()
            row_copy(part, beside, end, True).wait_send()

    def reduce_copy(k, w, s):
        order = order_of(k, w)
        return remote(
            grads[k].at[w, plane.block(order, s, other=True)],
            landings[4 * s + k].at[w],
            rs_send.at[k, w, s],
            rs_recv.at[k, w, s],
            (plane.partner(order, s), z),
        )

    def reduce_add(k, w, s):
        reduce_copy(k, w, s).wait_recv()
        rows = plane.block(order_of(k, w), s)
        grads[k][w, rows] = (grads[k][w, rows].astype(F32) + landings[4 * s + k][w].astype(F32)).astype(BF16)
        if s > 0:
            reduce_copy(k, w, s - 1).start()
        else:
            line_send(k, w)

    def line_copy(k, w, way=None):
        rows = plane.block(order_of(k, w), 0)
        if way == "end":
            return remote(grads[k].at[w, rows], from_end[k], zl_send.at[k, w], zx_recv.at[k], (c, near_inner))
        if way == "inner":
            return remote(grads[k].at[w, rows], from_inner[k], zl_send.at[k, w], zy_recv.at[k], (c, beside))
        return remote(grads[k].at[w, rows], from_line[k].at[z], zl_send.at[k, w], zl_recv.at[k, z], (c, w))

    chained = (False, relays, relays, False)

    def line_send(k, w):
        over = jnp.logical_not(inner) & (w == beside) if chained[k] else jnp.bool_(False)
        waits = inner & ((w == across) | (w == end)) if chained[k] else jnp.bool_(False)

        @pl.when(over)
        def _():
            line_copy(k, w, "end").start()

        @pl.when((w != z) & jnp.logical_not(over | waits))
        def _():
            line_copy(k, w).start()

    def line_add(k, w, landed):
        rows = plane.block(order_of(k, w), 0)
        grads[k][w, rows] = (grads[k][w, rows].astype(F32) + landed[k][...].astype(F32)).astype(BF16)

    def line_over(k):
        @pl.when(inner)
        def _():
            line_copy(k, across, "end").wait_recv()
            line_add(k, across, from_end)
            line_copy(k, across, "inner").start()

    def line_pass(k):
        @pl.when(inner)
        def _():
            line_copy(k, across, "inner").wait_recv()
            line_add(k, end, from_inner)
            line_copy(k, end).start()

    def line_drain(k, w):
        @pl.when(w != z)
        def _():
            line_copy(k, w).wait_send()

    def own_rows(k):
        return plane.block(order_of(k, z), 0)

    def line_end(k):
        rows = own_rows(k)
        total_now = grads[k][z, rows].astype(F32)
        for step in range(1, W):
            source = lax.rem(z + step, W)
            block = from_line[k].at[source]
            comes = inner | (source == near_inner) if chained[k] else jnp.bool_(True)

            @pl.when(comes)
            def _():
                remote(block, block, zl_send.at[k, source], zl_recv.at[k, source], (c, source)).wait_recv()

            total_now = total_now + jnp.where(comes, from_line[k][source].astype(F32), 0.0)
        reduced[k][rows] = total_now.astype(BF16)

    def gather_copy(k, j, s):
        order = order_of(k, z)
        rows = plane.block(order, 0) if j < 0 else plane.block(order, j, other=True)
        at = s * (s + 1) // 2 + j + 1
        block = reduced[k].at[rows]
        return remote(block, block, ag_send.at[k - 1, at], ag_recv.at[k - 1, at], (plane.partner(order, s), z))

    def gather_landing(k, j, s):
        order = order_of(k, z)
        device = plane.partner(order, s)
        rows = plane.block(order, 0, device=device) if j < 0 else plane.block(order, j, other=True, device=device)
        at = s * (s + 1) // 2 + j + 1
        block = reduced[k].at[rows]
        return remote(block, block, ag_send.at[k - 1, at], ag_recv.at[k - 1, at], (device, z))

    def gather_plane(k, offset, landing=False):
        device = plane.flips(2 * offset)
        block = reduced[k].at[plane.block(order_of(k, z), 0, device=device if landing else None)]
        return remote(block, block, gp_send.at[k // 3, offset], gp_recv.at[k // 3, offset], (device, z))

    def gather_core(k, offset, landing=False):
        block = reduced[k].at[plane.block(order_of(k, z), 0, device=plane.flips(2 * offset + int(landing)))]
        return remote(block, block, gc_send.at[k // 3, offset], gc_recv.at[k // 3, offset], (plane.flips(1), z))

    straight = (True, False, False, True)

    def gather_event(k, s):
        if straight[k]:
            offsets = range(1, C // 2) if s < 2 else range(C // 2)
            for offset in offsets:
                if s == 0:
                    gather_plane(k, offset).start()
                elif s == 1:
                    gather_plane(k, offset, True).wait_recv()
                    gather_core(k, offset).start()
                elif s == 2:
                    gather_core(k, offset, True).wait_recv()
            if s == 0:
                gather_core(k, 0).start()
            return
        if s > 0:
            for j in range(-1, s - 1):
                gather_landing(k, j, s - 1).wait_recv()
        for later in range(s, B):
            gather_copy(k, s - 1, later).start()

    def gather_drain(k):
        if straight[k]:
            for offset in range(C // 2):
                if offset:
                    gather_plane(k, offset).wait_send()
                gather_core(k, offset).wait_send()
            return
        for s in range(B):
            for j in range(-1, s):
                gather_copy(k, j, s).wait_send()

    held = {}
    shard_of = [z] + arrivals
    feed_of = [z] + arrivals_of[2]
    turn = [w for step in range((W + 1) // 2) for w in dict.fromkeys((step, W - 1 - step))]

    def send_shards(k):
        for at in {0: (0, 1, 2), 3: (3,)}.get(k, ()):
            loads[at].wait()
        if k == 3:
            weights[3][z] = o_own[...].T
        weight_first(k)

    def send_biases():
        for at in (0, 1, 2):
            small[at].wait()
        extra[z, 0:1, :] = up_bias[...]
        extra[z, 1:2, :LANES] = q_bias[...]
        extra[z, 1:2, LANES : 2 * LANES] = v_bias[...]
        for step in range(1, W):
            extra_copy(step).start()

    def wait_biases():
        for step in range(1, W):
            extra_from(step).wait_recv()

    def first_norm():
        loads[6].wait()
        small[3].wait()
        small[4].wait()
        normed, _ = norm_parts(x[...].astype(F32))
        n1[...] = (normed * n1g[...] + n1b[...]).astype(BF16)

    def masks():
        small[5].wait()
        bias[0] = mask_bias(geo, c, segs[pl.ds(z, 1), :], 0)
        bias[1] = mask_bias(geo, c, segs[pl.ds(z, 1), :], 1)
        held["pick"] = far_matrix(geo, c)

    def projection(i):
        w = shard_of[i]
        project(w, n1, weights, extra, q, own, cells, near_send, far_send)
        halo_start(w)

    def attention(i):
        w = shard_of[i]
        halo_wait(w)
        tables(geo, w, held["pick"], own, cells, near_in, far_in, table)
        for tile in (0, 1):
            attend(geo, w, tile, q, table, bias, probs, mixed)

    def event(k, i, s):
        for stage in {0: [0], 1: [1], 2: range(2, B), 3: [B]}[s]:
            weight_event(k, i, stage)

    def second_norm():
        for at in (4, 5, 7):
            loads[at].wait()
        for at in range(6, 10):
            small[at].wait()
        acc = x[...].astype(F32) + out_bias[...]
        for w in range(W):
            acc = acc + dot_nt(mixed[w], weights[3][w])
        middle[...] = acc
        normed, _ = norm_parts(acc)
        n2[...] = (normed * n2g[...] + n2b[...]).astype(BF16)
        result[...] = acc + down_bias[...]

    def forth(i):
        feed(feed_of[i], n2, weights, extra, hidden, slope, result)

    def layer_rows():
        gathered[z] = result[...].astype(BF16)

    def back(i):
        first = "total" not in held
        held["total"] = True
        feed_back(first, feed_of[i], g2, weights, n2, hidden, slope, sums, grads, total)

    def shard(k, i):
        return feed_of[i] if k in (1, 2) else turn[i]

    def halve(k, i):
        reduce_copy(k, shard(k, i), B - 1).start()

    def add(k, i, s):
        for stage in {2: [B - 1], 1: range(B - 2, 0, -1), 0: [0]}[s]:
            reduce_add(k, shard(k, i), stage)

    def second_back():
        hat, inverse = norm_parts(middle[...])
        d_normed = total[...]
        wide = g2[...].astype(F32)
        first = wide + norm_backward(d_normed, hat, inverse, n2g[...])
        g1[...] = first
        g1_low[...] = first.astype(BF16)
        put_sums(geo, sums, 2, jnp.sum(first, axis=0, keepdims=True))
        put_sums(geo, sums, 3, jnp.sum(d_normed * hat, axis=0, keepdims=True))
        put_sums(geo, sums, 4, jnp.sum(d_normed, axis=0, keepdims=True))
        put_sums(geo, sums, 5, jnp.sum(wide, axis=0, keepdims=True))
        del held["total"]

    def out_back(i):
        w = turn[i]
        d_mixed[w] = dot_nn(g1_low[...], weights[3][w]).astype(BF16)
        grads[3][w] = dot_tn(g1_low[...], mixed[w]).astype(BF16)

    def give(i):
        w = turn[i]
        for tile in (0, 1):
            attend_back(geo, w, tile, q, table, probs, d_mixed, d_queries, d_table)
        return_cells(geo, w, held["pick"], d_table, near_give, far_give)
        give_start(w)

    def take(i):
        w = turn[i]
        give_wait(w)
        first = "total" not in held
        held["total"] = True
        project_back(geo, first, w, weights, n1, d_queries, d_table, near_back, far_back, sums, grads, total)

    def source():
        normed, inverse = norm_parts(x[...].astype(F32))
        d_normed = total[...]
        source_all[z] = (g1[...] + norm_backward(d_normed, normed, inverse, n1g[...])).astype(BF16)
        put_sums(geo, sums, 0, jnp.sum(d_normed * normed, axis=0, keepdims=True))
        put_sums(geo, sums, 1, jnp.sum(d_normed, axis=0, keepdims=True))

    def sums_copy(step):
        to = lax.rem(z + step, W)
        return remote(sums.at[to], sums_in.at[step], sm_send.at[step], sm_recv.at[step], (c, to))

    def sums_stage(s):
        return remote(sums_all.at[s], sums_got.at[s], sc_send.at[s], sc_recv.at[s], (plane.flip(1 << s), z))

    def send_sums():
        for step in range(1, W):
            sums_copy(step).start()

    def add_sums(s):
        if s == 0:
            total_sums = sums[z]
            for step in range(1, W):
                sums_copy(step).wait_recv()
                total_sums = total_sums + sums_in[step]
            sums_all[0] = total_sums
            sums_stage(0).start()
        for stage in {0: [], 1: [0], 2: range(1, B - 1), 3: [B - 1]}[s]:
            sums_stage(stage).wait_recv()
            sums_all[stage + 1] = sums_all[stage] + sums_got[stage]
            if stage + 1 < B:
                sums_stage(stage + 1).start()

    def gather(k, s):
        for stage in {0: [0], 1: [1], 2: range(2, B), 3: [B]}[s]:
            gather_event(k, stage)

    stores = [
        pltpu.make_async_copy(gathered, out_result, store_sem.at[0]),
        pltpu.make_async_copy(source_all, out_source, store_sem.at[1]),
        pltpu.make_async_copy(sums_all.at[B], out_sums, store_sem.at[2]),
        pltpu.make_async_copy(r_a, out_a, store_sem.at[3]),
        pltpu.make_async_copy(r_u, out_u, store_sem.at[4]),
        pltpu.make_async_copy(r_d, out_d, store_sem.at[5]),
        pltpu.make_async_copy(r_o, out_o, store_sem.at[6]),
    ]

    def store(i):
        stores[i].start()

    def reduce_drain(k):
        for w in range(W):
            for s in range(B):
                reduce_copy(k, w, s).wait_send()

    def lines_drain(k):
        for w in range(W):
            line_drain(k, w)

    def settle(group):
        if group < 4:
            weight_drain(group)
        elif group < 8:
            reduce_drain(group - 4)
        elif group < 12:
            lines_drain(group - 8)
        elif group < 16:
            gather_drain(group - 12)
        elif group < 20:
            rows_drain(group - 16)
        elif group == 20:
            for step in range(1, W):
                extra_copy(step).wait_send()
        elif group == 21:
            for step in range(1, W):
                sums_copy(step).wait_send()
            for s in range(B):
                sums_stage(s).wait_send()
        else:
            for w in range(W):
                if group == 22:

                    @pl.when(c < C - 1)
                    def _():
                        halo(w, False).wait_send()

                    each_after(lambda device: far_copy(w, device, c).wait_send())
                else:

                    @pl.when(c > 0)
                    def _():
                        halo(w, True).wait_send()

                    each_before(lambda device: give_copy(w, device, c).wait_send())

    steps = {
        step.__name__: step
        for step in (
            send_shards, send_biases, wait_biases, first_norm, masks, projection, attention, event, second_norm, forth,
            layer_rows, back, halve, add, second_back, out_back, give, take, source, send_sums, add_sums, gather, store,
            rows_first, rows_relay, rows_wait, line_over, line_pass, line_end, settle,
        )
    }
    for name, *args in SCHEDULE:
        steps[name](*args)

    for copy in stores:
        copy.wait()


def unpack(
    result_in, source_in, a_in, u_in, d_in, o_in, sums_in,
    result_out, source_out, d_n1g, d_n1b, d_q, d_qb, d_k, d_v, d_vb, d_o, d_ob, d_n2g, d_n2b, d_up, d_upb, d_down, d_db,
    result, source, a, u, d, o, sums, result_f, source_f, a_f, o_f, u_f, d_f, row_f, load_sem, store_sem,
):
    runs = result.shape[0]
    pairs = [(result_in.at[m], result.at[m]) for m in range(runs)] + [(source_in.at[m], source.at[m]) for m in range(runs)]
    pairs += [(a_in, a), (u_in, u), (d_in, d), (o_in, o), (sums_in, sums)]
    loads = [pltpu.make_async_copy(*pair, load_sem.at[at]) for at, pair in enumerate(pairs)]
    for copy in loads:
        copy.start()
    stores = []

    def put(held, target):
        copy = pltpu.make_async_copy(held, target, store_sem.at[len(stores)])
        copy.start()
        stores.append(copy)

    for m in range(runs):
        loads[m].wait()
        result_f[m] = result[m].astype(F32)
        put(result_f.at[m], result_out.at[m])
    for m in range(runs):
        loads[runs + m].wait()
        source_f[m] = source[m].astype(F32)
        put(source_f.at[m], source_out.at[m])
    loads[2 * runs].wait()
    for at, target in enumerate((d_q, d_k, d_v)):
        a_f[at] = a[:, at * LANES : (at + 1) * LANES].astype(F32)
        put(a_f.at[at], target)
    loads[2 * runs + 1].wait()
    u_f[...] = u[...].astype(F32)
    put(u_f, d_up)
    loads[2 * runs + 2].wait()
    d_f[...] = d[...].astype(F32)
    put(d_f, d_down)
    loads[2 * runs + 3].wait()
    o_f[...] = o[...].astype(F32).T
    put(o_f, d_o)
    loads[2 * runs + 4].wait()
    for at, target in enumerate((d_n1g, d_n1b, d_ob, d_n2g, d_n2b, d_db)):
        row, lane = 2 + at // 4, at % 4 * LANES
        row_f[at, :, :LANES] = sums[row : row + 1, lane : lane + LANES]
        put(row_f.at[at, :, pl.ds(0, LANES)], target)
    for at, target in ((6, d_qb), (7, d_vb)):
        row_f[at, :, :LANES] = sums[1:2, (at - 6) * LANES : (at - 5) * LANES]
        put(row_f.at[at, :, pl.ds(0, LANES)], target)
    row_f[8] = sums[0:1, :]
    put(row_f.at[8], d_upb)
    for copy in stores:
        copy.wait()


def shards(
    x_in,
    grad_out,
    seg_ids,
    norm1_gain,
    norm1_bias,
    q_weight,
    q_bias,
    k_weight,
    v_weight,
    v_bias,
    out_weight,
    out_bias,
    norm2_gain,
    norm2_bias,
    up_weight,
    up_bias,
    down_weight,
    down_bias,
):
    C, W = lax.axis_size("ctx"), lax.axis_size("wt")
    runs, T, width = x_in.shape
    hidden = up_weight.shape[1]
    geo = Geometry(C, W, T)
    S, B = geo.slots, C.bit_length() - 1
    each = width // C
    assert runs == W and hidden == width and q_weight.shape[1] == LANES and T == 256
    sds = jax.ShapeDtypeStruct
    vmem, dma = pltpu.VMEM, pltpu.SemaphoreType.DMA
    row = lambda v: v.reshape(1, -1)
    pair = 2 * LANES
    wide_of = (3 * LANES, hidden, width, LANES)
    slots = sum(1 + s - f for f in (FIRST_STAGE if B > 2 else (0,) * 4) for s in range(f, B))
    scratch = [
        vmem(seg_ids.shape, jnp.int32),
        *[vmem((1, n), F32) for n in (width, width, LANES, LANES, width, width, width, hidden, width)],
        *[vmem((W, width, n), BF16) for n in wide_of],
        vmem((W, 8, width), F32),
        vmem((T, width), BF16),
        vmem((T, width), BF16),
        vmem((LANES, width), BF16),
        vmem((T, width), BF16),
        vmem((W, T, LANES), BF16),
        vmem((W, T, pair), BF16),
        vmem((W, 224, pair), BF16),
        vmem((W, 80, pair), BF16),
        vmem((W, 16, pair), BF16),
        vmem((W, 80, pair), BF16),
        vmem((C, W, 16, pair), BF16),
        vmem((W, 2, S, pair), BF16),
        vmem((2, S, geo.tile), F32),
        vmem((W, 2, S, pair), BF16),
        vmem((W, T, LANES), BF16),
        vmem((T, width), F32),
        vmem((T, width), BF16),
        vmem((W, T, hidden), BF16),
        vmem((W, T, hidden), F32),
        vmem((T, width), F32),
        vmem((T, width), F32),
        vmem((T, width), F32),
        vmem((W, T, LANES), BF16),
        vmem((W, T, LANES), BF16),
        vmem((W, 2, S, pair), F32),
        vmem((T, width), BF16),
        vmem((W, 80, pair), BF16),
        vmem((C, W, 16, pair), BF16),
        vmem((W, 80, pair), BF16),
        vmem((C, W, 16, pair), BF16),
        *[vmem((W, width, n), BF16) for n in wide_of],
        vmem((W, 8, width), F32),
        vmem((W, T, width), BF16),
        vmem((W, T, width), BF16),
        *[vmem((W, each, n), BF16) for n in wide_of],
        *[vmem((each, n), BF16) for n in wide_of],
        *[vmem((each, n), BF16) for n in wide_of],
        *[vmem((width, n), BF16) for n in wide_of],
        vmem((W, 8, width), F32),
        vmem((B + 1, 8, width), F32),
        vmem((B, 8, width), F32),
        dma((8,)),
        dma((10,)),
        dma((7,)),
        dma((4, W)),
        dma((4, W)),
        dma((slots, W - 1)),
        dma((slots, W - 1)),
        dma((W,)),
        dma((W,)),
        dma((W,)),
        dma((W,)),
        dma((C, W)),
        dma((C, W)),
        dma((W,)),
        dma((W,)),
        dma((4, W, B)),
        dma((4, W, B)),
        dma((4, W)),
        dma((4, W)),
        dma((4,)),
        dma((4,)),
        dma((2, B * (B + 1) // 2)),
        dma((2, B * (B + 1) // 2)),
        dma((2, C // 2)),
        dma((2, C // 2)),
        dma((2, C // 2)),
        dma((2, C // 2)),
        dma((4, W)),
        dma((4, W)),
        dma((W,)),
        dma((W,)),
        dma((B,)),
        dma((B,)),
    ] + [vmem((W, each * 2**s, n), BF16) for s in range(B) for n in wide_of]
    far = pl.BlockSpec(memory_space=pl.ANY)
    result, source, d_a, d_u, d_d, d_o, sums = pl.pallas_call(
        functools.partial(fused, geo),
        name="fused",
        out_shape=[sds((W, T, width), BF16), sds((W, T, width), BF16), *[sds((width, n), BF16) for n in wide_of], sds((8, width), F32)],
        in_specs=[far] * 18,
        out_specs=[far] * 7,
        scratch_shapes=scratch,
        compiler_params=pltpu.CompilerParams(collective_id=0, has_side_effects=True, vmem_limit_bytes=58 * 2**20),
    )(
        x_in, grad_out, seg_ids, row(norm1_gain), row(norm1_bias), q_weight, row(q_bias), k_weight, v_weight, row(v_bias),
        out_weight, row(out_bias), row(norm2_gain), row(norm2_bias), up_weight, row(up_bias), down_weight, row(down_bias),
    )
    one, thin, full = (1, LANES), (width, LANES), (width, width)
    shapes = [(W, T, width)] * 2 + [one, one, thin, one, thin, thin, one, (LANES, width), one, one, one, full, (1, hidden), full, one]
    values = pl.pallas_call(
        unpack,
        name="unpack",
        out_shape=[sds(shape, F32) for shape in shapes],
        in_specs=[far] * 7,
        out_specs=[far] * 17,
        scratch_shapes=[
            vmem((W, T, width), BF16),
            vmem((W, T, width), BF16),
            *[vmem((width, n), BF16) for n in wide_of],
            vmem((8, width), F32),
            vmem((W, T, width), F32),
            vmem((W, T, width), F32),
            vmem((3, width, LANES), F32),
            vmem((LANES, width), F32),
            vmem(full, F32),
            vmem(full, F32),
            vmem((9, 1, hidden), F32),
            dma((2 * W + 5,)),
            dma((2 * W + 15,)),
        ],
        compiler_params=pltpu.CompilerParams(vmem_limit_bytes=58 * 2**20),
    )(result, source, d_a, d_u, d_d, d_o, sums)
    return tuple(v.reshape(-1) if v.shape[0] == 1 else v for v in values)


def solution(mesh):
    in_specs = (
        P(None, "ctx", None),
        P(None, "ctx", None),
        P(),
        P(),
        P(),
        P(None, "wt"),
        P("wt"),
        P(None, "wt"),
        P(None, "wt"),
        P("wt"),
        P("wt", None),
        P(),
        P(),
        P(),
        P(None, "wt"),
        P("wt"),
        P("wt", None),
        P(),
    )
    out_specs = (
        P(None, "ctx", None),
        P(None, "ctx", None),
        P("wt"),
        P("wt"),
        P(None, "wt"),
        P("wt"),
        P(None, "wt"),
        P(None, "wt"),
        P("wt"),
        P("wt", None),
        P("wt"),
        P("wt"),
        P("wt"),
        P(None, "wt"),
        P("wt"),
        P("wt", None),
        P("wt"),
    )
    return jax.shard_map(shards, mesh=mesh, in_specs=in_specs, out_specs=out_specs, check_vma=False)
```

```python
import functools

import jax
import jax.numpy as jnp
from jax import lax
from jax.experimental import pallas as pl
from jax.experimental.pallas import tpu as pltpu
from jax.sharding import PartitionSpec as P

HEAD_DIM = 64
BLOCK = 16
LEVELS = 10
FINE = 3
EPSILON = 1e-05
NEGATIVE = -1e30
LOG_TWO = 0.6931471805599453
LANES = 128
BF16 = jnp.bfloat16
F32 = jnp.float32


def dot(left, right, dims):
    return lax.dot_general(left, right, (dims, ((), ())), preferred_element_type=F32)


def dot_nn(left, right):
    return dot(left, right, ((1,), (0,)))


def dot_nt(left, right):
    return dot(left, right, ((1,), (1,)))


def dot_tn(left, right):
    return dot(left, right, ((0,), (0,)))


def norm_parts(source):
    centre = jnp.mean(source, axis=-1, keepdims=True)
    centred = source - centre
    variance = jnp.mean(centred * centred, axis=-1, keepdims=True)
    inverse = lax.rsqrt(variance + EPSILON)
    return centred * inverse, inverse


def norm_backward(upstream, normed, inverse, gain):
    scaled = upstream * gain
    first_mean = jnp.mean(scaled, axis=-1, keepdims=True)
    second_mean = jnp.mean(scaled * normed, axis=-1, keepdims=True)
    return inverse * (scaled - first_mean - normed * second_mean)


def iota(shape, axis):
    return lax.broadcasted_iota(jnp.int32, shape, axis)


class Geometry:
    def __init__(self, ctx, wt, tok_dev):
        self.ctx, self.wt, self.tok_dev = ctx, wt, tok_dev
        tokens = ctx * tok_dev
        self.levels = len([l for l in range(LEVELS) if BLOCK * 2**l < tokens])
        self.own_cells = [tok_dev // 2**l if l <= FINE else 0 for l in range(self.levels)]
        self.tile = tok_dev // 2
        self.tile_slots = [BLOCK + self.tile] + [BLOCK * 4 >> (l - 1) if l < FINE else BLOCK for l in range(1, self.levels)]
        self.slots = sum(self.tile_slots)
        self.slot_at = [sum(self.tile_slots[:l]) for l in range(self.levels + 1)]
        self.far = self.levels - (FINE + 2)
        self.near = FINE + 2


def pool_matrix():
    parts = []
    for level, count in ((1, 128), (2, 64), (3, 32)):
        hit = (iota((count, 256), 1) >> level) == iota((count, 256), 0)
        parts.append(jnp.where(hit, 1.0 / 2**level, 0.0))
    return jnp.concatenate(parts, axis=0).astype(BF16)


def coarse_matrix():
    row, column = iota((32, 32), 0), iota((32, 32), 1)
    out = jnp.zeros((32, 32), F32)
    first = 0
    for level, count in ((4, 16), (5, 8), (6, 4), (7, 2), (8, 1)):
        up = level - FINE
        hit = (row >= first) & (row < first + count) & ((column >> up) == row - first)
        out = jnp.where(hit, 1.0 / 2**up, out)
        first += count
    return out.astype(BF16)


def far_matrix(geo, me):
    parts = []
    first = 0
    for step in range(geo.far):
        up = step + 1
        each = BLOCK >> up
        row, column = iota((BLOCK, geo.ctx * BLOCK), 0), iota((BLOCK, geo.ctx * BLOCK), 1)
        group = (me >> up) - 1
        device = (group << up) + (row >> (4 - up))
        wanted = device * BLOCK + first + (row & (each - 1))
        parts.append(jnp.where((column == wanted) & (group >= 0), 1.0, 0.0))
        first += each
    return jnp.concatenate(parts, axis=0).astype(BF16)


def mask_bias(geo, me, segs, tile):
    first_pos = me * geo.tok_dev + tile * geo.tile
    seg_one = jnp.sum((segs < 1).astype(jnp.int32), axis=1, keepdims=True)
    seg_two = jnp.sum((segs < 2).astype(jnp.int32), axis=1, keepdims=True)
    position = first_pos + iota((1, geo.tile), 1)
    begins = jnp.where(position >= seg_two, seg_two, jnp.where(position >= seg_one, seg_one, 0))
    parts = []
    for level in range(geo.levels):
        size, shift = 2**level, level + 4
        count = geo.tile_slots[level]
        span = BLOCK * size
        if level <= FINE:
            base = first_pos - span
        else:
            base = (((me * geo.tok_dev) >> shift) - 1) << shift
        begin = base + size * iota((count, geo.tile), 0)
        lower = jnp.maximum(((position >> shift) - 1) << shift, begins)
        if level == 0:
            upper = position + 1
        else:
            upper = ((position >> (shift - 1)) - 1) << (shift - 1)
        valid = (begin >= lower) & (begin + size <= upper)
        parts.append(jnp.where(valid, level * LOG_TWO, NEGATIVE))
    return jnp.concatenate(parts, axis=0)


def both_heads(pair):
    lane = iota(pair.shape, 1)
    zero = jnp.zeros_like(pair)
    return jnp.concatenate([jnp.where(lane < HEAD_DIM, pair, zero), jnp.where(lane >= HEAD_DIM, pair, zero)], axis=0)


def own_lanes(stacked):
    rows = stacked.shape[0] // 2
    lane = iota((rows, stacked.shape[1]), 1)
    return jnp.where(lane < HEAD_DIM, stacked[:rows], stacked[rows:])


def project(w, n1, weights, extra, q, own, cells, near, far):
    out = dot_nn(n1[...], weights[0][w])
    bias = extra[w, 1:2, :]
    q[w] = ((out[:, :LANES] + bias[:, :LANES]).astype(BF16) * 0.125).astype(BF16)
    kv = jnp.concatenate(
        [out[:, LANES : 2 * LANES], out[:, 2 * LANES :] + bias[:, LANES : 2 * LANES]], axis=1
    ).astype(BF16)
    own[w] = kv
    fine = dot_nn(pool_matrix(), kv).astype(BF16)
    cells[w] = fine
    rough = dot_nn(coarse_matrix(), fine[192:224]).astype(BF16)
    near[w, 0:16] = kv[240:256]
    near[w, 16:32] = fine[112:128]
    near[w, 32:48] = fine[176:192]
    near[w, 48:64] = fine[208:224]
    near[w, 64:80] = rough[0:16]
    far[w] = rough[16:32]


def tables(geo, w, pick, own, cells, near_in, far_in, table):
    blocks = far_in[:, w].reshape(geo.ctx * BLOCK, 2 * LANES)
    rough = dot_nn(pick, blocks).astype(BF16)
    at = geo.slot_at
    table[w, 0, 0:16] = near_in[w, 0:16]
    table[w, 0, 16:144] = own[w, 0:128]
    table[w, 1, 0:144] = own[w, 112:256]
    table[w, 0, at[1] : at[1] + 16] = near_in[w, 16:32]
    table[w, 0, at[1] + 16 : at[2]] = cells[w, 0:48]
    table[w, 1, at[1] : at[2]] = cells[w, 48:112]
    table[w, 0, at[2] : at[2] + 16] = near_in[w, 32:48]
    table[w, 0, at[2] + 16 : at[3]] = cells[w, 128:144]
    table[w, 1, at[2] : at[3]] = cells[w, 144:176]
    table[w, 0, at[3] : at[4]] = near_in[w, 48:64]
    table[w, 1, at[3] : at[4]] = cells[w, 192:208]
    for tile in (0, 1):
        table[w, tile, at[4] : at[5]] = near_in[w, 64:80]
        table[w, tile, at[5] :] = rough


def attend(geo, w, tile, q, table, bias, probs, mixed):
    rows = slice(tile * geo.tile, (tile + 1) * geo.tile)
    both = both_heads(q[w, rows, :])
    level_bias = bias[tile]
    scores = dot_nt(table[w, tile, :, :LANES], both)
    scores = scores + jnp.concatenate([level_bias, level_bias], axis=1)
    top = jnp.max(scores, axis=0, keepdims=True)
    exponent = jnp.exp(scores - top)
    total = jnp.sum(exponent, axis=0, keepdims=True)
    low = (exponent * (1.0 / total)).astype(BF16)
    probs[w, tile] = low
    mixed[w, rows, :] = own_lanes(dot_tn(low, table[w, tile, :, LANES:])).astype(BF16)


def attend_back(geo, w, tile, q, table, probs, d_mixed, d_queries, d_table):
    rows = slice(tile * geo.tile, (tile + 1) * geo.tile)
    both = both_heads(q[w, rows, :])
    d_both = both_heads(d_mixed[w, rows, :])
    low = probs[w, tile]
    d_probs = dot_nt(table[w, tile, :, LANES:], d_both)
    wide = low.astype(F32)
    product = wide * d_probs
    centre = jnp.sum(product, axis=0, keepdims=True)
    d_scores = (product - wide * centre).astype(BF16)
    d_table[w, tile, :, :LANES] = dot_nn(d_scores, both)
    d_table[w, tile, :, LANES:] = dot_nn(low, d_both)
    back = own_lanes(dot_tn(d_scores, table[w, tile, :, :LANES]))
    d_queries[w, rows, :] = (back * 0.125).astype(BF16)


def return_cells(geo, w, pick, d_table, near, far):
    at = geo.slot_at
    near[w, 0:16] = d_table[w, 0, 0:16].astype(BF16)
    near[w, 16:32] = d_table[w, 0, at[1] : at[1] + 16].astype(BF16)
    near[w, 32:48] = d_table[w, 0, at[2] : at[2] + 16].astype(BF16)
    near[w, 48:64] = d_table[w, 0, at[3] : at[4]].astype(BF16)
    near[w, 64:80] = (d_table[w, 0, at[4] : at[5]] + d_table[w, 1, at[4] : at[5]]).astype(BF16)
    rough = (d_table[w, 0, at[5] :] + d_table[w, 1, at[5] :]).astype(BF16)
    far[:, w] = dot_tn(pick, rough).astype(BF16).reshape(geo.ctx, BLOCK, 2 * LANES)


def own_gradients(geo, w, d_table, near_back, far_back):
    at = geo.slot_at
    first, second = d_table.at[w, 0], d_table.at[w, 1]
    back = near_back[w].astype(F32)
    tokens = jnp.concatenate(
        [first[16:128], first[128:144] + second[0:16], second[16:128], second[128:144] + back[0:16]], axis=0
    )
    far = jnp.sum(far_back[:, w].astype(F32), axis=0)
    rough = jnp.concatenate([back[64:80], far], axis=0)
    fine = dot_tn(coarse_matrix(), rough.astype(BF16))
    level3 = jnp.concatenate([second[at[3] : at[4]], back[48:64]], axis=0) + fine
    cells = jnp.concatenate(
        [
            first[at[1] + 16 : at[2]],
            second[at[1] : at[2]],
            back[16:32],
            first[at[2] + 16 : at[3]],
            second[at[2] : at[3]],
            back[32:48],
            level3,
        ],
        axis=0,
    )
    return tokens + dot_tn(pool_matrix(), cells.astype(BF16))


def feed(w, n2, weights, extra, hidden, slope, result):
    pre = dot_nn(n2[...], weights[1][w]) + extra[w, 0:1, :]
    gate = jax.nn.sigmoid(pre)
    hidden[w] = (pre * gate).astype(BF16)
    slope[w] = gate * (1.0 + pre * (1.0 - gate))
    result[...] += dot_nn(hidden[w], weights[2][w])


def feed_back(first, w, g2, weights, n2, hidden, slope, sums, grads, total):
    d_hidden = dot_nt(g2[...], weights[2][w]).astype(BF16).astype(F32)
    d_up = (d_hidden * slope[w]).astype(BF16)
    sums[w, 0:1, :] = jnp.sum(d_up.astype(F32), axis=0, keepdims=True)
    grads[2][w] = dot_tn(hidden[w], g2[...]).astype(BF16)
    grads[1][w] = dot_tn(n2[...], d_up).astype(BF16)
    part = dot_nt(d_up, weights[1][w])
    total[...] = part if first else total[...] + part


def put_sums(geo, sums, column, row):
    at, lanes = 2 + column // 4, slice(column % 4 * LANES, (column % 4 + 1) * LANES)
    for w in range(geo.wt):
        sums[w, at : at + 1, lanes] = row[:, w * LANES : (w + 1) * LANES]


def project_back(geo, first, w, weights, n1, d_queries, d_table, near_back, far_back, sums, grads, total):
    kv = own_gradients(geo, w, d_table, near_back, far_back).astype(BF16)
    d_qkv = jnp.concatenate([d_queries[w], kv], axis=1)
    sums[w, 1:2, :LANES] = jnp.sum(d_qkv[:, :LANES].astype(F32), axis=0, keepdims=True)
    sums[w, 1:2, LANES : 2 * LANES] = jnp.sum(d_qkv[:, 2 * LANES :].astype(F32), axis=0, keepdims=True)
    grads[0][w] = dot_tn(n1[...], d_qkv).astype(BF16)
    part = dot_nt(d_qkv, weights[0][w])
    total[...] = part if first else total[...] + part


def remote(source, target, sent, landed, device):
    return pltpu.make_async_remote_copy(source, target, sent, landed, device_id=device, device_id_type=pl.DeviceIdType.MESH)


class Plane:
    def __init__(self, ctx, c, rows):
        self.ctx, self.c = ctx, c
        self.bits = ctx.bit_length() - 1
        self.each = rows // ctx
        plane_bits = self.bits - 1
        half = plane_bits // 2
        self.plane_bits, self.half = plane_bits, half
        self.places = self.places_of(c)
        self.masks = (
            [2 << s for s in range(plane_bits)] + [1],
            [2 << (s + half) % plane_bits for s in range(plane_bits)] + [1],
        )

    def places_of(self, device):
        plane, core = device // 2, device % 2
        turned = plane // 2**self.half + plane % 2**self.half * 2 ** (self.plane_bits - self.half)
        top = core * 2**self.plane_bits
        return plane + top, turned + top

    def place(self, order, device=None):
        places = self.places if device is None else self.places_of(device)
        if isinstance(order, int):
            return places[order]
        return jnp.where(order == 0, places[0], places[1])

    def partner(self, order, stage):
        if isinstance(order, int):
            return self.flip(self.masks[order][stage])
        return jnp.where(order == 0, self.flip(self.masks[0][stage]), self.flip(self.masks[1][stage]))

    def flip(self, mask):
        return self.c + mask * (1 - 2 * (self.c // mask % 2))

    def flips(self, bits):
        device = self.c
        for s in range(self.bits):
            if bits >> s & 1:
                device = device + (1 << s) * (1 - 2 * (self.c // (1 << s) % 2))
        return device

    def block(self, order, stage, other=False, device=None):
        index = self.place(order, device) // 2**stage
        if other:
            index = index + 1 - 2 * (index % 2)
        size = self.each * 2**stage
        return pl.ds(pl.multiple_of(index * size, size), size)


SCHEDULE = (
    ("send_shards", 0), ("first_norm",), ("send_shards", 1), ("send_shards", 3), ("event", 0, 0, 0),
    ("event", 0, 1, 0), ("event", 1, 0, 0), ("event", 0, 0, 1), ("event", 3, 0, 0), ("send_biases",),
    ("projection", 0), ("event", 1, 1, 0), ("event", 0, 2, 0), ("event", 3, 1, 0), ("event", 3, 1, 1), ("masks",),
    ("event", 1, 0, 1), ("send_shards", 2), ("event", 0, 0, 2), ("event", 1, 2, 0), ("event", 0, 1, 1),
    ("event", 3, 1, 2), ("event", 0, 2, 1), ("event", 1, 1, 1), ("wait_biases",), ("attention", 0),
    ("event", 0, 0, 3), ("projection", 1), ("event", 3, 2, 0), ("event", 1, 1, 2), ("event", 2, 0, 0),
    ("event", 2, 0, 1), ("event", 2, 1, 0), ("event", 2, 1, 1), ("event", 0, 1, 2), ("event", 0, 2, 2),
    ("event", 1, 0, 2), ("event", 1, 0, 3), ("event", 0, 2, 3), ("projection", 3), ("event", 3, 0, 1),
    ("event", 0, 1, 3), ("event", 3, 2, 1), ("event", 3, 2, 2), ("event", 1, 2, 1), ("projection", 2),
    ("event", 2, 1, 2), ("event", 2, 2, 0), ("event", 2, 0, 2), ("event", 3, 0, 2), ("event", 3, 0, 3),
    ("event", 3, 1, 3), ("attention", 1), ("attention", 3), ("event", 3, 2, 3), ("attention", 2), ("second_norm",),
    ("event", 2, 0, 3), ("forth", 1), ("event", 2, 2, 1), ("event", 2, 2, 2), ("event", 2, 1, 3), ("event", 1, 2, 2),
    ("forth", 0), ("back", 0), ("halve", 1, 0), ("halve", 2, 0), ("event", 2, 2, 3), ("event", 1, 1, 3),
    ("event", 1, 2, 3), ("forth", 2), ("back", 2), ("halve", 1, 2), ("forth", 3), ("layer_rows",), ("rows_first", 0),
    ("back", 1), ("add", 1, 0, 2), ("add", 2, 0, 2), ("back", 3), ("second_back",), ("halve", 2, 3), ("out_back", 1),
    ("rows_first", 1), ("halve", 2, 1), ("out_back", 0), ("give", 0), ("out_back", 2), ("give", 2), ("out_back", 3),
    ("give", 1), ("give", 3), ("halve", 3, 0), ("halve", 1, 1), ("add", 3, 0, 2), ("add", 1, 1, 2), ("halve", 1, 3),
    ("add", 1, 2, 2), ("add", 2, 3, 2), ("rows_relay", 0, 0), ("take", 0), ("add", 1, 3, 2), ("add", 2, 1, 2),
    ("take", 1), ("take", 2), ("take", 3), ("add", 1, 2, 1), ("rows_relay", 1, 0), ("halve", 0, 2), ("halve", 2, 2),
    ("source",), ("rows_first", 2), ("settle", 0), ("settle", 3), ("settle", 20), ("add", 2, 3, 1), ("add", 3, 0, 1),
    ("add", 1, 3, 1), ("add", 1, 0, 1), ("rows_relay", 0, 1), ("send_sums",), ("halve", 3, 1), ("add", 3, 1, 2),
    ("add", 2, 0, 1), ("add", 0, 2, 2), ("settle", 1), ("add", 3, 0, 0), ("rows_relay", 1, 1), ("halve", 3, 2),
    ("add", 2, 2, 2), ("add", 2, 3, 0), ("halve", 0, 0), ("add", 1, 3, 0), ("add", 3, 2, 2), ("halve", 0, 1),
    ("add", 3, 1, 1), ("add", 1, 1, 1), ("halve", 3, 3), ("add", 3, 3, 2), ("add", 1, 0, 0), ("halve", 0, 3),
    ("add", 2, 1, 1), ("add", 0, 0, 2), ("add", 1, 2, 0), ("add", 2, 0, 0), ("settle", 2), ("settle", 23),
    ("add", 2, 2, 1), ("rows_relay", 2, 1), ("add", 3, 1, 0), ("add", 1, 1, 0), ("line_over", 1), ("add", 3, 3, 1),
    ("add_sums", 0), ("add", 0, 1, 2), ("add", 0, 2, 1), ("add", 2, 1, 0), ("settle", 22), ("add", 2, 2, 0),
    ("line_over", 2), ("add_sums", 1), ("add", 3, 2, 1), ("rows_first", 3), ("add", 0, 2, 0), ("line_pass", 1),
    ("line_pass", 2), ("add", 0, 3, 2), ("add", 0, 1, 1), ("add", 0, 0, 1), ("rows_relay", 2, 0), ("add_sums", 2),
    ("settle", 5), ("settle", 6), ("settle", 16), ("settle", 17), ("add", 0, 1, 0), ("add", 0, 3, 1),
    ("add", 0, 0, 0), ("add", 3, 3, 0), ("line_end", 1), ("gather", 1, 0), ("add", 3, 2, 0), ("line_end", 2),
    ("gather", 2, 0), ("add", 0, 3, 0), ("settle", 9), ("settle", 10), ("settle", 7), ("gather", 2, 1),
    ("gather", 1, 1), ("rows_relay", 3, 0), ("rows_wait", 2), ("line_end", 3), ("gather", 3, 0), ("rows_relay", 3, 1),
    ("settle", 4), ("line_end", 0), ("gather", 0, 0), ("gather", 2, 2), ("gather", 1, 2), ("gather", 3, 1),
    ("settle", 18), ("settle", 11), ("gather", 0, 1), ("rows_wait", 0), ("settle", 21), ("settle", 8),
    ("gather", 3, 2), ("add_sums", 3), ("store", 2), ("gather", 1, 3), ("rows_wait", 1), ("store", 0),
    ("rows_wait", 3), ("store", 1), ("store", 6), ("gather", 2, 3), ("store", 5), ("store", 4), ("settle", 13),
    ("settle", 14), ("gather", 0, 2), ("store", 3), ("settle", 12), ("settle", 15), ("settle", 19),
)
FIRST_STAGE = (0, 0, 1, 1)
WAYS = (1, 1, 1, 1)


def fused(geo, *refs):
    (
        x_hbm, g_hbm, segs_hbm, n1g_hbm, n1b_hbm, q_hbm, q_bias_hbm, k_hbm, v_hbm, v_bias_hbm, o_hbm, out_bias_hbm,
        n2g_hbm, n2b_hbm, up_hbm, up_bias_hbm, down_hbm, down_bias_hbm,
        out_result, out_source, out_a, out_u, out_d, out_o, out_sums,
        segs, n1g, n1b, q_bias, v_bias, out_bias, n2g, n2b, up_bias, down_bias,
        w_a, w_u, w_d, w_o, extra, x, g2, o_own, n1, q, own, cells, near_send, far_send, near_in, far_in,
        table, bias, probs, mixed, middle, n2, hidden, slope, result, total, g1, d_mixed, d_queries, d_table,
        g1_low, near_give, far_give, near_back, far_back, g_a, g_u, g_d, g_o, sums, gathered, source_all,
        line_a, line_u, line_d, line_o, end_a, end_u, end_d, end_o, in_a, in_u, in_d, in_o, r_a, r_u, r_d, r_o, sums_in, sums_all, sums_got,
        load_sem, small_sem, store_sem, zw_send, zw_recv, pw_send, pw_recv, ex_send, ex_recv, halo_send, halo_recv,
        far_s, far_r, back_send, back_recv, rs_send, rs_recv, zl_send, zl_recv, zx_recv, zy_recv,
        ag_send, ag_recv, gp_send, gp_recv, gc_send, gc_recv, out_send, out_recv, sm_send, sm_recv, sc_send, sc_recv,
        *landings,
    ) = refs
    weights, grads, reduced = (w_a, w_u, w_d, w_o), (g_a, g_u, g_d, g_o), (r_a, r_u, r_d, r_o)
    from_line, from_end, from_inner = (line_a, line_u, line_d, line_o), (end_a, end_u, end_d, end_o), (in_a, in_u, in_d, in_o)
    C, W = geo.ctx, geo.wt
    c, z = lax.axis_index("ctx"), lax.axis_index("wt")
    plane = Plane(C, c, 512)
    B = plane.bits

    loads = [
        pltpu.make_async_copy(q_hbm, weights[0].at[z, :, pl.ds(0, LANES)], load_sem.at[0]),
        pltpu.make_async_copy(k_hbm, weights[0].at[z, :, pl.ds(LANES, LANES)], load_sem.at[1]),
        pltpu.make_async_copy(v_hbm, weights[0].at[z, :, pl.ds(2 * LANES, LANES)], load_sem.at[2]),
        pltpu.make_async_copy(o_hbm, o_own, load_sem.at[3]),
        pltpu.make_async_copy(up_hbm, weights[1].at[z], load_sem.at[4]),
        pltpu.make_async_copy(down_hbm, weights[2].at[z], load_sem.at[5]),
        pltpu.make_async_copy(x_hbm.at[z], x, load_sem.at[6]),
        pltpu.make_async_copy(g_hbm.at[z], g2, load_sem.at[7]),
    ]
    small = [
        pltpu.make_async_copy(source, target, small_sem.at[at])
        for at, (source, target) in enumerate(
            (
                (q_bias_hbm, q_bias), (v_bias_hbm, v_bias), (up_bias_hbm, up_bias), (n1g_hbm, n1g), (n1b_hbm, n1b),
                (segs_hbm, segs), (out_bias_hbm, out_bias), (n2g_hbm, n2g), (n2b_hbm, n2b), (down_bias_hbm, down_bias),
            )
        )
    ]

    for copy in loads + small:
        copy.start()
    near_in[...] = jnp.zeros_like(near_in)
    far_in[...] = jnp.zeros_like(far_in)
    near_back[...] = jnp.zeros_like(near_back)
    far_back[...] = jnp.zeros_like(far_back)

    barrier = pltpu.get_barrier_semaphore()
    for step in range(1, C):
        pl.semaphore_signal(barrier, inc=1, device_id=(lax.rem(c + step, C), z), device_id_type=pl.DeviceIdType.MESH)
    for step in range(1, W):
        pl.semaphore_signal(barrier, inc=1, device_id=(c, lax.rem(z + step, W)), device_id_type=pl.DeviceIdType.MESH)
    sums[...] = jnp.zeros_like(sums)
    extra[z] = jnp.zeros_like(extra[z])
    pl.semaphore_wait(barrier, C + W - 2)

    def order_of(k, w):
        return (k + w) % 2

    def sent(block, semaphore):
        pltpu.make_async_copy(block, block, semaphore).wait()

    relays = W == 4
    inner = (z > 0) & (z < W - 1) if relays else jnp.bool_(False)
    across = jnp.where(z < W // 2, z + 2, z - 2)
    beside = W - 1 - z
    end = jnp.where(z < W // 2, 0, W - 1)
    near_inner = jnp.where(z < W // 2, 1, W - 2)

    def arrival(i, way):
        table_of = []
        for at in range(W):
            seen = []
            for step in range(1, W):
                seen += [w for w in (at - step, at + step) if 0 <= w < W]
            if way == 1 and 0 < at < W - 1:
                seen = [at - 1, at + 2, at + 1] if at < W // 2 else [at + 1, at - 2, at - 1]
            if way == 2 and 0 < at < W - 1:
                seen = [at - 1, at + 1, at + 2] if at < W // 2 else [at + 1, at - 1, at - 2]
            table_of.append(seen[i])
        w = jnp.int32(table_of[0])
        for at in range(1, W):
            w = jnp.where(z == at, table_of[at], w)
        return w

    ways = WAYS if relays else (0, 0, 0, 0)
    first_stage = FIRST_STAGE if B > 2 else (0, 0, 0, 0)
    arrivals_of = [[arrival(i, way) for i in range(W - 1)] for way in ways]
    arrivals = arrivals_of[0]

    def each_direct(action, way):
        for step in range(1, W):
            for to, there in ((z - step, z >= step), (z + step, z + step < W)):
                skip = jnp.bool_(False)
                if way == 1:
                    skip = z + to == W - 1
                if way == 2:
                    skip = (z + to == W - 1) & jnp.logical_not(inner) | inner & (to == across)

                @pl.when(there & jnp.logical_not(skip))
                def _():
                    action(to)

    def weight_line(k, w, to, relayed=False, own=False):
        rows = plane.block(order_of(k, w), first_stage[k])
        slot = jnp.where(w == across, z, across) if relayed else to
        mine = {1: up_hbm, 2: down_hbm}.get(k) if own else None
        return remote(
            weights[k].at[w, rows] if mine is None else mine.at[rows], weights[k].at[w, rows], zw_send.at[k, slot], zw_recv.at[k, w], (c, to)
        )

    def weight_first(k):
        each_direct(lambda to: weight_line(k, z, to, own=True).start(), ways[k])

    def held_at(k, s):
        return [-1, *range(first_stage[k], s)] if s >= first_stage[k] else []

    plane_slots = {}
    for k in range(4):
        for s in range(B):
            for j in held_at(k, s):
                plane_slots[k, j, s] = len(plane_slots)

    def weight_copy(k, w, j, s, landing=False):
        order = order_of(k, w)
        device = plane.partner(order, s)
        seen = device if landing else None
        if j < 0:
            rows = plane.block(order, first_stage[k], device=seen)
        else:
            rows = plane.block(order, j, other=True, device=seen)
        at, rank = plane_slots[k, j, s], lax.rem(w - z + W, W) - 1
        block = weights[k].at[w, rows]
        return remote(block, block, pw_send.at[k], pw_recv.at[at, rank], (device, z))

    def weight_event(k, i, s):
        w = arrivals_of[k][i]
        if s == 0:
            weight_line(k, w, lax.rem(z + 1, W)).wait_recv()
            if i == 1 and ways[k] == 1:

                @pl.when(inner)
                def _():
                    weight_line(k, w, end, True).start()
                    weight_line(k, z, beside, own=True).start()

            if i > 0 and ways[k] == 2:

                @pl.when(inner)
                def _():
                    weight_line(k, w, end, True).start()

            for later in range(first_stage[k], B):
                weight_copy(k, w, -1, later).start()
        else:
            for j in held_at(k, s - 1):
                weight_copy(k, w, j, s - 1, True).wait_recv()
            if s > first_stage[k]:
                for later in range(s, B):
                    weight_copy(k, w, s - 1, later).start()

    def weight_drain(k):
        each_direct(lambda to: weight_line(k, z, to, own=True).wait_send(), ways[k])
        if ways[k]:

            @pl.when(inner)
            def _():
                weight_line(k, across, end, True).wait_send()
                if ways[k] == 1:
                    weight_line(k, z, beside, own=True).wait_send()
                else:
                    weight_line(k, beside, end, True).wait_send()

        sent(weights[k].at[pl.ds(0, W - 1), pl.ds(0, plane.each * (C - 2 ** first_stage[k]))], pw_send.at[k])

    def extra_copy(step):
        to = lax.rem(z + step, W)
        return remote(extra.at[z], extra.at[z], ex_send.at[step], ex_recv.at[step], (c, to))

    def extra_from(step):
        source = lax.rem(z + W - step, W)
        return remote(extra.at[source], extra.at[source], ex_send.at[step], ex_recv.at[step], (c, source))

    def halo(w, back):
        if back:
            return remote(near_give.at[w], near_back.at[w], back_send.at[w], back_recv.at[w], (c - 1, z))
        return remote(near_send.at[w], near_in.at[w], halo_send.at[w], halo_recv.at[w], (c + 1, z))

    def needs(source, target):
        need = jnp.bool_(False)
        for step in range(geo.far):
            size = 2 ** (step + 1)
            need = need | (target // size == source // size + 1)
        return need

    def far_copy(w, device, source):
        return remote(far_send.at[w], far_in.at[source, w], far_s.at[device, w], far_r.at[source, w], (device, z))

    def give_copy(w, device, source):
        return remote(
            far_give.at[device, w], far_back.at[source, w], far_s.at[device, w], far_r.at[source, w], (device, z)
        )

    def each_after(action):
        for step in range(1, C):
            device = jnp.minimum(c + step, C - 1)

            @pl.when((c + step < C) & needs(c, device))
            def _():
                action(device)

    def each_before(action):
        for step in range(1, C):
            device = jnp.maximum(c - step, 0)

            @pl.when((c - step >= 0) & needs(device, c))
            def _():
                action(device)

    def halo_start(w):
        @pl.when(c < C - 1)
        def _():
            halo(w, False).start()

        each_after(lambda device: far_copy(w, device, c).start())

    def halo_wait(w):
        @pl.when(c > 0)
        def _():
            halo(w, False).wait_recv()

        each_before(lambda device: far_copy(w, device, device).wait_recv())

    def give_start(w):
        @pl.when(c > 0)
        def _():
            halo(w, True).start()

        each_before(lambda device: give_copy(w, device, c).start())

    def give_wait(w):
        @pl.when(c < C - 1)
        def _():
            halo(w, True).wait_recv()

        each_after(lambda device: give_copy(w, device, device).wait_recv())

    def row_copy(part, w, to, relayed=False):
        rows = (gathered, source_all)[part // 2].at[w, pl.ds(part % 2 * geo.tile, geo.tile)]
        slot = jnp.where(w == across, across, z) if relayed else to
        return remote(rows, rows, out_send.at[part, slot], out_recv.at[part, w], (c, to))

    def rows_first(part):
        each_direct(lambda to: row_copy(part, z, to).start(), 2 if relays else 0)

    def rows_relay(part, far):
        w = across if far else beside

        @pl.when(inner)
        def _():
            row_copy(part, w, end).wait_recv()
            row_copy(part, w, end, True).start()

    def rows_wait(part):
        for step in range(1, W):
            w = lax.rem(z + step, W)

            @pl.when(jnp.logical_not(inner) | (w == end))
            def _():
                row_copy(part, w, w).wait_recv()

    def rows_drain(part):
        each_direct(lambda to: row_copy(part, z, to).wait_send(), 2 if relays else 0)

        @pl.when(inner)
        def _():
            row_copy(part, across, end, True).wait_send()
            row_copy(part, beside, end, True).wait_send()

    def reduce_copy(k, w, s):
        order = order_of(k, w)
        return remote(
            grads[k].at[w, plane.block(order, s, other=True)],
            landings[4 * s + k].at[w],
            rs_send.at[k],
            rs_recv.at[k, w, s],
            (plane.partner(order, s), z),
        )

    def reduce_add(k, w, s):
        reduce_copy(k, w, s).wait_recv()
        rows = plane.block(order_of(k, w), s)
        grads[k][w, rows] = (grads[k][w, rows].astype(F32) + landings[4 * s + k][w].astype(F32)).astype(BF16)
        if s > 0:
            reduce_copy(k, w, s - 1).start()
        else:
            line_send(k, w)

    def line_copy(k, w, way=None):
        rows = plane.block(order_of(k, w), 0)
        if way == "end":
            return remote(grads[k].at[w, rows], from_end[k], zl_send.at[k], zx_recv.at[k], (c, near_inner))
        if way == "inner":
            return remote(grads[k].at[w, rows], from_inner[k], zl_send.at[k], zy_recv.at[k], (c, beside))
        return remote(grads[k].at[w, rows], from_line[k].at[z], zl_send.at[k], zl_recv.at[k, z], (c, w))

    chained = (False, relays, relays, False)

    def line_send(k, w):
        over = jnp.logical_not(inner) & (w == beside) if chained[k] else jnp.bool_(False)
        waits = inner & ((w == across) | (w == end)) if chained[k] else jnp.bool_(False)

        @pl.when(over)
        def _():
            line_copy(k, w, "end").start()

        @pl.when((w != z) & jnp.logical_not(over | waits))
        def _():
            line_copy(k, w).start()

    def line_add(k, w, landed):
        rows = plane.block(order_of(k, w), 0)
        grads[k][w, rows] = (grads[k][w, rows].astype(F32) + landed[k][...].astype(F32)).astype(BF16)

    def line_over(k):
        @pl.when(inner)
        def _():
            line_copy(k, across, "end").wait_recv()
            line_add(k, across, from_end)
            line_copy(k, across, "inner").start()

    def line_pass(k):
        @pl.when(inner)
        def _():
            line_copy(k, across, "inner").wait_recv()
            line_add(k, end, from_inner)
            line_copy(k, end).start()

    def own_rows(k):
        return plane.block(order_of(k, z), 0)

    def line_end(k):
        rows = own_rows(k)
        total_now = grads[k][z, rows].astype(F32)
        for step in range(1, W):
            source = lax.rem(z + step, W)
            block = from_line[k].at[source]
            comes = inner | (source == near_inner) if chained[k] else jnp.bool_(True)

            @pl.when(comes)
            def _():
                remote(block, block, zl_send.at[k], zl_recv.at[k, source], (c, source)).wait_recv()

            total_now = total_now + jnp.where(comes, from_line[k][source].astype(F32), 0.0)
        reduced[k][rows] = total_now.astype(BF16)

    def gather_copy(k, j, s):
        order = order_of(k, z)
        rows = plane.block(order, 0) if j < 0 else plane.block(order, j, other=True)
        at = s * (s + 1) // 2 + j + 1
        block = reduced[k].at[rows]
        return remote(block, block, ag_send.at[k - 1], ag_recv.at[k - 1, at], (plane.partner(order, s), z))

    def gather_landing(k, j, s):
        order = order_of(k, z)
        device = plane.partner(order, s)
        rows = plane.block(order, 0, device=device) if j < 0 else plane.block(order, j, other=True, device=device)
        at = s * (s + 1) // 2 + j + 1
        block = reduced[k].at[rows]
        return remote(block, block, ag_send.at[k - 1], ag_recv.at[k - 1, at], (device, z))

    def gather_plane(k, offset, landing=False):
        device = plane.flips(2 * offset)
        block = reduced[k].at[plane.block(order_of(k, z), 0, device=device if landing else None)]
        return remote(block, block, gp_send.at[k // 3], gp_recv.at[k // 3, offset], (device, z))

    def gather_core(k, offset, landing=False):
        block = reduced[k].at[plane.block(order_of(k, z), 0, device=plane.flips(2 * offset + int(landing)))]
        return remote(block, block, gc_send.at[k // 3], gc_recv.at[k // 3, offset], (plane.flips(1), z))

    straight = (True, False, False, True)

    def gather_event(k, s):
        if straight[k]:
            offsets = range(1, C // 2) if s < 2 else range(C // 2)
            for offset in offsets:
                if s == 0:
                    gather_plane(k, offset).start()
                elif s == 1:
                    gather_plane(k, offset, True).wait_recv()
                    gather_core(k, offset).start()
                elif s == 2:
                    gather_core(k, offset, True).wait_recv()
            if s == 0:
                gather_core(k, 0).start()
            return
        if s > 0:
            for j in range(-1, s - 1):
                gather_landing(k, j, s - 1).wait_recv()
        for later in range(s, B):
            gather_copy(k, s - 1, later).start()

    def gather_drain(k):
        if straight[k]:
            sent(reduced[k].at[pl.ds(0, plane.each * (C // 2 - 1))], gp_send.at[k // 3])
            sent(reduced[k].at[pl.ds(0, plane.each * (C // 2))], gc_send.at[k // 3])
        else:
            sent(reduced[k].at[pl.ds(0, plane.each * (C - 1))], ag_send.at[k - 1])

    held = {}
    shard_of = [z] + arrivals
    feed_of = [z] + arrivals_of[2]
    turn = [w for step in range((W + 1) // 2) for w in dict.fromkeys((step, W - 1 - step))]

    def send_shards(k):
        for at in {0: (0, 1, 2), 3: (3,)}.get(k, ()):
            loads[at].wait()
        if k == 3:
            weights[3][z] = o_own[...].T
        weight_first(k)

    def send_biases():
        for at in (0, 1, 2):
            small[at].wait()
        extra[z, 0:1, :] = up_bias[...]
        extra[z, 1:2, :LANES] = q_bias[...]
        extra[z, 1:2, LANES : 2 * LANES] = v_bias[...]
        for step in range(1, W):
            extra_copy(step).start()

    def wait_biases():
        for step in range(1, W):
            extra_from(step).wait_recv()

    def first_norm():
        loads[6].wait()
        small[3].wait()
        small[4].wait()
        normed, _ = norm_parts(x[...].astype(F32))
        n1[...] = (normed * n1g[...] + n1b[...]).astype(BF16)

    def masks():
        small[5].wait()
        bias[0] = mask_bias(geo, c, segs[pl.ds(z, 1), :], 0)
        bias[1] = mask_bias(geo, c, segs[pl.ds(z, 1), :], 1)
        held["pick"] = far_matrix(geo, c)

    def projection(i):
        w = shard_of[i]
        project(w, n1, weights, extra, q, own, cells, near_send, far_send)
        halo_start(w)

    def attention(i):
        w = shard_of[i]
        halo_wait(w)
        tables(geo, w, held["pick"], own, cells, near_in, far_in, table)
        for tile in (0, 1):
            attend(geo, w, tile, q, table, bias, probs, mixed)

    def event(k, i, s):
        for stage in {0: [0], 1: [1], 2: range(2, B), 3: [B]}[s]:
            weight_event(k, i, stage)

    def second_norm():
        for at in (4, 5, 7):
            loads[at].wait()
        for at in range(6, 10):
            small[at].wait()
        acc = x[...].astype(F32) + out_bias[...]
        for w in range(W):
            acc = acc + dot_nt(mixed[w], weights[3][w])
        middle[...] = acc
        normed, _ = norm_parts(acc)
        n2[...] = (normed * n2g[...] + n2b[...]).astype(BF16)
        result[...] = acc + down_bias[...]

    def forth(i):
        feed(feed_of[i], n2, weights, extra, hidden, slope, result)

    def layer_rows():
        gathered[z] = result[...].astype(BF16)

    def back(i):
        first = "total" not in held
        held["total"] = True
        feed_back(first, feed_of[i], g2, weights, n2, hidden, slope, sums, grads, total)

    def shard(k, i):
        return feed_of[i] if k in (1, 2) else turn[i]

    def halve(k, i):
        reduce_copy(k, shard(k, i), B - 1).start()

    def add(k, i, s):
        for stage in {2: [B - 1], 1: range(B - 2, 0, -1), 0: [0]}[s]:
            reduce_add(k, shard(k, i), stage)

    def second_back():
        hat, inverse = norm_parts(middle[...])
        d_normed = total[...]
        wide = g2[...].astype(F32)
        first = wide + norm_backward(d_normed, hat, inverse, n2g[...])
        g1[...] = first
        g1_low[...] = first.astype(BF16)
        put_sums(geo, sums, 2, jnp.sum(first, axis=0, keepdims=True))
        put_sums(geo, sums, 3, jnp.sum(d_normed * hat, axis=0, keepdims=True))
        put_sums(geo, sums, 4, jnp.sum(d_normed, axis=0, keepdims=True))
        put_sums(geo, sums, 5, jnp.sum(wide, axis=0, keepdims=True))
        del held["total"]

    def out_back(i):
        w = turn[i]
        d_mixed[w] = dot_nn(g1_low[...], weights[3][w]).astype(BF16)
        grads[3][w] = dot_tn(g1_low[...], mixed[w]).astype(BF16)

    def give(i):
        w = turn[i]
        for tile in (0, 1):
            attend_back(geo, w, tile, q, table, probs, d_mixed, d_queries, d_table)
        return_cells(geo, w, held["pick"], d_table, near_give, far_give)
        give_start(w)

    def take(i):
        w = turn[i]
        give_wait(w)
        first = "total" not in held
        held["total"] = True
        project_back(geo, first, w, weights, n1, d_queries, d_table, near_back, far_back, sums, grads, total)

    def source():
        normed, inverse = norm_parts(x[...].astype(F32))
        d_normed = total[...]
        source_all[z] = (g1[...] + norm_backward(d_normed, normed, inverse, n1g[...])).astype(BF16)
        put_sums(geo, sums, 0, jnp.sum(d_normed * normed, axis=0, keepdims=True))
        put_sums(geo, sums, 1, jnp.sum(d_normed, axis=0, keepdims=True))

    def sums_copy(step):
        to = lax.rem(z + step, W)
        return remote(sums.at[to], sums_in.at[step], sm_send.at[step], sm_recv.at[step], (c, to))

    def sums_stage(s):
        return remote(sums_all.at[s], sums_got.at[s], sc_send.at[s], sc_recv.at[s], (plane.flip(1 << s), z))

    def send_sums():
        for step in range(1, W):
            sums_copy(step).start()

    def add_sums(s):
        if s == 0:
            total_sums = sums[z]
            for step in range(1, W):
                sums_copy(step).wait_recv()
                total_sums = total_sums + sums_in[step]
            sums_all[0] = total_sums
            sums_stage(0).start()
        for stage in {0: [], 1: [0], 2: range(1, B - 1), 3: [B - 1]}[s]:
            sums_stage(stage).wait_recv()
            sums_all[stage + 1] = sums_all[stage] + sums_got[stage]
            if stage + 1 < B:
                sums_stage(stage + 1).start()

    def gather(k, s):
        for stage in {0: [0], 1: [1], 2: range(2, B), 3: [B]}[s]:
            gather_event(k, stage)

    stores = [
        pltpu.make_async_copy(gathered, out_result, store_sem.at[0]),
        pltpu.make_async_copy(source_all, out_source, store_sem.at[1]),
        pltpu.make_async_copy(sums_all.at[B], out_sums, store_sem.at[2]),
        pltpu.make_async_copy(r_a, out_a, store_sem.at[3]),
        pltpu.make_async_copy(r_u, out_u, store_sem.at[4]),
        pltpu.make_async_copy(r_d, out_d, store_sem.at[5]),
        pltpu.make_async_copy(r_o, out_o, store_sem.at[6]),
    ]

    def store(i):
        stores[i].start()

    def reduce_drain(k):
        sent(grads[k].at[:, pl.ds(0, plane.each * (C - 1))], rs_send.at[k])

    def lines_drain(k):
        sent(reduced[k].at[pl.ds(0, plane.each * (W - 1))], zl_send.at[k])

    def settle(group):
        if group < 4:
            weight_drain(group)
        elif group < 8:
            reduce_drain(group - 4)
        elif group < 12:
            lines_drain(group - 8)
        elif group < 16:
            gather_drain(group - 12)
        elif group < 20:
            rows_drain(group - 16)
        elif group == 20:
            for step in range(1, W):
                extra_copy(step).wait_send()
        elif group == 21:
            for step in range(1, W):
                sums_copy(step).wait_send()
            for s in range(B):
                sums_stage(s).wait_send()
        else:
            for w in range(W):
                if group == 22:

                    @pl.when(c < C - 1)
                    def _():
                        halo(w, False).wait_send()

                    each_after(lambda device: far_copy(w, device, c).wait_send())
                else:

                    @pl.when(c > 0)
                    def _():
                        halo(w, True).wait_send()

                    each_before(lambda device: give_copy(w, device, c).wait_send())

    steps = {
        step.__name__: step
        for step in (
            send_shards, send_biases, wait_biases, first_norm, masks, projection, attention, event, second_norm, forth,
            layer_rows, back, halve, add, second_back, out_back, give, take, source, send_sums, add_sums, gather, store,
            rows_first, rows_relay, rows_wait, line_over, line_pass, line_end, settle,
        )
    }
    for name, *args in SCHEDULE:
        steps[name](*args)

    for copy in stores:
        copy.wait()


def unpack(
    result_in, source_in, a_in, u_in, d_in, o_in, sums_in,
    result_out, source_out, d_n1g, d_n1b, d_q, d_qb, d_k, d_v, d_vb, d_o, d_ob, d_n2g, d_n2b, d_up, d_upb, d_down, d_db,
    result, source, a, u, d, o, sums, result_f, source_f, a_f, o_f, u_f, d_f, row_f, load_sem, store_sem,
):
    runs = result.shape[0]
    pairs = [(result_in.at[m], result.at[m]) for m in range(runs)] + [(source_in.at[m], source.at[m]) for m in range(runs)]
    pairs += [(a_in, a), (u_in, u), (d_in, d), (o_in, o), (sums_in, sums)]
    loads = [pltpu.make_async_copy(*pair, load_sem.at[at]) for at, pair in enumerate(pairs)]
    for copy in loads:
        copy.start()
    stores = []

    def put(held, target):
        copy = pltpu.make_async_copy(held, target, store_sem.at[len(stores)])
        copy.start()
        stores.append(copy)

    for m in range(runs):
        loads[m].wait()
        result_f[m] = result[m].astype(F32)
        put(result_f.at[m], result_out.at[m])
    for m in range(runs):
        loads[runs + m].wait()
        source_f[m] = source[m].astype(F32)
        put(source_f.at[m], source_out.at[m])
    loads[2 * runs].wait()
    for at, target in enumerate((d_q, d_k, d_v)):
        a_f[at] = a[:, at * LANES : (at + 1) * LANES].astype(F32)
        put(a_f.at[at], target)
    loads[2 * runs + 1].wait()
    u_f[...] = u[...].astype(F32)
    put(u_f, d_up)
    loads[2 * runs + 2].wait()
    d_f[...] = d[...].astype(F32)
    put(d_f, d_down)
    loads[2 * runs + 3].wait()
    o_f[...] = o[...].astype(F32).T
    put(o_f, d_o)
    loads[2 * runs + 4].wait()
    for at, target in enumerate((d_n1g, d_n1b, d_ob, d_n2g, d_n2b, d_db)):
        row, lane = 2 + at // 4, at % 4 * LANES
        row_f[at, :, :LANES] = sums[row : row + 1, lane : lane + LANES]
        put(row_f.at[at, :, pl.ds(0, LANES)], target)
    for at, target in ((6, d_qb), (7, d_vb)):
        row_f[at, :, :LANES] = sums[1:2, (at - 6) * LANES : (at - 5) * LANES]
        put(row_f.at[at, :, pl.ds(0, LANES)], target)
    row_f[8] = sums[0:1, :]
    put(row_f.at[8], d_upb)
    for copy in stores:
        copy.wait()


def shards(
    x_in,
    grad_out,
    seg_ids,
    norm1_gain,
    norm1_bias,
    q_weight,
    q_bias,
    k_weight,
    v_weight,
    v_bias,
    out_weight,
    out_bias,
    norm2_gain,
    norm2_bias,
    up_weight,
    up_bias,
    down_weight,
    down_bias,
):
    C, W = lax.axis_size("ctx"), lax.axis_size("wt")
    runs, T, width = x_in.shape
    hidden = up_weight.shape[1]
    geo = Geometry(C, W, T)
    S, B = geo.slots, C.bit_length() - 1
    each = width // C
    assert runs == W and hidden == width and q_weight.shape[1] == LANES and T == 256
    sds = jax.ShapeDtypeStruct
    vmem, dma = pltpu.VMEM, pltpu.SemaphoreType.DMA
    row = lambda v: v.reshape(1, -1)
    pair = 2 * LANES
    wide_of = (3 * LANES, hidden, width, LANES)
    slots = sum(1 + s - f for f in (FIRST_STAGE if B > 2 else (0,) * 4) for s in range(f, B))
    scratch = [
        vmem(seg_ids.shape, jnp.int32),
        *[vmem((1, n), F32) for n in (width, width, LANES, LANES, width, width, width, hidden, width)],
        *[vmem((W, width, n), BF16) for n in wide_of],
        vmem((W, 8, width), F32),
        vmem((T, width), BF16),
        vmem((T, width), BF16),
        vmem((LANES, width), BF16),
        vmem((T, width), BF16),
        vmem((W, T, LANES), BF16),
        vmem((W, T, pair), BF16),
        vmem((W, 224, pair), BF16),
        vmem((W, 80, pair), BF16),
        vmem((W, 16, pair), BF16),
        vmem((W, 80, pair), BF16),
        vmem((C, W, 16, pair), BF16),
        vmem((W, 2, S, pair), BF16),
        vmem((2, S, geo.tile), F32),
        vmem((W, 2, S, pair), BF16),
        vmem((W, T, LANES), BF16),
        vmem((T, width), F32),
        vmem((T, width), BF16),
        vmem((W, T, hidden), BF16),
        vmem((W, T, hidden), F32),
        vmem((T, width), F32),
        vmem((T, width), F32),
        vmem((T, width), F32),
        vmem((W, T, LANES), BF16),
        vmem((W, T, LANES), BF16),
        vmem((W, 2, S, pair), F32),
        vmem((T, width), BF16),
        vmem((W, 80, pair), BF16),
        vmem((C, W, 16, pair), BF16),
        vmem((W, 80, pair), BF16),
        vmem((C, W, 16, pair), BF16),
        *[vmem((W, width, n), BF16) for n in wide_of],
        vmem((W, 8, width), F32),
        vmem((W, T, width), BF16),
        vmem((W, T, width), BF16),
        *[vmem((W, each, n), BF16) for n in wide_of],
        *[vmem((each, n), BF16) for n in wide_of],
        *[vmem((each, n), BF16) for n in wide_of],
        *[vmem((width, n), BF16) for n in wide_of],
        vmem((W, 8, width), F32),
        vmem((B + 1, 8, width), F32),
        vmem((B, 8, width), F32),
        dma((8,)),
        dma((10,)),
        dma((7,)),
        dma((4, W)),
        dma((4, W)),
        dma((4,)),
        dma((slots, W - 1)),
        dma((W,)),
        dma((W,)),
        dma((W,)),
        dma((W,)),
        dma((C, W)),
        dma((C, W)),
        dma((W,)),
        dma((W,)),
        dma((4,)),
        dma((4, W, B)),
        dma((4,)),
        dma((4, W)),
        dma((4,)),
        dma((4,)),
        dma((2,)),
        dma((2, B * (B + 1) // 2)),
        dma((2,)),
        dma((2, C // 2)),
        dma((2,)),
        dma((2, C // 2)),
        dma((4, W)),
        dma((4, W)),
        dma((W,)),
        dma((W,)),
        dma((B,)),
        dma((B,)),
    ] + [vmem((W, each * 2**s, n), BF16) for s in range(B) for n in wide_of]
    far = pl.BlockSpec(memory_space=pl.ANY)
    result, source, d_a, d_u, d_d, d_o, sums = pl.pallas_call(
        functools.partial(fused, geo),
        name="fused",
        out_shape=[sds((W, T, width), BF16), sds((W, T, width), BF16), *[sds((width, n), BF16) for n in wide_of], sds((8, width), F32)],
        in_specs=[far] * 18,
        out_specs=[far] * 7,
        scratch_shapes=scratch,
        compiler_params=pltpu.CompilerParams(collective_id=0, has_side_effects=True, vmem_limit_bytes=58 * 2**20),
    )(
        x_in, grad_out, seg_ids, row(norm1_gain), row(norm1_bias), q_weight, row(q_bias), k_weight, v_weight, row(v_bias),
        out_weight, row(out_bias), row(norm2_gain), row(norm2_bias), up_weight, row(up_bias), down_weight, row(down_bias),
    )
    one, thin, full = (1, LANES), (width, LANES), (width, width)
    shapes = [(W, T, width)] * 2 + [one, one, thin, one, thin, thin, one, (LANES, width), one, one, one, full, (1, hidden), full, one]
    values = pl.pallas_call(
        unpack,
        name="unpack",
        out_shape=[sds(shape, F32) for shape in shapes],
        in_specs=[far] * 7,
        out_specs=[far] * 17,
        scratch_shapes=[
            vmem((W, T, width), BF16),
            vmem((W, T, width), BF16),
            *[vmem((width, n), BF16) for n in wide_of],
            vmem((8, width), F32),
            vmem((W, T, width), F32),
            vmem((W, T, width), F32),
            vmem((3, width, LANES), F32),
            vmem((LANES, width), F32),
            vmem(full, F32),
            vmem(full, F32),
            vmem((9, 1, hidden), F32),
            dma((2 * W + 5,)),
            dma((2 * W + 15,)),
        ],
        compiler_params=pltpu.CompilerParams(vmem_limit_bytes=58 * 2**20),
    )(result, source, d_a, d_u, d_d, d_o, sums)
    return tuple(v.reshape(-1) if v.shape[0] == 1 else v for v in values)


def solution(mesh):
    in_specs = (
        P(None, "ctx", None),
        P(None, "ctx", None),
        P(),
        P(),
        P(),
        P(None, "wt"),
        P("wt"),
        P(None, "wt"),
        P(None, "wt"),
        P("wt"),
        P("wt", None),
        P(),
        P(),
        P(),
        P(None, "wt"),
        P("wt"),
        P("wt", None),
        P(),
    )
    out_specs = (
        P(None, "ctx", None),
        P(None, "ctx", None),
        P("wt"),
        P("wt"),
        P(None, "wt"),
        P("wt"),
        P(None, "wt"),
        P(None, "wt"),
        P("wt"),
        P("wt", None),
        P("wt"),
        P("wt"),
        P("wt"),
        P(None, "wt"),
        P("wt"),
        P("wt", None),
        P("wt"),
    )
    return jax.shard_map(shards, mesh=mesh, in_specs=in_specs, out_specs=out_specs, check_vma=False)
```

```python
import functools

import jax
import jax.numpy as jnp
from jax import lax
from jax.experimental import pallas as pl
from jax.experimental.pallas import tpu as pltpu
from jax.sharding import PartitionSpec as P

HEAD_DIM = 64
BLOCK = 16
LEVELS = 10
FINE = 3
EPSILON = 1e-05
NEGATIVE = -1e30
LOG_TWO = 0.6931471805599453
LANES = 128
BF16 = jnp.bfloat16
F32 = jnp.float32


def dot(left, right, dims):
    return lax.dot_general(left, right, (dims, ((), ())), preferred_element_type=F32)


def dot_nn(left, right):
    return dot(left, right, ((1,), (0,)))


def dot_nt(left, right):
    return dot(left, right, ((1,), (1,)))


def dot_tn(left, right):
    return dot(left, right, ((0,), (0,)))


def norm_parts(source):
    centre = jnp.mean(source, axis=-1, keepdims=True)
    centred = source - centre
    variance = jnp.mean(centred * centred, axis=-1, keepdims=True)
    inverse = lax.rsqrt(variance + EPSILON)
    return centred * inverse, inverse


def norm_backward(upstream, normed, inverse, gain):
    scaled = upstream * gain
    first_mean = jnp.mean(scaled, axis=-1, keepdims=True)
    second_mean = jnp.mean(scaled * normed, axis=-1, keepdims=True)
    return inverse * (scaled - first_mean - normed * second_mean)


def iota(shape, axis):
    return lax.broadcasted_iota(jnp.int32, shape, axis)


class Geometry:
    def __init__(self, ctx, wt, tok_dev):
        self.ctx, self.wt, self.tok_dev = ctx, wt, tok_dev
        tokens = ctx * tok_dev
        self.levels = len([l for l in range(LEVELS) if BLOCK * 2**l < tokens])
        self.own_cells = [tok_dev // 2**l if l <= FINE else 0 for l in range(self.levels)]
        self.tile = tok_dev // 2
        self.tile_slots = [BLOCK + self.tile] + [BLOCK * 4 >> (l - 1) if l < FINE else BLOCK for l in range(1, self.levels)]
        self.slots = sum(self.tile_slots)
        self.slot_at = [sum(self.tile_slots[:l]) for l in range(self.levels + 1)]
        self.far = self.levels - (FINE + 2)
        self.near = FINE + 2


def pool_matrix():
    parts = []
    for level, count in ((1, 128), (2, 64), (3, 32)):
        hit = (iota((count, 256), 1) >> level) == iota((count, 256), 0)
        parts.append(jnp.where(hit, 1.0 / 2**level, 0.0))
    return jnp.concatenate(parts, axis=0).astype(BF16)


def coarse_matrix():
    row, column = iota((32, 32), 0), iota((32, 32), 1)
    out = jnp.zeros((32, 32), F32)
    first = 0
    for level, count in ((4, 16), (5, 8), (6, 4), (7, 2), (8, 1)):
        up = level - FINE
        hit = (row >= first) & (row < first + count) & ((column >> up) == row - first)
        out = jnp.where(hit, 1.0 / 2**up, out)
        first += count
    return out.astype(BF16)


def far_matrix(geo, me):
    parts = []
    first = 0
    for step in range(geo.far):
        up = step + 1
        each = BLOCK >> up
        row, column = iota((BLOCK, geo.ctx * BLOCK), 0), iota((BLOCK, geo.ctx * BLOCK), 1)
        group = (me >> up) - 1
        device = (group << up) + (row >> (4 - up))
        wanted = device * BLOCK + first + (row & (each - 1))
        parts.append(jnp.where((column == wanted) & (group >= 0), 1.0, 0.0))
        first += each
    return jnp.concatenate(parts, axis=0).astype(BF16)


def mask_bias(geo, me, segs, tile):
    first_pos = me * geo.tok_dev + tile * geo.tile
    seg_one = jnp.sum((segs < 1).astype(jnp.int32), axis=1, keepdims=True)
    seg_two = jnp.sum((segs < 2).astype(jnp.int32), axis=1, keepdims=True)
    position = first_pos + iota((1, geo.tile), 1)
    begins = jnp.where(position >= seg_two, seg_two, jnp.where(position >= seg_one, seg_one, 0))
    parts = []
    for level in range(geo.levels):
        size, shift = 2**level, level + 4
        count = geo.tile_slots[level]
        span = BLOCK * size
        if level <= FINE:
            base = first_pos - span
        else:
            base = (((me * geo.tok_dev) >> shift) - 1) << shift
        begin = base + size * iota((count, geo.tile), 0)
        lower = jnp.maximum(((position >> shift) - 1) << shift, begins)
        if level == 0:
            upper = position + 1
        else:
            upper = ((position >> (shift - 1)) - 1) << (shift - 1)
        valid = (begin >= lower) & (begin + size <= upper)
        parts.append(jnp.where(valid, level * LOG_TWO, NEGATIVE))
    return jnp.concatenate(parts, axis=0)


def both_heads(pair):
    lane = iota(pair.shape, 1)
    zero = jnp.zeros_like(pair)
    return jnp.concatenate([jnp.where(lane < HEAD_DIM, pair, zero), jnp.where(lane >= HEAD_DIM, pair, zero)], axis=0)


def own_lanes(stacked):
    rows = stacked.shape[0] // 2
    lane = iota((rows, stacked.shape[1]), 1)
    return jnp.where(lane < HEAD_DIM, stacked[:rows], stacked[rows:])


def project(w, n1, weights, extra, q, own, cells, near, far):
    out = dot_nn(n1[...], weights[0][w])
    bias = extra[w, 1:2, :]
    q[w] = ((out[:, :LANES] + bias[:, :LANES]).astype(BF16) * 0.125).astype(BF16)
    kv = jnp.concatenate(
        [out[:, LANES : 2 * LANES], out[:, 2 * LANES :] + bias[:, LANES : 2 * LANES]], axis=1
    ).astype(BF16)
    own[w] = kv
    fine = dot_nn(pool_matrix(), kv).astype(BF16)
    cells[w] = fine
    rough = dot_nn(coarse_matrix(), fine[192:224]).astype(BF16)
    near[w, 0:16] = kv[240:256]
    near[w, 16:32] = fine[112:128]
    near[w, 32:48] = fine[176:192]
    near[w, 48:64] = fine[208:224]
    near[w, 64:80] = rough[0:16]
    far[w] = rough[16:32]


def tables(geo, w, pick, own, cells, near_in, far_in, table):
    blocks = far_in[:, w].reshape(geo.ctx * BLOCK, 2 * LANES)
    rough = dot_nn(pick, blocks).astype(BF16)
    at = geo.slot_at
    table[w, 0, 0:16] = near_in[w, 0:16]
    table[w, 0, 16:144] = own[w, 0:128]
    table[w, 1, 0:144] = own[w, 112:256]
    table[w, 0, at[1] : at[1] + 16] = near_in[w, 16:32]
    table[w, 0, at[1] + 16 : at[2]] = cells[w, 0:48]
    table[w, 1, at[1] : at[2]] = cells[w, 48:112]
    table[w, 0, at[2] : at[2] + 16] = near_in[w, 32:48]
    table[w, 0, at[2] + 16 : at[3]] = cells[w, 128:144]
    table[w, 1, at[2] : at[3]] = cells[w, 144:176]
    table[w, 0, at[3] : at[4]] = near_in[w, 48:64]
    table[w, 1, at[3] : at[4]] = cells[w, 192:208]
    for tile in (0, 1):
        table[w, tile, at[4] : at[5]] = near_in[w, 64:80]
        table[w, tile, at[5] :] = rough


def attend(geo, w, tile, q, table, bias, probs, mixed):
    rows = slice(tile * geo.tile, (tile + 1) * geo.tile)
    both = both_heads(q[w, rows, :])
    level_bias = bias[tile]
    scores = dot_nt(table[w, tile, :, :LANES], both)
    scores = scores + jnp.concatenate([level_bias, level_bias], axis=1)
    top = jnp.max(scores, axis=0, keepdims=True)
    exponent = jnp.exp(scores - top)
    total = jnp.sum(exponent, axis=0, keepdims=True)
    low = (exponent * (1.0 / total)).astype(BF16)
    probs[w, tile] = low
    mixed[w, rows, :] = own_lanes(dot_tn(low, table[w, tile, :, LANES:])).astype(BF16)


def attend_back(geo, w, tile, q, table, probs, d_mixed, d_queries, d_table):
    rows = slice(tile * geo.tile, (tile + 1) * geo.tile)
    both = both_heads(q[w, rows, :])
    d_both = both_heads(d_mixed[w, rows, :])
    low = probs[w, tile]
    d_probs = dot_nt(table[w, tile, :, LANES:], d_both)
    wide = low.astype(F32)
    product = wide * d_probs
    centre = jnp.sum(product, axis=0, keepdims=True)
    d_scores = (product - wide * centre).astype(BF16)
    d_table[w, tile, :, :LANES] = dot_nn(d_scores, both)
    d_table[w, tile, :, LANES:] = dot_nn(low, d_both)
    back = own_lanes(dot_tn(d_scores, table[w, tile, :, :LANES]))
    d_queries[w, rows, :] = (back * 0.125).astype(BF16)


def return_cells(geo, w, pick, d_table, near, far):
    at = geo.slot_at
    near[w, 0:16] = d_table[w, 0, 0:16].astype(BF16)
    near[w, 16:32] = d_table[w, 0, at[1] : at[1] + 16].astype(BF16)
    near[w, 32:48] = d_table[w, 0, at[2] : at[2] + 16].astype(BF16)
    near[w, 48:64] = d_table[w, 0, at[3] : at[4]].astype(BF16)
    near[w, 64:80] = (d_table[w, 0, at[4] : at[5]] + d_table[w, 1, at[4] : at[5]]).astype(BF16)
    rough = (d_table[w, 0, at[5] :] + d_table[w, 1, at[5] :]).astype(BF16)
    far[:, w] = dot_tn(pick, rough).astype(BF16).reshape(geo.ctx, BLOCK, 2 * LANES)


def own_gradients(geo, w, d_table, near_back, far_back):
    at = geo.slot_at
    first, second = d_table.at[w, 0], d_table.at[w, 1]
    back = near_back[w].astype(F32)
    tokens = jnp.concatenate(
        [first[16:128], first[128:144] + second[0:16], second[16:128], second[128:144] + back[0:16]], axis=0
    )
    far = jnp.sum(far_back[:, w].astype(F32), axis=0)
    rough = jnp.concatenate([back[64:80], far], axis=0)
    fine = dot_tn(coarse_matrix(), rough.astype(BF16))
    level3 = jnp.concatenate([second[at[3] : at[4]], back[48:64]], axis=0) + fine
    cells = jnp.concatenate(
        [
            first[at[1] + 16 : at[2]],
            second[at[1] : at[2]],
            back[16:32],
            first[at[2] + 16 : at[3]],
            second[at[2] : at[3]],
            back[32:48],
            level3,
        ],
        axis=0,
    )
    return tokens + dot_tn(pool_matrix(), cells.astype(BF16))


def feed(w, n2, weights, extra, hidden, slope, result):
    pre = dot_nn(n2[...], weights[1][w]) + extra[w, 0:1, :]
    gate = jax.nn.sigmoid(pre)
    hidden[w] = (pre * gate).astype(BF16)
    slope[w] = gate * (1.0 + pre * (1.0 - gate))
    result[...] += dot_nn(hidden[w], weights[2][w])


def feed_back(first, w, g2, weights, n2, hidden, slope, sums, grads, total):
    d_hidden = dot_nt(g2[...], weights[2][w]).astype(BF16).astype(F32)
    d_up = (d_hidden * slope[w]).astype(BF16)
    sums[w, 0:1, :] = jnp.sum(d_up.astype(F32), axis=0, keepdims=True)
    grads[2][w] = dot_tn(hidden[w], g2[...]).astype(BF16)
    grads[1][w] = dot_tn(n2[...], d_up).astype(BF16)
    part = dot_nt(d_up, weights[1][w])
    total[...] = part if first else total[...] + part


def put_sums(geo, sums, column, row):
    at, lanes = 2 + column // 4, slice(column % 4 * LANES, (column % 4 + 1) * LANES)
    for w in range(geo.wt):
        sums[w, at : at + 1, lanes] = row[:, w * LANES : (w + 1) * LANES]


def project_back(geo, first, w, weights, n1, d_queries, d_table, near_back, far_back, sums, grads, total):
    kv = own_gradients(geo, w, d_table, near_back, far_back).astype(BF16)
    d_qkv = jnp.concatenate([d_queries[w], kv], axis=1)
    sums[w, 1:2, :LANES] = jnp.sum(d_qkv[:, :LANES].astype(F32), axis=0, keepdims=True)
    sums[w, 1:2, LANES : 2 * LANES] = jnp.sum(d_qkv[:, 2 * LANES :].astype(F32), axis=0, keepdims=True)
    grads[0][w] = dot_tn(n1[...], d_qkv).astype(BF16)
    part = dot_nt(d_qkv, weights[0][w])
    total[...] = part if first else total[...] + part


def remote(source, target, sent, landed, device):
    return pltpu.make_async_remote_copy(source, target, sent, landed, device_id=device, device_id_type=pl.DeviceIdType.MESH)


class Plane:
    def __init__(self, ctx, c, rows):
        self.ctx, self.c = ctx, c
        self.bits = ctx.bit_length() - 1
        self.each = rows // ctx
        plane_bits = self.bits - 1
        half = plane_bits // 2
        self.plane_bits, self.half = plane_bits, half
        self.places = self.places_of(c)
        self.masks = (
            [2 << s for s in range(plane_bits)] + [1],
            [2 << (s + half) % plane_bits for s in range(plane_bits)] + [1],
        )

    def places_of(self, device):
        plane, core = device // 2, device % 2
        turned = plane // 2**self.half + plane % 2**self.half * 2 ** (self.plane_bits - self.half)
        top = core * 2**self.plane_bits
        return plane + top, turned + top

    def place(self, order, device=None):
        places = self.places if device is None else self.places_of(device)
        if isinstance(order, int):
            return places[order]
        return jnp.where(order == 0, places[0], places[1])

    def partner(self, order, stage):
        if isinstance(order, int):
            return self.flip(self.masks[order][stage])
        return jnp.where(order == 0, self.flip(self.masks[0][stage]), self.flip(self.masks[1][stage]))

    def flip(self, mask):
        return self.c + mask * (1 - 2 * (self.c // mask % 2))

    def flips(self, bits):
        device = self.c
        for s in range(self.bits):
            if bits >> s & 1:
                device = device + (1 << s) * (1 - 2 * (self.c // (1 << s) % 2))
        return device

    def block(self, order, stage, other=False, device=None):
        index = self.place(order, device) // 2**stage
        if other:
            index = index + 1 - 2 * (index % 2)
        size = self.each * 2**stage
        return pl.ds(pl.multiple_of(index * size, size), size)


SCHEDULE = (
    ("send_shards", 0), ("first_norm",), ("send_shards", 1), ("send_shards", 3), ("event", 0, 0, 0),
    ("event", 0, 1, 0), ("event", 1, 0, 0), ("event", 0, 0, 1), ("event", 3, 0, 0), ("send_biases",),
    ("projection", 0), ("event", 1, 1, 0), ("event", 0, 2, 0), ("event", 3, 1, 0), ("event", 3, 1, 1), ("masks",),
    ("event", 1, 0, 1), ("send_shards", 2), ("event", 0, 0, 2), ("event", 1, 2, 0), ("event", 0, 1, 1),
    ("event", 3, 1, 2), ("event", 0, 2, 1), ("event", 1, 1, 1), ("wait_biases",), ("attention", 0),
    ("event", 0, 0, 3), ("projection", 1), ("event", 3, 2, 0), ("event", 1, 1, 2), ("event", 2, 0, 0),
    ("event", 2, 0, 1), ("event", 2, 1, 0), ("event", 2, 1, 1), ("event", 0, 1, 2), ("event", 0, 2, 2),
    ("event", 1, 0, 2), ("event", 1, 0, 3), ("event", 0, 2, 3), ("projection", 3), ("event", 3, 0, 1),
    ("event", 0, 1, 3), ("event", 3, 2, 1), ("event", 3, 2, 2), ("event", 1, 2, 1), ("projection", 2),
    ("event", 2, 1, 2), ("event", 2, 2, 0), ("event", 2, 0, 2), ("event", 3, 0, 2), ("event", 3, 0, 3),
    ("event", 3, 1, 3), ("attention", 1), ("attention", 3), ("event", 3, 2, 3), ("attention", 2), ("second_norm",),
    ("event", 2, 0, 3), ("forth", 1), ("event", 2, 2, 1), ("event", 2, 2, 2), ("event", 2, 1, 3), ("event", 1, 2, 2),
    ("forth", 0), ("back", 0), ("halve", 1, 0), ("halve", 2, 0), ("event", 2, 2, 3), ("event", 1, 1, 3),
    ("event", 1, 2, 3), ("forth", 2), ("back", 2), ("halve", 1, 2), ("forth", 3), ("layer_rows",), ("rows_first", 0),
    ("back", 1), ("add", 1, 0, 2), ("add", 2, 0, 2), ("back", 3), ("second_back",), ("halve", 2, 3), ("out_back", 1),
    ("rows_first", 1), ("halve", 2, 1), ("out_back", 0), ("give", 0), ("out_back", 2), ("give", 2), ("out_back", 3),
    ("give", 1), ("give", 3), ("halve", 3, 0), ("halve", 1, 1), ("add", 3, 0, 2), ("add", 1, 1, 2), ("halve", 1, 3),
    ("add", 1, 2, 2), ("add", 2, 3, 2), ("rows_relay", 0, 0), ("take", 0), ("add", 1, 3, 2), ("add", 2, 1, 2),
    ("take", 1), ("take", 2), ("take", 3), ("add", 1, 2, 1), ("rows_relay", 1, 0), ("halve", 0, 2), ("halve", 2, 2),
    ("source",), ("rows_first", 2), ("settle", 0), ("settle", 3), ("settle", 20), ("add", 2, 3, 1), ("add", 3, 0, 1),
    ("add", 1, 3, 1), ("add", 1, 0, 1), ("rows_relay", 0, 1), ("send_sums",), ("halve", 3, 1), ("add", 3, 1, 2),
    ("add", 2, 0, 1), ("add", 0, 2, 2), ("settle", 1), ("add", 3, 0, 0), ("rows_relay", 1, 1), ("halve", 3, 2),
    ("add", 2, 2, 2), ("add", 2, 3, 0), ("halve", 0, 0), ("add", 1, 3, 0), ("add", 3, 2, 2), ("halve", 0, 1),
    ("add", 3, 1, 1), ("add", 1, 1, 1), ("halve", 3, 3), ("add", 3, 3, 2), ("add", 1, 0, 0), ("halve", 0, 3),
    ("add", 2, 1, 1), ("add", 0, 0, 2), ("add", 1, 2, 0), ("add", 2, 0, 0), ("settle", 2), ("settle", 23),
    ("add", 2, 2, 1), ("rows_relay", 2, 1), ("add", 3, 1, 0), ("add", 1, 1, 0), ("line_over", 1), ("add", 3, 3, 1),
    ("add_sums", 0), ("add", 0, 1, 2), ("add", 0, 2, 1), ("add", 2, 1, 0), ("settle", 22), ("add", 2, 2, 0),
    ("line_over", 2), ("add_sums", 1), ("add", 3, 2, 1), ("rows_first", 3), ("add", 0, 2, 0), ("line_pass", 1),
    ("line_pass", 2), ("add", 0, 3, 2), ("add", 0, 1, 1), ("add", 0, 0, 1), ("rows_relay", 2, 0), ("add_sums", 2),
    ("settle", 5), ("settle", 6), ("settle", 16), ("settle", 17), ("add", 0, 1, 0), ("add", 0, 3, 1),
    ("add", 0, 0, 0), ("add", 3, 3, 0), ("line_end", 1), ("gather", 1, 0), ("add", 3, 2, 0), ("line_end", 2),
    ("gather", 2, 0), ("add", 0, 3, 0), ("settle", 9), ("settle", 10), ("settle", 7), ("gather", 2, 1),
    ("gather", 1, 1), ("rows_relay", 3, 0), ("rows_wait", 2), ("line_end", 3), ("gather", 3, 0), ("rows_relay", 3, 1),
    ("settle", 4), ("line_end", 0), ("gather", 0, 0), ("gather", 2, 2), ("gather", 1, 2), ("gather", 3, 1),
    ("settle", 18), ("settle", 11), ("gather", 0, 1), ("rows_wait", 0), ("settle", 21), ("settle", 8),
    ("gather", 3, 2), ("add_sums", 3), ("store", 2), ("gather", 1, 3), ("rows_wait", 1), ("store", 0),
    ("rows_wait", 3), ("store", 1), ("store", 6), ("gather", 2, 3), ("store", 5), ("store", 4), ("settle", 13),
    ("settle", 14), ("gather", 0, 2), ("store", 3), ("settle", 12), ("settle", 15), ("settle", 19),
)
FIRST_STAGE = (0, 0, 1, 1)
WAYS = (1, 1, 1, 1)


def fused(geo, *refs):
    (
        x_hbm, g_hbm, segs_hbm, n1g_hbm, n1b_hbm, q_hbm, q_bias_hbm, k_hbm, v_hbm, v_bias_hbm, o_hbm, out_bias_hbm,
        n2g_hbm, n2b_hbm, up_hbm, up_bias_hbm, down_hbm, down_bias_hbm,
        out_result, out_source, out_a, out_u, out_d, out_o, out_sums,
        segs, n1g, n1b, q_bias, v_bias, out_bias, n2g, n2b, up_bias, down_bias,
        w_a, w_u, w_d, w_o, extra, x, g2, o_own, n1, q, own, cells, near_send, far_send, near_in, far_in,
        table, bias, probs, mixed, middle, n2, hidden, slope, result, total, g1, d_mixed, d_queries, d_table,
        g1_low, near_give, far_give, near_back, far_back, g_a, g_u, g_d, g_o, sums, gathered, source_all,
        line_a, line_u, line_d, line_o, end_a, end_u, end_d, end_o, in_a, in_u, in_d, in_o, r_a, r_u, r_d, r_o, sums_in, sums_all, sums_got,
        load_sem, small_sem, store_sem, zw_send, zw_recv, pw_send, pw_recv, ex_send, ex_recv, halo_send, halo_recv,
        far_s, far_r, back_send, back_recv, rs_send, rs_recv, zl_send, zl_recv, zx_recv, zy_recv,
        ag_send, ag_recv, gp_send, gp_recv, gc_send, gc_recv, out_send, out_recv, sm_send, sm_recv, sc_send, sc_recv,
        *landings,
    ) = refs
    weights, grads, reduced = (w_a, w_u, w_d, w_o), (g_a, g_u, g_d, g_o), (r_a, r_u, r_d, r_o)
    from_line, from_end, from_inner = (line_a, line_u, line_d, line_o), (end_a, end_u, end_d, end_o), (in_a, in_u, in_d, in_o)
    C, W = geo.ctx, geo.wt
    c, z = lax.axis_index("ctx"), lax.axis_index("wt")
    plane = Plane(C, c, 512)
    B = plane.bits

    loads = [
        pltpu.make_async_copy(q_hbm, weights[0].at[z, :, pl.ds(0, LANES)], load_sem.at[0]),
        pltpu.make_async_copy(k_hbm, weights[0].at[z, :, pl.ds(LANES, LANES)], load_sem.at[1]),
        pltpu.make_async_copy(v_hbm, weights[0].at[z, :, pl.ds(2 * LANES, LANES)], load_sem.at[2]),
        pltpu.make_async_copy(o_hbm, o_own, load_sem.at[3]),
        pltpu.make_async_copy(up_hbm, weights[1].at[z], load_sem.at[4]),
        pltpu.make_async_copy(down_hbm, weights[2].at[z], load_sem.at[5]),
        pltpu.make_async_copy(x_hbm.at[z], x, load_sem.at[6]),
        pltpu.make_async_copy(g_hbm.at[z], g2, load_sem.at[7]),
    ]
    small = [
        pltpu.make_async_copy(source, target, small_sem.at[at])
        for at, (source, target) in enumerate(
            (
                (q_bias_hbm, q_bias), (v_bias_hbm, v_bias), (up_bias_hbm, up_bias), (n1g_hbm, n1g), (n1b_hbm, n1b),
                (segs_hbm, segs), (out_bias_hbm, out_bias), (n2g_hbm, n2g), (n2b_hbm, n2b), (down_bias_hbm, down_bias),
            )
        )
    ]

    for copy in loads + small:
        copy.start()
    near_in[...] = jnp.zeros_like(near_in)
    far_in[...] = jnp.zeros_like(far_in)
    near_back[...] = jnp.zeros_like(near_back)
    far_back[...] = jnp.zeros_like(far_back)

    barrier = pltpu.get_barrier_semaphore()
    for step in range(1, C):
        pl.semaphore_signal(barrier, inc=1, device_id=(lax.rem(c + step, C), z), device_id_type=pl.DeviceIdType.MESH)
    for step in range(1, W):
        pl.semaphore_signal(barrier, inc=1, device_id=(c, lax.rem(z + step, W)), device_id_type=pl.DeviceIdType.MESH)
    sums[...] = jnp.zeros_like(sums)
    extra[z] = jnp.zeros_like(extra[z])
    pl.semaphore_wait(barrier, C + W - 2)

    def order_of(k, w):
        return (k + w) % 2

    def sent(block, semaphore):
        pltpu.make_async_copy(block, block, semaphore).wait()

    relays = W == 4
    inner = (z > 0) & (z < W - 1) if relays else jnp.bool_(False)
    across = jnp.where(z < W // 2, z + 2, z - 2)
    beside = W - 1 - z
    end = jnp.where(z < W // 2, 0, W - 1)
    near_inner = jnp.where(z < W // 2, 1, W - 2)

    def arrival(i, way):
        table_of = []
        for at in range(W):
            seen = []
            for step in range(1, W):
                seen += [w for w in (at - step, at + step) if 0 <= w < W]
            if way == 1 and 0 < at < W - 1:
                seen = [at - 1, at + 2, at + 1] if at < W // 2 else [at + 1, at - 2, at - 1]
            if way == 2 and 0 < at < W - 1:
                seen = [at - 1, at + 1, at + 2] if at < W // 2 else [at + 1, at - 1, at - 2]
            table_of.append(seen[i])
        w = jnp.int32(table_of[0])
        for at in range(1, W):
            w = jnp.where(z == at, table_of[at], w)
        return w

    ways = WAYS if relays else (0, 0, 0, 0)
    first_stage = FIRST_STAGE if B > 2 else (0, 0, 0, 0)
    arrivals_of = [[arrival(i, way) for i in range(W - 1)] for way in ways]
    arrivals = arrivals_of[0]

    def each_direct(action, way):
        for step in range(1, W):
            for to, there in ((z - step, z >= step), (z + step, z + step < W)):
                skip = jnp.bool_(False)
                if way == 1:
                    skip = z + to == W - 1
                if way == 2:
                    skip = (z + to == W - 1) & jnp.logical_not(inner) | inner & (to == across)

                @pl.when(there & jnp.logical_not(skip))
                def _():
                    action(to)

    def weight_line(k, w, to, relayed=False, own=False):
        rows = plane.block(order_of(k, w), first_stage[k])
        slot = jnp.where(w == across, z, across) if relayed else to
        mine = {1: up_hbm, 2: down_hbm}.get(k) if own else None
        return remote(
            weights[k].at[w, rows] if mine is None else mine.at[rows], weights[k].at[w, rows], zw_send.at[k, slot], zw_recv.at[k, w], (c, to)
        )

    def weight_first(k):
        each_direct(lambda to: weight_line(k, z, to, own=True).start(), ways[k])

    def held_at(k, s):
        return [-1, *range(first_stage[k], s)] if s >= first_stage[k] else []

    plane_slots = {}
    for k in range(4):
        for s in range(B):
            if s >= first_stage[k]:
                plane_slots[k, s] = len(plane_slots)

    def weight_copy(k, w, j, s, landing=False):
        order = order_of(k, w)
        device = plane.partner(order, s)
        seen = device if landing else None
        if j < 0:
            rows = plane.block(order, first_stage[k], device=seen)
        else:
            rows = plane.block(order, j, other=True, device=seen)
        at, rank = plane_slots[k, s], lax.rem(w - z + W, W) - 1
        block = weights[k].at[w, rows]
        return remote(block, block, pw_send.at[k], pw_recv.at[at, rank], (device, z))

    def weight_event(k, i, s):
        w = arrivals_of[k][i]
        if s == 0:
            weight_line(k, w, lax.rem(z + 1, W)).wait_recv()
            if i == 1 and ways[k] == 1:

                @pl.when(inner)
                def _():
                    weight_line(k, w, end, True).start()
                    weight_line(k, z, beside, own=True).start()

            if i > 0 and ways[k] == 2:

                @pl.when(inner)
                def _():
                    weight_line(k, w, end, True).start()

            for later in range(first_stage[k], B):
                weight_copy(k, w, -1, later).start()
        else:
            if s > first_stage[k]:
                at, rank = plane_slots[k, s - 1], lax.rem(w - z + W, W) - 1
                sent(weights[k].at[w, plane.block(order_of(k, w), s - 1, other=True)], pw_recv.at[at, rank])
            if s > first_stage[k]:
                for later in range(s, B):
                    weight_copy(k, w, s - 1, later).start()

    def weight_drain(k):
        each_direct(lambda to: weight_line(k, z, to, own=True).wait_send(), ways[k])
        if ways[k]:

            @pl.when(inner)
            def _():
                weight_line(k, across, end, True).wait_send()
                if ways[k] == 1:
                    weight_line(k, z, beside, own=True).wait_send()
                else:
                    weight_line(k, beside, end, True).wait_send()

        sent(weights[k].at[pl.ds(0, W - 1), pl.ds(0, plane.each * (C - 2 ** first_stage[k]))], pw_send.at[k])

    def extra_copy(step):
        to = lax.rem(z + step, W)
        return remote(extra.at[z], extra.at[z], ex_send.at[step], ex_recv.at[step], (c, to))

    def extra_from(step):
        source = lax.rem(z + W - step, W)
        return remote(extra.at[source], extra.at[source], ex_send.at[step], ex_recv.at[step], (c, source))

    def halo(w, back):
        if back:
            return remote(near_give.at[w], near_back.at[w], back_send.at[w], back_recv.at[w], (c - 1, z))
        return remote(near_send.at[w], near_in.at[w], halo_send.at[w], halo_recv.at[w], (c + 1, z))

    def needs(source, target):
        need = jnp.bool_(False)
        for step in range(geo.far):
            size = 2 ** (step + 1)
            need = need | (target // size == source // size + 1)
        return need

    def far_copy(w, device, source):
        return remote(far_send.at[w], far_in.at[source, w], far_s.at[device, w], far_r.at[source, w], (device, z))

    def give_copy(w, device, source):
        return remote(
            far_give.at[device, w], far_back.at[source, w], far_s.at[device, w], far_r.at[source, w], (device, z)
        )

    def each_after(action):
        for step in range(1, C):
            device = jnp.minimum(c + step, C - 1)

            @pl.when((c + step < C) & needs(c, device))
            def _():
                action(device)

    def each_before(action):
        for step in range(1, C):
            device = jnp.maximum(c - step, 0)

            @pl.when((c - step >= 0) & needs(device, c))
            def _():
                action(device)

    def halo_start(w):
        @pl.when(c < C - 1)
        def _():
            halo(w, False).start()

        each_after(lambda device: far_copy(w, device, c).start())

    def halo_wait(w):
        @pl.when(c > 0)
        def _():
            halo(w, False).wait_recv()

        each_before(lambda device: far_copy(w, device, device).wait_recv())

    def give_start(w):
        @pl.when(c > 0)
        def _():
            halo(w, True).start()

        each_before(lambda device: give_copy(w, device, c).start())

    def give_wait(w):
        @pl.when(c < C - 1)
        def _():
            halo(w, True).wait_recv()

        each_after(lambda device: give_copy(w, device, device).wait_recv())

    def row_copy(part, w, to, relayed=False):
        rows = (gathered, source_all)[part // 2].at[w, pl.ds(part % 2 * geo.tile, geo.tile)]
        slot = jnp.where(w == across, across, z) if relayed else to
        return remote(rows, rows, out_send.at[part, slot], out_recv.at[part, w], (c, to))

    def rows_first(part):
        each_direct(lambda to: row_copy(part, z, to).start(), 2 if relays else 0)

    def rows_relay(part, far):
        w = across if far else beside

        @pl.when(inner)
        def _():
            row_copy(part, w, end).wait_recv()
            row_copy(part, w, end, True).start()

    def rows_wait(part):
        for step in range(1, W):
            w = lax.rem(z + step, W)

            @pl.when(jnp.logical_not(inner) | (w == end))
            def _():
                row_copy(part, w, w).wait_recv()

    def rows_drain(part):
        each_direct(lambda to: row_copy(part, z, to).wait_send(), 2 if relays else 0)

        @pl.when(inner)
        def _():
            row_copy(part, across, end, True).wait_send()
            row_copy(part, beside, end, True).wait_send()

    def reduce_copy(k, w, s):
        order = order_of(k, w)
        return remote(
            grads[k].at[w, plane.block(order, s, other=True)],
            landings[4 * s + k].at[w],
            rs_send.at[k],
            rs_recv.at[k, w, s],
            (plane.partner(order, s), z),
        )

    def reduce_add(k, w, s):
        reduce_copy(k, w, s).wait_recv()
        rows = plane.block(order_of(k, w), s)
        grads[k][w, rows] = (grads[k][w, rows].astype(F32) + landings[4 * s + k][w].astype(F32)).astype(BF16)
        if s > 0:
            reduce_copy(k, w, s - 1).start()
        else:
            line_send(k, w)

    def line_copy(k, w, way=None):
        rows = plane.block(order_of(k, w), 0)
        if way == "end":
            return remote(grads[k].at[w, rows], from_end[k], zl_send.at[k], zx_recv.at[k], (c, near_inner))
        if way == "inner":
            return remote(grads[k].at[w, rows], from_inner[k], zl_send.at[k], zy_recv.at[k], (c, beside))
        return remote(grads[k].at[w, rows], from_line[k].at[z], zl_send.at[k], zl_recv.at[k, z], (c, w))

    chained = (False, relays, relays, False)

    def line_send(k, w):
        over = jnp.logical_not(inner) & (w == beside) if chained[k] else jnp.bool_(False)
        waits = inner & ((w == across) | (w == end)) if chained[k] else jnp.bool_(False)

        @pl.when(over)
        def _():
            line_copy(k, w, "end").start()

        @pl.when((w != z) & jnp.logical_not(over | waits))
        def _():
            line_copy(k, w).start()

    def line_add(k, w, landed):
        rows = plane.block(order_of(k, w), 0)
        grads[k][w, rows] = (grads[k][w, rows].astype(F32) + landed[k][...].astype(F32)).astype(BF16)

    def line_over(k):
        @pl.when(inner)
        def _():
            line_copy(k, across, "end").wait_recv()
            line_add(k, across, from_end)
            line_copy(k, across, "inner").start()

    def line_pass(k):
        @pl.when(inner)
        def _():
            line_copy(k, across, "inner").wait_recv()
            line_add(k, end, from_inner)
            line_copy(k, end).start()

    def own_rows(k):
        return plane.block(order_of(k, z), 0)

    def line_end(k):
        rows = own_rows(k)
        total_now = grads[k][z, rows].astype(F32)
        for step in range(1, W):
            source = lax.rem(z + step, W)
            block = from_line[k].at[source]
            comes = inner | (source == near_inner) if chained[k] else jnp.bool_(True)

            @pl.when(comes)
            def _():
                remote(block, block, zl_send.at[k], zl_recv.at[k, source], (c, source)).wait_recv()

            total_now = total_now + jnp.where(comes, from_line[k][source].astype(F32), 0.0)
        reduced[k][rows] = total_now.astype(BF16)

    def gather_copy(k, j, s):
        order = order_of(k, z)
        rows = plane.block(order, 0) if j < 0 else plane.block(order, j, other=True)
        at = s * (s + 1) // 2 + j + 1
        block = reduced[k].at[rows]
        return remote(block, block, ag_send.at[k - 1], ag_recv.at[k - 1, s], (plane.partner(order, s), z))

    def gather_landing(k, j, s):
        order = order_of(k, z)
        device = plane.partner(order, s)
        rows = plane.block(order, 0, device=device) if j < 0 else plane.block(order, j, other=True, device=device)
        at = s * (s + 1) // 2 + j + 1
        block = reduced[k].at[rows]
        return remote(block, block, ag_send.at[k - 1], ag_recv.at[k - 1, s], (device, z))

    def gather_plane(k, offset, landing=False):
        device = plane.flips(2 * offset)
        block = reduced[k].at[plane.block(order_of(k, z), 0, device=device if landing else None)]
        return remote(block, block, gp_send.at[k // 3], gp_recv.at[k // 3, offset], (device, z))

    def gather_core(k, offset, landing=False):
        block = reduced[k].at[plane.block(order_of(k, z), 0, device=plane.flips(2 * offset + int(landing)))]
        return remote(block, block, gc_send.at[k // 3], gc_recv.at[k // 3, offset], (plane.flips(1), z))

    straight = (True, False, False, True)

    def gather_event(k, s):
        if straight[k]:
            offsets = range(1, C // 2) if s < 2 else range(C // 2)
            for offset in offsets:
                if s == 0:
                    gather_plane(k, offset).start()
                elif s == 1:
                    gather_plane(k, offset, True).wait_recv()
                    gather_core(k, offset).start()
                elif s == 2:
                    gather_core(k, offset, True).wait_recv()
            if s == 0:
                gather_core(k, 0).start()
            return
        if s > 0:
            sent(reduced[k].at[plane.block(order_of(k, z), s - 1, other=True)], ag_recv.at[k - 1, s - 1])
        for later in range(s, B):
            gather_copy(k, s - 1, later).start()

    def gather_drain(k):
        if straight[k]:
            sent(reduced[k].at[pl.ds(0, plane.each * (C // 2 - 1))], gp_send.at[k // 3])
            sent(reduced[k].at[pl.ds(0, plane.each * (C // 2))], gc_send.at[k // 3])
        else:
            sent(reduced[k].at[pl.ds(0, plane.each * (C - 1))], ag_send.at[k - 1])

    held = {}
    shard_of = [z] + arrivals
    feed_of = [z] + arrivals_of[2]
    turn = [w for step in range((W + 1) // 2) for w in dict.fromkeys((step, W - 1 - step))]

    def send_shards(k):
        for at in {0: (0, 1, 2), 3: (3,)}.get(k, ()):
            loads[at].wait()
        if k == 3:
            weights[3][z] = o_own[...].T
        weight_first(k)

    def send_biases():
        for at in (0, 1, 2):
            small[at].wait()
        extra[z, 0:1, :] = up_bias[...]
        extra[z, 1:2, :LANES] = q_bias[...]
        extra[z, 1:2, LANES : 2 * LANES] = v_bias[...]
        for step in range(1, W):
            extra_copy(step).start()

    def wait_biases():
        for step in range(1, W):
            extra_from(step).wait_recv()

    def first_norm():
        loads[6].wait()
        small[3].wait()
        small[4].wait()
        normed, _ = norm_parts(x[...].astype(F32))
        n1[...] = (normed * n1g[...] + n1b[...]).astype(BF16)

    def masks():
        small[5].wait()
        bias[0] = mask_bias(geo, c, segs[pl.ds(z, 1), :], 0)
        bias[1] = mask_bias(geo, c, segs[pl.ds(z, 1), :], 1)
        held["pick"] = far_matrix(geo, c)

    def projection(i):
        w = shard_of[i]
        project(w, n1, weights, extra, q, own, cells, near_send, far_send)
        halo_start(w)

    def attention(i):
        w = shard_of[i]
        halo_wait(w)
        tables(geo, w, held["pick"], own, cells, near_in, far_in, table)
        for tile in (0, 1):
            attend(geo, w, tile, q, table, bias, probs, mixed)

    def event(k, i, s):
        for stage in {0: [0], 1: [1], 2: range(2, B), 3: [B]}[s]:
            weight_event(k, i, stage)

    def second_norm():
        for at in (4, 5, 7):
            loads[at].wait()
        for at in range(6, 10):
            small[at].wait()
        acc = x[...].astype(F32) + out_bias[...]
        for w in range(W):
            acc = acc + dot_nt(mixed[w], weights[3][w])
        middle[...] = acc
        normed, _ = norm_parts(acc)
        n2[...] = (normed * n2g[...] + n2b[...]).astype(BF16)
        result[...] = acc + down_bias[...]

    def forth(i):
        feed(feed_of[i], n2, weights, extra, hidden, slope, result)

    def layer_rows():
        gathered[z] = result[...].astype(BF16)

    def back(i):
        first = "total" not in held
        held["total"] = True
        feed_back(first, feed_of[i], g2, weights, n2, hidden, slope, sums, grads, total)

    def shard(k, i):
        return feed_of[i] if k in (1, 2) else turn[i]

    def halve(k, i):
        reduce_copy(k, shard(k, i), B - 1).start()

    def add(k, i, s):
        for stage in {2: [B - 1], 1: range(B - 2, 0, -1), 0: [0]}[s]:
            reduce_add(k, shard(k, i), stage)

    def second_back():
        hat, inverse = norm_parts(middle[...])
        d_normed = total[...]
        wide = g2[...].astype(F32)
        first = wide + norm_backward(d_normed, hat, inverse, n2g[...])
        g1[...] = first
        g1_low[...] = first.astype(BF16)
        put_sums(geo, sums, 2, jnp.sum(first, axis=0, keepdims=True))
        put_sums(geo, sums, 3, jnp.sum(d_normed * hat, axis=0, keepdims=True))
        put_sums(geo, sums, 4, jnp.sum(d_normed, axis=0, keepdims=True))
        put_sums(geo, sums, 5, jnp.sum(wide, axis=0, keepdims=True))
        del held["total"]

    def out_back(i):
        w = turn[i]
        d_mixed[w] = dot_nn(g1_low[...], weights[3][w]).astype(BF16)
        grads[3][w] = dot_tn(g1_low[...], mixed[w]).astype(BF16)

    def give(i):
        w = turn[i]
        for tile in (0, 1):
            attend_back(geo, w, tile, q, table, probs, d_mixed, d_queries, d_table)
        return_cells(geo, w, held["pick"], d_table, near_give, far_give)
        give_start(w)

    def take(i):
        w = turn[i]
        give_wait(w)
        first = "total" not in held
        held["total"] = True
        project_back(geo, first, w, weights, n1, d_queries, d_table, near_back, far_back, sums, grads, total)

    def source():
        normed, inverse = norm_parts(x[...].astype(F32))
        d_normed = total[...]
        source_all[z] = (g1[...] + norm_backward(d_normed, normed, inverse, n1g[...])).astype(BF16)
        put_sums(geo, sums, 0, jnp.sum(d_normed * normed, axis=0, keepdims=True))
        put_sums(geo, sums, 1, jnp.sum(d_normed, axis=0, keepdims=True))

    def sums_copy(step):
        to = lax.rem(z + step, W)
        return remote(sums.at[to], sums_in.at[step], sm_send.at[step], sm_recv.at[step], (c, to))

    def sums_stage(s):
        return remote(sums_all.at[s], sums_got.at[s], sc_send.at[s], sc_recv.at[s], (plane.flip(1 << s), z))

    def send_sums():
        for step in range(1, W):
            sums_copy(step).start()

    def add_sums(s):
        if s == 0:
            total_sums = sums[z]
            for step in range(1, W):
                sums_copy(step).wait_recv()
                total_sums = total_sums + sums_in[step]
            sums_all[0] = total_sums
            sums_stage(0).start()
        for stage in {0: [], 1: [0], 2: range(1, B - 1), 3: [B - 1]}[s]:
            sums_stage(stage).wait_recv()
            sums_all[stage + 1] = sums_all[stage] + sums_got[stage]
            if stage + 1 < B:
                sums_stage(stage + 1).start()

    def gather(k, s):
        for stage in {0: [0], 1: [1], 2: range(2, B), 3: [B]}[s]:
            gather_event(k, stage)

    stores = [
        pltpu.make_async_copy(gathered, out_result, store_sem.at[0]),
        pltpu.make_async_copy(source_all, out_source, store_sem.at[1]),
        pltpu.make_async_copy(sums_all.at[B], out_sums, store_sem.at[2]),
        pltpu.make_async_copy(r_a, out_a, store_sem.at[3]),
        pltpu.make_async_copy(r_u, out_u, store_sem.at[4]),
        pltpu.make_async_copy(r_d, out_d, store_sem.at[5]),
        pltpu.make_async_copy(r_o, out_o, store_sem.at[6]),
    ]

    def store(i):
        stores[i].start()

    def reduce_drain(k):
        sent(grads[k].at[:, pl.ds(0, plane.each * (C - 1))], rs_send.at[k])

    def lines_drain(k):
        sent(reduced[k].at[pl.ds(0, plane.each * (W - 1))], zl_send.at[k])

    def settle(group):
        if group < 4:
            weight_drain(group)
        elif group < 8:
            reduce_drain(group - 4)
        elif group < 12:
            lines_drain(group - 8)
        elif group < 16:
            gather_drain(group - 12)
        elif group < 20:
            rows_drain(group - 16)
        elif group == 20:
            for step in range(1, W):
                extra_copy(step).wait_send()
        elif group == 21:
            for step in range(1, W):
                sums_copy(step).wait_send()
            for s in range(B):
                sums_stage(s).wait_send()
        else:
            for w in range(W):
                if group == 22:

                    @pl.when(c < C - 1)
                    def _():
                        halo(w, False).wait_send()

                    each_after(lambda device: far_copy(w, device, c).wait_send())
                else:

                    @pl.when(c > 0)
                    def _():
                        halo(w, True).wait_send()

                    each_before(lambda device: give_copy(w, device, c).wait_send())

    steps = {
        step.__name__: step
        for step in (
            send_shards, send_biases, wait_biases, first_norm, masks, projection, attention, event, second_norm, forth,
            layer_rows, back, halve, add, second_back, out_back, give, take, source, send_sums, add_sums, gather, store,
            rows_first, rows_relay, rows_wait, line_over, line_pass, line_end, settle,
        )
    }
    for name, *args in SCHEDULE:
        steps[name](*args)

    for copy in stores:
        copy.wait()


def unpack(
    result_in, source_in, a_in, u_in, d_in, o_in, sums_in,
    result_out, source_out, d_n1g, d_n1b, d_q, d_qb, d_k, d_v, d_vb, d_o, d_ob, d_n2g, d_n2b, d_up, d_upb, d_down, d_db,
    result, source, a, u, d, o, sums, result_f, source_f, a_f, o_f, u_f, d_f, row_f, load_sem, store_sem,
):
    runs = result.shape[0]
    pairs = [(result_in.at[m], result.at[m]) for m in range(runs)] + [(source_in.at[m], source.at[m]) for m in range(runs)]
    pairs += [(a_in, a), (u_in, u), (d_in, d), (o_in, o), (sums_in, sums)]
    loads = [pltpu.make_async_copy(*pair, load_sem.at[at]) for at, pair in enumerate(pairs)]
    for copy in loads:
        copy.start()
    stores = []

    def put(held, target):
        copy = pltpu.make_async_copy(held, target, store_sem.at[len(stores)])
        copy.start()
        stores.append(copy)

    for m in range(runs):
        loads[m].wait()
        result_f[m] = result[m].astype(F32)
        put(result_f.at[m], result_out.at[m])
    for m in range(runs):
        loads[runs + m].wait()
        source_f[m] = source[m].astype(F32)
        put(source_f.at[m], source_out.at[m])
    loads[2 * runs].wait()
    for at, target in enumerate((d_q, d_k, d_v)):
        a_f[at] = a[:, at * LANES : (at + 1) * LANES].astype(F32)
        put(a_f.at[at], target)
    loads[2 * runs + 1].wait()
    u_f[...] = u[...].astype(F32)
    put(u_f, d_up)
    loads[2 * runs + 2].wait()
    d_f[...] = d[...].astype(F32)
    put(d_f, d_down)
    loads[2 * runs + 3].wait()
    o_f[...] = o[...].astype(F32).T
    put(o_f, d_o)
    loads[2 * runs + 4].wait()
    for at, target in enumerate((d_n1g, d_n1b, d_ob, d_n2g, d_n2b, d_db)):
        row, lane = 2 + at // 4, at % 4 * LANES
        row_f[at, :, :LANES] = sums[row : row + 1, lane : lane + LANES]
        put(row_f.at[at, :, pl.ds(0, LANES)], target)
    for at, target in ((6, d_qb), (7, d_vb)):
        row_f[at, :, :LANES] = sums[1:2, (at - 6) * LANES : (at - 5) * LANES]
        put(row_f.at[at, :, pl.ds(0, LANES)], target)
    row_f[8] = sums[0:1, :]
    put(row_f.at[8], d_upb)
    for copy in stores:
        copy.wait()


def shards(
    x_in,
    grad_out,
    seg_ids,
    norm1_gain,
    norm1_bias,
    q_weight,
    q_bias,
    k_weight,
    v_weight,
    v_bias,
    out_weight,
    out_bias,
    norm2_gain,
    norm2_bias,
    up_weight,
    up_bias,
    down_weight,
    down_bias,
):
    C, W = lax.axis_size("ctx"), lax.axis_size("wt")
    runs, T, width = x_in.shape
    hidden = up_weight.shape[1]
    geo = Geometry(C, W, T)
    S, B = geo.slots, C.bit_length() - 1
    each = width // C
    assert runs == W and hidden == width and q_weight.shape[1] == LANES and T == 256
    sds = jax.ShapeDtypeStruct
    vmem, dma = pltpu.VMEM, pltpu.SemaphoreType.DMA
    row = lambda v: v.reshape(1, -1)
    pair = 2 * LANES
    wide_of = (3 * LANES, hidden, width, LANES)
    slots = sum(B - f for f in (FIRST_STAGE if B > 2 else (0,) * 4))
    scratch = [
        vmem(seg_ids.shape, jnp.int32),
        *[vmem((1, n), F32) for n in (width, width, LANES, LANES, width, width, width, hidden, width)],
        *[vmem((W, width, n), BF16) for n in wide_of],
        vmem((W, 8, width), F32),
        vmem((T, width), BF16),
        vmem((T, width), BF16),
        vmem((LANES, width), BF16),
        vmem((T, width), BF16),
        vmem((W, T, LANES), BF16),
        vmem((W, T, pair), BF16),
        vmem((W, 224, pair), BF16),
        vmem((W, 80, pair), BF16),
        vmem((W, 16, pair), BF16),
        vmem((W, 80, pair), BF16),
        vmem((C, W, 16, pair), BF16),
        vmem((W, 2, S, pair), BF16),
        vmem((2, S, geo.tile), F32),
        vmem((W, 2, S, pair), BF16),
        vmem((W, T, LANES), BF16),
        vmem((T, width), F32),
        vmem((T, width), BF16),
        vmem((W, T, hidden), BF16),
        vmem((W, T, hidden), F32),
        vmem((T, width), F32),
        vmem((T, width), F32),
        vmem((T, width), F32),
        vmem((W, T, LANES), BF16),
        vmem((W, T, LANES), BF16),
        vmem((W, 2, S, pair), F32),
        vmem((T, width), BF16),
        vmem((W, 80, pair), BF16),
        vmem((C, W, 16, pair), BF16),
        vmem((W, 80, pair), BF16),
        vmem((C, W, 16, pair), BF16),
        *[vmem((W, width, n), BF16) for n in wide_of],
        vmem((W, 8, width), F32),
        vmem((W, T, width), BF16),
        vmem((W, T, width), BF16),
        *[vmem((W, each, n), BF16) for n in wide_of],
        *[vmem((each, n), BF16) for n in wide_of],
        *[vmem((each, n), BF16) for n in wide_of],
        *[vmem((width, n), BF16) for n in wide_of],
        vmem((W, 8, width), F32),
        vmem((B + 1, 8, width), F32),
        vmem((B, 8, width), F32),
        dma((8,)),
        dma((10,)),
        dma((7,)),
        dma((4, W)),
        dma((4, W)),
        dma((4,)),
        dma((slots, W - 1)),
        dma((W,)),
        dma((W,)),
        dma((W,)),
        dma((W,)),
        dma((C, W)),
        dma((C, W)),
        dma((W,)),
        dma((W,)),
        dma((4,)),
        dma((4, W, B)),
        dma((4,)),
        dma((4, W)),
        dma((4,)),
        dma((4,)),
        dma((2,)),
        dma((2, B)),
        dma((2,)),
        dma((2, C // 2)),
        dma((2,)),
        dma((2, C // 2)),
        dma((4, W)),
        dma((4, W)),
        dma((W,)),
        dma((W,)),
        dma((B,)),
        dma((B,)),
    ] + [vmem((W, each * 2**s, n), BF16) for s in range(B) for n in wide_of]
    far = pl.BlockSpec(memory_space=pl.ANY)
    result, source, d_a, d_u, d_d, d_o, sums = pl.pallas_call(
        functools.partial(fused, geo),
        name="fused",
        out_shape=[sds((W, T, width), BF16), sds((W, T, width), BF16), *[sds((width, n), BF16) for n in wide_of], sds((8, width), F32)],
        in_specs=[far] * 18,
        out_specs=[far] * 7,
        scratch_shapes=scratch,
        compiler_params=pltpu.CompilerParams(collective_id=0, has_side_effects=True, vmem_limit_bytes=58 * 2**20),
    )(
        x_in, grad_out, seg_ids, row(norm1_gain), row(norm1_bias), q_weight, row(q_bias), k_weight, v_weight, row(v_bias),
        out_weight, row(out_bias), row(norm2_gain), row(norm2_bias), up_weight, row(up_bias), down_weight, row(down_bias),
    )
    one, thin, full = (1, LANES), (width, LANES), (width, width)
    shapes = [(W, T, width)] * 2 + [one, one, thin, one, thin, thin, one, (LANES, width), one, one, one, full, (1, hidden), full, one]
    values = pl.pallas_call(
        unpack,
        name="unpack",
        out_shape=[sds(shape, F32) for shape in shapes],
        in_specs=[far] * 7,
        out_specs=[far] * 17,
        scratch_shapes=[
            vmem((W, T, width), BF16),
            vmem((W, T, width), BF16),
            *[vmem((width, n), BF16) for n in wide_of],
            vmem((8, width), F32),
            vmem((W, T, width), F32),
            vmem((W, T, width), F32),
            vmem((3, width, LANES), F32),
            vmem((LANES, width), F32),
            vmem(full, F32),
            vmem(full, F32),
            vmem((9, 1, hidden), F32),
            dma((2 * W + 5,)),
            dma((2 * W + 15,)),
        ],
        compiler_params=pltpu.CompilerParams(vmem_limit_bytes=58 * 2**20),
    )(result, source, d_a, d_u, d_d, d_o, sums)
    return tuple(v.reshape(-1) if v.shape[0] == 1 else v for v in values)


def solution(mesh):
    in_specs = (
        P(None, "ctx", None),
        P(None, "ctx", None),
        P(),
        P(),
        P(),
        P(None, "wt"),
        P("wt"),
        P(None, "wt"),
        P(None, "wt"),
        P("wt"),
        P("wt", None),
        P(),
        P(),
        P(),
        P(None, "wt"),
        P("wt"),
        P("wt", None),
        P(),
    )
    out_specs = (
        P(None, "ctx", None),
        P(None, "ctx", None),
        P("wt"),
        P("wt"),
        P(None, "wt"),
        P("wt"),
        P(None, "wt"),
        P(None, "wt"),
        P("wt"),
        P("wt", None),
        P("wt"),
        P("wt"),
        P("wt"),
        P(None, "wt"),
        P("wt"),
        P("wt", None),
        P("wt"),
    )
    return jax.shard_map(shards, mesh=mesh, in_specs=in_specs, out_specs=out_specs, check_vma=False)
```
